256 devices in a mesh: node: 16 (over x, z_lo), hid: 16 (over z_hi, y, core).
Axes of the slice: x: 4, y: 4, z: 8 (z_hi: 2, z_lo: 4; z = z_hi * 4 + z_lo), core: 2. Of those that a mesh axis runs over, the one named last changes fastest.
Arguments:
- feats: bfloat16 [512, 32768], P('hid', 'node'), may hold values from -6 to 6
- weight: bfloat16 [512, 512], P(None, 'hid'), may hold values from -0.25 to 0.25
- bias: float32 [512], P('hid'), may hold values from -3 to 3
- adjacency: bfloat16 [256, 16, 128, 128], P('node'), may hold values from -0.19921875 to 0.19921875
- columns: int32 [256, 16], P('node'), may hold values from 0 to 255, as said below
- counts: int32 [256], P('node'), may hold values from 1 to 16, as said below
- cotangent: bfloat16 [512, 32768], P('hid', 'node'), may hold values from -6 to 6
Outputs:
- hidden: bfloat16 [512, 32768], P('hid', 'node')
- feat_grad: bfloat16 [512, 32768], P('hid', 'node')
- weight_grad: float32 [512, 512], P('node', 'hid')
- bias_grad: float32 [512], P('hid')
The draws below stay inside these ranges and needn't reach their ends.
Inputs may be any that keep to these rules, and one draw needn't show every extreme that they name: `columns`: the first counts[r] entries of row r are distinct block numbers; later entries are block numbers too. `counts`: at least one row block has 16 nonzero blocks.
All inputs are finite; a program needn't handle non-finite values.
Results may differ from the reference program's by a relative error of at most 0.027.
Values may be sent and summed in bfloat16 or wider, within the bound.
No kernel may reach another device: no remote copies, remote signals or barrier semaphores. Data moves between devices by JAX's collectives and lax.ppermute only.
A program may use at most 64 MiB of HBM per device.

```python
import math
import jax
import jax.numpy as jnp
from jax import lax

F = 512
BS = 128
MAXNZ = 16
RB = 16
NB = 256
NODES = 32768
N_NODE = 16


def block_lists(key):
    key_level, key_count, key_peak, key_order = jax.random.split(key, 4)
    lowest = max(MAXNZ // 4, 1)
    levels = jax.random.randint(key_level, (NB // RB,), lowest, MAXNZ + 1)
    levels = jnp.repeat(levels, RB)
    floors = jnp.maximum(levels // 2, 1)
    drawn = jax.random.randint(key_count, (NB,), 0, 1 << 20)
    counts_row = floors + drawn % (levels - floors + 1)
    peak_row = jax.random.randint(key_peak, (), 0, NB)
    counts_row = jnp.where(jnp.arange(NB) == peak_row, MAXNZ, counts_row)
    orders = jax.vmap(lambda single: jax.random.permutation(single, NB)[:MAXNZ])(jax.random.split(key_order, NB))
    return (orders.astype(jnp.int32), counts_row.astype(jnp.int32))


def draw_columns(key, part):
    return block_lists(key)[0]


def draw_counts(key, part):
    return block_lists(key)[1]


def block_scale(stream_key, extent, cuts, low, top_value):
    def one(position, shards_of):
        heights = jax.random.uniform(jax.random.fold_in(jax.random.fold_in(stream_key, 6), position), (shards_of,), jnp.float32, low / len(cuts), top_value / len(cuts))
        return jnp.repeat(jnp.exp(heights), extent[position] // shards_of).reshape((-1,) + (1,) * (len(extent) - position - 1))

    gain = one(*cuts[0])
    for cut in cuts[1:]:
        gain = gain * one(*cut)
    return gain


def noise(rng, extent, spread, bound, cuts=(), held_as=jnp.bfloat16):
    entries = spread * jax.random.normal(rng, extent, jnp.float32)
    if cuts:
        entries = entries * block_scale(rng, extent, cuts, -0.22, 0.18)
    return jnp.clip(entries, -bound, bound).astype(held_as)


def setup_inputs(seed: int = 0) -> dict:
    keys = jax.random.split(jax.random.key(seed), 8)
    feats = noise(keys[0], (F, NODES), 1.0, 6.0, ((0, 16), (1, 16)))
    weight = noise(keys[1], (F, F), F ** -0.5, 0.25, ((1, 16),))
    bias = noise(keys[2], (F,), 0.5, 3.0, ((0, 16),), jnp.float32)
    adjacency = noise(keys[3], (NB, MAXNZ, BS, BS), 0.03125, 0.19921875, ((0, 16),))
    columns = draw_columns(jax.random.fold_in(keys[7], 71), 0)
    counts = draw_counts(jax.random.fold_in(keys[7], 71), 0)
    cotangent = noise(keys[6], (F, NODES), 1.0, 6.0, ((0, 16), (1, 16)))
    return dict(feats=feats, weight=weight, bias=bias, adjacency=adjacency, columns=columns, counts=counts, cotangent=cotangent)


def reference(feats, weight, bias, adjacency, columns, counts, cotangent):
    width = feats.shape[0]
    block_total = adjacency.shape[0]
    capacity = adjacency.shape[1]
    block = adjacency.shape[2]
    nodes_all = feats.shape[1]
    projected = jnp.dot(weight.T, feats, preferred_element_type=jnp.float32).astype(jnp.bfloat16)
    by_block = projected.reshape(width, block_total, block)
    in_use = (lax.broadcasted_iota(jnp.int32, (block_total, capacity), 1) < counts[:, None]).astype(jnp.float32)

    def row_block(items):
        targets, usable, blocks = items
        chosen = jnp.take(by_block, targets, axis=1).astype(jnp.float32) * usable[None, :, None]
        return jnp.einsum('fkj,kij->fi', chosen, blocks.astype(jnp.float32))
    preact = lax.map(row_block, (columns, in_use, adjacency))
    preact = preact.transpose(1, 0, 2).reshape(width, nodes_all) + bias[:, None]
    hidden = jax.nn.silu(preact).astype(jnp.bfloat16)
    sigma = jax.nn.sigmoid(preact)
    slope = (cotangent.astype(jnp.float32) * sigma * (1.0 + preact * (1.0 - sigma))).astype(jnp.bfloat16)
    slope_blocks = slope.reshape(width, block_total, block).transpose(1, 0, 2)

    def step(summed, items):
        targets, usable, blocks, slope_row = items
        pieces = jnp.einsum('fi,kij->kfj', slope_row.astype(jnp.float32), blocks.astype(jnp.float32))
        pieces = pieces * usable[:, None, None]
        return (summed.at[targets].add(pieces), None)
    group_cols = columns.reshape(N_NODE, RB, capacity)
    group_use = in_use.reshape(N_NODE, RB, capacity)
    group_adj = adjacency.reshape(N_NODE, RB, capacity, block, block)
    group_slope = slope_blocks.reshape(N_NODE, RB, width, block)

    def device_part(total, items):
        start = jnp.zeros((block_total, width, block), jnp.float32)
        part, unused_inner = lax.scan(step, start, items)
        rounded = lax.optimization_barrier(part.astype(jnp.bfloat16))
        return (total + rounded.astype(jnp.float32), None)
    summed, unused = lax.scan(device_part, jnp.zeros((block_total, width, block), jnp.float32), (group_cols, group_use, group_adj, group_slope))
    grad_proj = summed.transpose(1, 0, 2).reshape(width, nodes_all).astype(jnp.bfloat16)
    grad_scale = 1.0 / math.sqrt(nodes_all)
    weight_grad = jnp.dot(feats, grad_proj.T, preferred_element_type=jnp.float32) * grad_scale
    bias_grad = lax.optimization_barrier(jnp.sum(slope.astype(jnp.float32), axis=1)) * grad_scale
    feat_grad = jnp.dot(weight, grad_proj, preferred_element_type=jnp.float32).astype(jnp.bfloat16)
    return (hidden, feat_grad, weight_grad, bias_grad)
```

```python
import math

import jax
import jax.numpy as jnp
from jax import lax
from jax.experimental import pallas as pl
from jax.experimental.pallas import tpu as pltpu
from jax.sharding import PartitionSpec as P

F32 = jnp.float32
BF16 = jnp.bfloat16
ZN = 4
UNROLL = 8
VMEM = pltpu.VMEM
LIMIT = 48 * 1024 * 1024


def shift_x(v, by, n):
    return lax.ppermute(v, "node", [(i, (i + ZN * by) % n) for i in range(n)])


def flip_z(v, by, n):
    return lax.ppermute(v, "node", [(i, i ^ by) for i in range(n)])


def split3(v):
    hi = lax.reduce_precision(v, 8, 7)
    mid = lax.reduce_precision(v - hi, 8, 7)
    return hi, mid, v - hi - mid


def list_slots(counts_ref, slots_ref, row_blocks, capacity):
    def row(r, n):
        def one(k, n):
            slots_ref[n] = r * capacity + k
            return n + 1

        return lax.fori_loop(0, counts_ref[r], one, n)

    used = lax.fori_loop(0, row_blocks, row, 0)
    for i in range(UNROLL):
        slots_ref[used + i] = 0
    return used


def fwd_kernel(place_ref, counts_ref, adj_ref, cot_ref, *refs):
    nsrc = len(refs) - 5
    srcs, out_ref, xs, acc, slots, sems = refs[:nsrc], *refs[nsrc:]
    row_blocks, capacity, block, _ = adj_ref.shape
    copies = [pltpu.make_async_copy(srcs[q], xs.at[q], sems.at[q]) for q in range(nsrc)]
    for c in copies:
        c.start()
    used = list_slots(counts_ref, slots, row_blocks, capacity)
    acc[...] = jnp.zeros_like(acc)
    for c in copies:
        c.wait()

    def step(i, carry):
        parts = []
        for u in range(UNROLL):
            at = i * UNROLL + u
            slot = slots[at]
            r, k = slot // capacity, slot % capacity
            where = place_ref[r, k]
            q, j = where // row_blocks, where % row_blocks
            x = xs[q, :, pl.ds(pl.multiple_of(j * block, block), block)]
            got = lax.dot_general(
                x, adj_ref[r, k], (((1,), (1,)), ((), ())), preferred_element_type=F32
            )
            parts.append((r, jnp.where(at < used, got, 0.0)))
        for r, got in parts:
            acc[r] += got
        return carry

    lax.fori_loop(0, (used + UNROLL - 1) // UNROLL, step, 0)
    for r in range(row_blocks):
        out_ref[r, :, :block] = acc[r].astype(BF16)
        out_ref[r, :, block:] = cot_ref[:, r * block : (r + 1) * block]


def mid_kernel(order_ref, got_ref, near_ref, far_ref, out_ref, wt):
    hid, width, _ = got_ref.shape
    block = got_ref.shape[2] // 2
    total = hid * width
    half = hid // 2
    for n in range(half):
        wt[order_ref[n]] = near_ref[n]
        wt[order_ref[half + n]] = far_ref[n]
    wall = wt[...].reshape(total, wt.shape[2])
    w = wall[:, :total]
    bias = jnp.sum(wall[:, total:].astype(F32), axis=1, keepdims=True)
    got = got_ref[...].reshape(total, 2 * block)
    agg, cot = got[:, :block], got[:, block:].astype(F32)
    pre = jnp.dot(w, agg, preferred_element_type=F32) + bias
    sig = jax.nn.sigmoid(pre)
    hidden = (pre * sig).astype(BF16)
    slope = (cot * sig * (1.0 + pre * (1.0 - sig))).astype(BF16)
    ws = lax.dot_general(w, slope, (((0,), (0,)), ((), ())), preferred_element_type=F32)
    wg = lax.dot_general(slope, agg, (((1,), (1,)), ((), ())), preferred_element_type=F32)
    bsum = jnp.sum(slope.astype(F32), axis=1, keepdims=True)
    hi = bsum.astype(BF16).astype(F32)
    mid = (bsum - hi).astype(BF16).astype(F32)
    low = bsum - hi - mid
    lane = lax.broadcasted_iota(jnp.int32, (total, 128), 1)
    tail = jnp.where(lane == 0, hi, jnp.where(lane == 1, mid, jnp.where(lane == 2, low, 0.0)))
    out_ref[:, :, :block] = ws.astype(BF16).reshape(hid, width, block)
    out_ref[:, :, block : 2 * block] = hidden.reshape(hid, width, block)
    out_ref[:, :, 2 * block : 2 * block + total] = wg.astype(BF16).reshape(hid, width, total)
    out_ref[:, :, 2 * block + total :] = tail.astype(BF16).reshape(hid, width, 128)


def bwd_kernel(
    place_ref, counts_ref, dest_ref, adj_ref, got_ref,
    hidden_ref, own_ref, d2a, d2b, ra, rb, la, lb, acc, ext, slots,
):
    row_blocks, capacity, block, _ = adj_ref.shape
    nodes, width, rows = acc.shape
    total = nodes * width
    used = list_slots(counts_ref, slots, row_blocks, capacity)
    acc[...] = jnp.zeros_like(acc)

    def step(i, carry):
        parts = []
        for u in range(UNROLL):
            at = i * UNROLL + u
            slot = slots[at]
            r, k = slot // capacity, slot % capacity
            where = place_ref[r, k]
            q, j = where // row_blocks, where % row_blocks
            made = jnp.dot(got_ref[r, :, :block], adj_ref[r, k], preferred_element_type=F32)
            parts.append((q, j, jnp.where(at < used, made, 0.0)))
        for q, j, made in parts:
            acc[q, :, pl.ds(pl.multiple_of(j * block, block), block)] += made
        return carry

    lax.fori_loop(0, (used + UNROLL - 1) // UNROLL, step, 0)

    wg = jnp.zeros((width, total), F32)
    tail = jnp.zeros((width, 128), F32)
    for b in range(row_blocks):
        hidden_ref[:, b * block : (b + 1) * block] = got_ref[b, :, block : 2 * block]
        wg = wg + got_ref[b, :, 2 * block : 2 * block + total].astype(F32)
        tail = tail + got_ref[b, :, 2 * block + total :].astype(F32)
    bsum = jnp.sum(tail, axis=1, keepdims=True)
    hi = bsum.astype(BF16).astype(F32)
    mid = (bsum - hi).astype(BF16).astype(F32)
    low = bsum - hi - mid
    lane = lax.broadcasted_iota(jnp.int32, (width, 128), 1)
    me = dest_ref[nodes]
    first = width + me
    tail = jnp.where(lane == first, hi, 0.0)
    tail = jnp.where(lane == first + nodes, mid, tail)
    tail = jnp.where(lane == first + 2 * nodes, low, tail)
    for a in range(nodes):
        tile = wg[:, (a * width) // 128 * 128 : (a * width) // 128 * 128 + 128]
        start = (a * width) % 128
        if start:
            tile = pltpu.roll(tile, 128 - start, 1)
        ext[dest_ref[a]] = jnp.where(lane < width, tile, tail)

    def put(ref, n, q):
        ref[n, :, :rows] = acc[q].astype(BF16)
        ref[n, :, rows:] = ext[q].astype(BF16)

    for s in range(ZN):
        put(own_ref, s, s)
        first, second = ((d2a, ra, la) if s < 2 else (d2b, rb, lb)), s % 2
        put(first[0], second, 2 * ZN + s)
        put(first[1], second, ZN + s)
        put(first[2], second, 3 * ZN + s)


def join_kernel(own_ref, ra, rb, la, lb, s0, s1, s2, s3):
    outs = (s0, s1, s2, s3)
    for s in range(ZN):
        left, right = (ra, la) if s < 2 else (rb, lb)
        n = s % 2
        total = own_ref[s].astype(F32) + left[n].astype(F32) + right[n].astype(F32)
        outs[s][...] = total.astype(BF16)


def last_kernel(scale, s0, s1, s2, s3, feat_ref, wg_ref, bias_ref):
    total = s0[...].astype(F32) + s1[...].astype(F32) + s2[...].astype(F32) + s3[...].astype(F32)
    width, rows = feat_ref.shape
    feat_ref[...] = total[:, :rows].astype(BF16)
    tail = total[:, rows:]
    lane = lax.broadcasted_iota(jnp.int32, tail.shape, 1)
    bsum = jnp.sum(jnp.where(lane >= width, tail, 0.0), axis=1, keepdims=True)
    bias_ref[...] = jnp.broadcast_to(bsum * scale, bias_ref.shape)
    wg_ref[...] = tail[:, :width].T * scale


def spec(space):
    return pl.BlockSpec(memory_space=space)


def params():
    return pltpu.CompilerParams(vmem_limit_bytes=LIMIT)


def per_device(feats, weight, bias, adjacency, columns, counts, cotangent):
    width, rows = feats.shape
    row_blocks, capacity, block, _ = adjacency.shape
    nodes, hid = lax.axis_size("node"), lax.axis_size("hid")
    total = weight.shape[0]
    scale = 1.0 / math.sqrt(nodes * rows)
    me, mine = lax.axis_index("node"), lax.axis_index("hid")
    x, z = me // ZN, me % ZN

    def rel(a):
        return ((a // ZN - x) % ZN) * ZN + ((a % ZN) ^ z)

    everyone = jnp.arange(nodes, dtype=jnp.int32)
    place = rel(columns // row_blocks) * row_blocks + columns % row_blocks
    dest = jnp.concatenate([rel(everyone), me[None].astype(jnp.int32)])

    with jax.named_scope("node_gather"):
        here = [feats] + [flip_z(feats, s, nodes) for s in range(1, ZN)]
        left = [shift_x(v, 1, nodes) for v in here]
        right = [shift_x(v, -1, nodes) for v in here]
        across = [shift_x(left[s], 1, nodes) for s in (0, 1)]
        across += [shift_x(right[s], -1, nodes) for s in (2, 3)]
    sources = here + right + across + left

    with jax.named_scope("weight_gather"):
        lanes = jnp.stack(split3(bias), axis=1).astype(BF16)
        own = jnp.concatenate([weight.T, jnp.pad(lanes, ((0, 0), (0, 125)))], axis=1)
        ny = hid // 4

        def hid_perm(v, f):
            return lax.ppermute(v, "hid", [(i, f(i)) for i in range(hid)])

        pair = jnp.stack([own, hid_perm(own, lambda i: (i + hid // 2) % hid)])

        def turn(d):
            return lambda i: i // (2 * ny) * (2 * ny) + (i + 2 * d) % (2 * ny)

        near = jnp.concatenate([pair] + [hid_perm(pair, turn(d)) for d in range(1, ny)])
        far = hid_perm(near, lambda i: i ^ 1)
        step_y = jnp.arange(ny, dtype=jnp.int32)[:, None]
        step_z = jnp.arange(2, dtype=jnp.int32)[None, :]
        py = (mine // 2 - step_y) % ny
        pz = (mine // (2 * ny)) ^ step_z
        near_at = (pz * 2 * ny + py * 2 + mine % 2).reshape(-1)
        order = jnp.concatenate([near_at, near_at ^ 1]).astype(jnp.int32)

    with jax.named_scope("aggregate"):
        agg = pl.pallas_call(
            fwd_kernel,
            out_shape=jax.ShapeDtypeStruct((row_blocks, width, 2 * block), BF16),
            in_specs=[spec(pltpu.SMEM)] * 2 + [spec(VMEM)] * 2 + [spec(pl.ANY)] * nodes,
            out_specs=spec(VMEM),
            scratch_shapes=[
                VMEM((nodes, width, rows), BF16),
                VMEM((row_blocks, width, block), F32),
                pltpu.SMEM((row_blocks * capacity + UNROLL,), jnp.int32),
                pltpu.SemaphoreType.DMA((nodes,)),
            ],
            compiler_params=params(),
        )(place, counts, adjacency, cotangent, *sources)
    got = lax.all_to_all(agg, "hid", 0, 0, tiled=True)

    with jax.named_scope("dense"):
        made = pl.pallas_call(
            mid_kernel,
            out_shape=jax.ShapeDtypeStruct((hid, width, 2 * block + total + 128), BF16),
            in_specs=[spec(pltpu.SMEM)] + [spec(VMEM)] * 3,
            out_specs=spec(VMEM),
            scratch_shapes=[VMEM((hid, width, total + 128), BF16)],
            compiler_params=params(),
        )(order, got, near, far)
    back = lax.all_to_all(made, "hid", 0, 0, tiled=True)

    wide = rows + 128
    with jax.named_scope("spread"):
        two = jax.ShapeDtypeStruct((2, width, wide), BF16)
        hidden, own_sum, d2a, d2b, ra, rb, la, lb = pl.pallas_call(
            bwd_kernel,
            out_shape=[
                jax.ShapeDtypeStruct((width, rows), BF16),
                jax.ShapeDtypeStruct((ZN, width, wide), BF16),
            ]
            + [two] * 6,
            in_specs=[spec(pltpu.SMEM)] * 3 + [spec(VMEM)] * 2,
            out_specs=[spec(VMEM)] * 8,
            scratch_shapes=[
                VMEM((nodes, width, rows), F32),
                VMEM((nodes, width, 128), F32),
                pltpu.SMEM((row_blocks * capacity + UNROLL,), jnp.int32),
            ],
            compiler_params=params(),
        )(place, counts, dest, adjacency, back)

    with jax.named_scope("node_sum"):

        def add(u, v):
            return (u.astype(F32) + v.astype(F32)).astype(BF16)

        rb = shift_x(rb, 1, nodes)
        la = shift_x(la, -1, nodes)
        ra = shift_x(add(ra, shift_x(d2a, 1, nodes)), 1, nodes)
        lb = shift_x(add(lb, shift_x(d2b, -1, nodes)), -1, nodes)
        one = jax.ShapeDtypeStruct((width, wide), BF16)
        sums = pl.pallas_call(
            join_kernel,
            out_shape=[one] * ZN,
            in_specs=[spec(VMEM)] * 5,
            out_specs=[spec(VMEM)] * ZN,
            compiler_params=params(),
        )(own_sum, ra, rb, la, lb)
        parts = [sums[0]] + [flip_z(sums[s], s, nodes) for s in range(1, ZN)]
        feat_grad, weight_grad, bias_grad = pl.pallas_call(
            lambda *refs: last_kernel(scale, *refs),
            out_shape=[
                jax.ShapeDtypeStruct((width, rows), BF16),
                jax.ShapeDtypeStruct((width, width), F32),
                jax.ShapeDtypeStruct((width, 128), F32),
            ],
            in_specs=[spec(VMEM)] * ZN,
            out_specs=[spec(VMEM)] * 3,
            compiler_params=params(),
        )(*parts)
    return hidden, feat_grad, weight_grad, bias_grad[:, 0]


def solution(mesh):
    placed = (
        P("hid", "node"),
        P(None, "hid"),
        P("hid"),
        P("node", None, None, None),
        P("node", None),
        P("node"),
        P("hid", "node"),
    )
    return jax.shard_map(
        per_device,
        mesh=mesh,
        in_specs=placed,
        out_specs=(P("hid", "node"), P("hid", "node"), P("node", "hid"), P("hid")),
        check_vma=False,
    )
```

```python
import math

import jax
import jax.numpy as jnp
from jax import lax
from jax.experimental import pallas as pl
from jax.experimental.pallas import tpu as pltpu
from jax.sharding import PartitionSpec as P

F32 = jnp.float32
BF16 = jnp.bfloat16
ZN = 4
UNROLL = 4
QUARTER = 4
PAIRS = 128
TS, TR, TQ0, TC0, TQ1, TC1, FIELDS = range(7)
VMEM = pltpu.VMEM
LIMIT = 56 * 1024 * 1024


def shift_x(v, by, n):
    return lax.ppermute(v, "node", [(i, (i + ZN * by) % n) for i in range(n)])


def flip_z(v, by, n):
    return lax.ppermute(v, "node", [(i, i ^ by) for i in range(n)])


def split3(v):
    hi = lax.reduce_precision(v, 8, 7)
    mid = lax.reduce_precision(v - hi, 8, 7)
    return hi, mid, v - hi - mid


def load_rows(counts_ref, adj_hbm, adj, sems, begin):
    row_blocks, pieces = sems.shape

    def one(r, q):
        at = pl.ds((r * pieces + q) * QUARTER, QUARTER)
        return pltpu.make_async_copy(adj_hbm.at[at], adj.at[at], sems.at[r, q])

    def row(r, carry):
        for q in range(pieces):

            @pl.when(counts_ref[r] > q * QUARTER)
            def _():
                one(r, q).start() if begin else one(r, q).wait()

        return carry

    return row


def two_slots(adj, slot):
    return jnp.concatenate([adj[slot], adj[slot + 1]], axis=1)


def fwd_kernel(tab_ref, counts_ref, adj_hbm, cot_ref, *refs):
    nsrc = len(refs) - 6
    srcs, out_ref, xs, adj, acc, sems, rsems = refs[:nsrc], *refs[nsrc:]
    row_blocks, _, block = acc.shape
    copies = [pltpu.make_async_copy(srcs[q], xs.at[q], sems.at[q]) for q in range(nsrc)]
    for c in copies:
        c.start()
    lax.fori_loop(0, row_blocks, load_rows(counts_ref, adj_hbm, adj, rsems, True), 0)
    acc[...] = jnp.zeros_like(acc)
    xs[nsrc] = jnp.zeros_like(xs[nsrc])
    for r in range(row_blocks):
        out_ref[r, :, block:] = cot_ref[:, r * block : (r + 1) * block]
    for c in copies:
        c.wait()

    def step(i, ready):
        last = tab_ref[TR * PAIRS + i * UNROLL + UNROLL - 1]
        lax.fori_loop(ready, last + 1, load_rows(counts_ref, adj_hbm, adj, rsems, False), 0)
        parts = []
        for u in range(UNROLL):
            t = i * UNROLL + u

            def pick(q, c):
                at = pl.ds(pl.multiple_of(tab_ref[c * PAIRS + t], block), block)
                return xs[tab_ref[q * PAIRS + t], :, at]

            x = jnp.concatenate([pick(TQ0, TC0), pick(TQ1, TC1)], axis=1)
            a = two_slots(adj, tab_ref[TS * PAIRS + t])
            got = lax.dot_general(x, a, (((1,), (1,)), ((), ())), preferred_element_type=F32)
            parts.append((tab_ref[TR * PAIRS + t], got))
        for r, got in parts:
            acc[r] += got
        return jnp.maximum(ready, last + 1)

    lax.fori_loop(0, tab_ref[FIELDS * PAIRS], step, 0)
    for r in range(row_blocks):
        out_ref[r, :, :block] = acc[r].astype(BF16)


def mid_kernel(order_ref, got_ref, near_ref, far_ref, out_ref, wt):
    hid, width, _ = got_ref.shape
    block = got_ref.shape[2] // 2
    total = hid * width
    half = hid // 2
    for n in range(half):
        wt[order_ref[n]] = near_ref[n]
        wt[order_ref[half + n]] = far_ref[n]
    wall = wt[...].reshape(total, wt.shape[2])
    w = wall[:, :total]
    bias = jnp.sum(wall[:, total:].astype(F32), axis=1, keepdims=True)
    got = got_ref[...].reshape(total, 2 * block)
    agg, cot = got[:, :block], got[:, block:].astype(F32)
    pre = jnp.dot(w, agg, preferred_element_type=F32) + bias
    sig = jax.nn.sigmoid(pre)
    hidden = (pre * sig).astype(BF16)
    slope = (cot * sig * (1.0 + pre * (1.0 - sig))).astype(BF16)
    ws = lax.dot_general(w, slope, (((0,), (0,)), ((), ())), preferred_element_type=F32)
    wg = lax.dot_general(slope, agg, (((1,), (1,)), ((), ())), preferred_element_type=F32)
    bsum = jnp.sum(slope.astype(F32), axis=1, keepdims=True)
    hi = bsum.astype(BF16).astype(F32)
    mid = (bsum - hi).astype(BF16).astype(F32)
    low = bsum - hi - mid
    lane = lax.broadcasted_iota(jnp.int32, (total, 128), 1)
    tail = jnp.where(lane == 0, hi, jnp.where(lane == 1, mid, jnp.where(lane == 2, low, 0.0)))
    out_ref[:, :, :block] = ws.astype(BF16).reshape(hid, width, block)
    out_ref[:, :, block : 2 * block] = hidden.reshape(hid, width, block)
    out_ref[:, :, 2 * block : 2 * block + total] = wg.astype(BF16).reshape(hid, width, total)
    out_ref[:, :, 2 * block + total :] = tail.astype(BF16).reshape(hid, width, 128)


def bwd_kernel(
    tab_ref, counts_ref, dest_ref, adj_hbm, got_ref,
    hidden_ref, own_ref, d2a, d2b, ra, rb, la, lb, acc, ext, adj, rsems,
):
    nodes, width, rows = acc.shape
    nodes = nodes - 1
    block = adj.shape[1]
    row_blocks = rows // block
    total = nodes * width
    lax.fori_loop(0, row_blocks, load_rows(counts_ref, adj_hbm, adj, rsems, True), 0)
    acc[...] = jnp.zeros_like(acc)

    def step(i, ready):
        last = tab_ref[TR * PAIRS + i * UNROLL + UNROLL - 1]
        lax.fori_loop(ready, last + 1, load_rows(counts_ref, adj_hbm, adj, rsems, False), 0)
        parts = []
        for u in range(UNROLL):
            t = i * UNROLL + u
            s = got_ref[tab_ref[TR * PAIRS + t], :, :block]
            a = two_slots(adj, tab_ref[TS * PAIRS + t])
            made = jnp.dot(s, a, preferred_element_type=F32)
            for n, (q, c) in enumerate(((TQ0, TC0), (TQ1, TC1))):
                at = pl.ds(pl.multiple_of(tab_ref[c * PAIRS + t], block), block)
                parts.append((tab_ref[q * PAIRS + t], at, made[:, n * block : (n + 1) * block]))
        for q, at, made in parts:
            acc[q, :, at] += made
        return jnp.maximum(ready, last + 1)

    lax.fori_loop(0, tab_ref[FIELDS * PAIRS], step, 0)

    wg = jnp.zeros((width, total), F32)
    tail = jnp.zeros((width, 128), F32)
    for b in range(row_blocks):
        hidden_ref[:, b * block : (b + 1) * block] = got_ref[b, :, block : 2 * block]
        wg = wg + got_ref[b, :, 2 * block : 2 * block + total].astype(F32)
        tail = tail + got_ref[b, :, 2 * block + total :].astype(F32)
    bsum = jnp.sum(tail, axis=1, keepdims=True)
    hi = bsum.astype(BF16).astype(F32)
    mid = (bsum - hi).astype(BF16).astype(F32)
    low = bsum - hi - mid
    lane = lax.broadcasted_iota(jnp.int32, (width, 128), 1)
    me = dest_ref[nodes]
    first = width + me
    tail = jnp.where(lane == first, hi, 0.0)
    tail = jnp.where(lane == first + nodes, mid, tail)
    tail = jnp.where(lane == first + 2 * nodes, low, tail)
    for a in range(nodes):
        tile = wg[:, (a * width) // 128 * 128 : (a * width) // 128 * 128 + 128]
        start = (a * width) % 128
        if start:
            tile = pltpu.roll(tile, 128 - start, 1)
        ext[dest_ref[a]] = jnp.where(lane < width, tile, tail)

    def put(ref, n, q):
        ref[n, :, :rows] = acc[q].astype(BF16)
        ref[n, :, rows:] = ext[q].astype(BF16)

    for s in range(ZN):
        put(own_ref, s, s)
        first, second = ((d2a, ra, la) if s < 2 else (d2b, rb, lb)), s % 2
        put(first[0], second, 2 * ZN + s)
        put(first[1], second, ZN + s)
        put(first[2], second, 3 * ZN + s)


def join_kernel(own_ref, ra, rb, la, lb, s0, s1, s2, s3):
    outs = (s0, s1, s2, s3)
    for s in range(ZN):
        left, right = (ra, la) if s < 2 else (rb, lb)
        n = s % 2
        total = own_ref[s].astype(F32) + left[n].astype(F32) + right[n].astype(F32)
        outs[s][...] = total.astype(BF16)


def last_kernel(scale, s0, s1, s2, s3, feat_ref, wg_ref, bias_ref):
    total = s0[...].astype(F32) + s1[...].astype(F32) + s2[...].astype(F32) + s3[...].astype(F32)
    width, rows = feat_ref.shape
    feat_ref[...] = total[:, :rows].astype(BF16)
    tail = total[:, rows:]
    lane = lax.broadcasted_iota(jnp.int32, tail.shape, 1)
    bsum = jnp.sum(jnp.where(lane >= width, tail, 0.0), axis=1, keepdims=True)
    bias_ref[...] = jnp.broadcast_to(bsum * scale, bias_ref.shape)
    wg_ref[...] = tail[:, :width].T * scale


def spec(space):
    return pl.BlockSpec(memory_space=space)


def params():
    return pltpu.CompilerParams(vmem_limit_bytes=LIMIT)


def per_device(feats, weight, bias, adjacency, columns, counts, cotangent):
    width, rows = feats.shape
    row_blocks, capacity, block, _ = adjacency.shape
    nodes, hid = lax.axis_size("node"), lax.axis_size("hid")
    total = weight.shape[0]
    scale = 1.0 / math.sqrt(nodes * rows)
    me, mine = lax.axis_index("node"), lax.axis_index("hid")
    x, z = me // ZN, me % ZN

    def rel(a):
        return ((a // ZN - x) % ZN) * ZN + ((a % ZN) ^ z)

    everyone = jnp.arange(nodes, dtype=jnp.int32)
    each = (counts + 1) // 2
    ends = jnp.cumsum(each)
    t = jnp.arange(PAIRS, dtype=jnp.int32)
    row = jnp.minimum(jnp.sum(t[:, None] >= ends[None, :], axis=1), row_blocks - 1).astype(jnp.int32)
    pick_row = (row[:, None] == jnp.arange(row_blocks)[None, :]).astype(jnp.int32)
    start = jnp.sum(pick_row * (ends - each)[None, :], axis=1)
    count = jnp.sum(pick_row * counts[None, :], axis=1)
    k = 2 * (t - start)
    kk = jnp.where(k < count, k, 0)
    cols = jnp.sum(pick_row[:, :, None] * columns[None, :, :], axis=1)
    tab = [row * capacity + kk, row]
    for n in (0, 1):
        pick_k = (kk + n)[:, None] == jnp.arange(capacity)[None, :]
        col = jnp.sum(jnp.where(pick_k, cols, 0), axis=1)
        tab += [jnp.where(k + n < count, rel(col // row_blocks), nodes), col % row_blocks * block]
    steps = (ends[-1] + UNROLL - 1) // UNROLL
    tab = jnp.concatenate(tab + [steps[None]]).astype(jnp.int32)
    blocks = adjacency.reshape(row_blocks * capacity, block, block)
    dest = jnp.concatenate([rel(everyone), me[None].astype(jnp.int32)])

    with jax.named_scope("node_gather"):
        here = [feats] + [flip_z(feats, s, nodes) for s in range(1, ZN)]
        left = [shift_x(v, 1, nodes) for v in here]
        right = [shift_x(v, -1, nodes) for v in here]
        across = [shift_x(left[s], 1, nodes) for s in (0, 1)]
        across += [shift_x(right[s], -1, nodes) for s in (2, 3)]
    sources = here + right + across + left

    with jax.named_scope("weight_gather"):
        lanes = jnp.stack(split3(bias), axis=1).astype(BF16)
        own = jnp.concatenate([weight.T, jnp.pad(lanes, ((0, 0), (0, 125)))], axis=1)
        ny = hid // 4

        def hid_perm(v, f):
            return lax.ppermute(v, "hid", [(i, f(i)) for i in range(hid)])

        pair = jnp.stack([own, hid_perm(own, lambda i: (i + hid // 2) % hid)])

        def turn(d):
            return lambda i: i // (2 * ny) * (2 * ny) + (i + 2 * d) % (2 * ny)

        near = jnp.concatenate([pair] + [hid_perm(pair, turn(d)) for d in range(1, ny)])
        far = hid_perm(near, lambda i: i ^ 1)
        step_y = jnp.arange(ny, dtype=jnp.int32)[:, None]
        step_z = jnp.arange(2, dtype=jnp.int32)[None, :]
        py = (mine // 2 - step_y) % ny
        pz = (mine // (2 * ny)) ^ step_z
        near_at = (pz * 2 * ny + py * 2 + mine % 2).reshape(-1)
        order = jnp.concatenate([near_at, near_at ^ 1]).astype(jnp.int32)

    with jax.named_scope("aggregate"):
        agg = pl.pallas_call(
            fwd_kernel,
            out_shape=jax.ShapeDtypeStruct((row_blocks, width, 2 * block), BF16),
            in_specs=[spec(pltpu.SMEM)] * 2 + [spec(pl.ANY), spec(VMEM)] + [spec(pl.ANY)] * nodes,
            out_specs=spec(VMEM),
            scratch_shapes=[
                VMEM((nodes + 1, width, rows), BF16),
                VMEM(blocks.shape, BF16),
                VMEM((row_blocks, width, block), F32),
                pltpu.SemaphoreType.DMA((nodes,)),
                pltpu.SemaphoreType.DMA((row_blocks, capacity // QUARTER)),
            ],
            compiler_params=params(),
        )(tab, counts, blocks, cotangent, *sources)
    got = lax.all_to_all(agg, "hid", 0, 0, tiled=True)

    with jax.named_scope("dense"):
        made = pl.pallas_call(
            mid_kernel,
            out_shape=jax.ShapeDtypeStruct((hid, width, 2 * block + total + 128), BF16),
            in_specs=[spec(pltpu.SMEM)] + [spec(VMEM)] * 3,
            out_specs=spec(VMEM),
            scratch_shapes=[VMEM((hid, width, total + 128), BF16)],
            compiler_params=params(),
        )(order, got, near, far)
    back = lax.all_to_all(made, "hid", 0, 0, tiled=True)

    wide = rows + 128
    with jax.named_scope("spread"):
        two = jax.ShapeDtypeStruct((2, width, wide), BF16)
        hidden, own_sum, d2a, d2b, ra, rb, la, lb = pl.pallas_call(
            bwd_kernel,
            out_shape=[
                jax.ShapeDtypeStruct((width, rows), BF16),
                jax.ShapeDtypeStruct((ZN, width, wide), BF16),
            ]
            + [two] * 6,
            in_specs=[spec(pltpu.SMEM)] * 3 + [spec(pl.ANY), spec(VMEM)],
            out_specs=[spec(VMEM)] * 8,
            scratch_shapes=[
                VMEM((nodes + 1, width, rows), F32),
                VMEM((nodes, width, 128), F32),
                VMEM(blocks.shape, BF16),
                pltpu.SemaphoreType.DMA((row_blocks, capacity // QUARTER)),
            ],
            compiler_params=params(),
        )(tab, counts, dest, blocks, back)

    with jax.named_scope("node_sum"):

        def add(u, v):
            return (u.astype(F32) + v.astype(F32)).astype(BF16)

        rb = shift_x(rb, 1, nodes)
        la = shift_x(la, -1, nodes)
        ra = shift_x(add(ra, shift_x(d2a, 1, nodes)), 1, nodes)
        lb = shift_x(add(lb, shift_x(d2b, -1, nodes)), -1, nodes)
        one = jax.ShapeDtypeStruct((width, wide), BF16)
        sums = pl.pallas_call(
            join_kernel,
            out_shape=[one] * ZN,
            in_specs=[spec(VMEM)] * 5,
            out_specs=[spec(VMEM)] * ZN,
            compiler_params=params(),
        )(own_sum, ra, rb, la, lb)
        parts = [sums[0]] + [flip_z(sums[s], s, nodes) for s in range(1, ZN)]
        feat_grad, weight_grad, bias_grad = pl.pallas_call(
            lambda *refs: last_kernel(scale, *refs),
            out_shape=[
                jax.ShapeDtypeStruct((width, rows), BF16),
                jax.ShapeDtypeStruct((width, width), F32),
                jax.ShapeDtypeStruct((width, 128), F32),
            ],
            in_specs=[spec(VMEM)] * ZN,
            out_specs=[spec(VMEM)] * 3,
            compiler_params=params(),
        )(*parts)
    return hidden, feat_grad, weight_grad, bias_grad[:, 0]


def solution(mesh):
    placed = (
        P("hid", "node"),
        P(None, "hid"),
        P("hid"),
        P("node", None, None, None),
        P("node", None),
        P("node"),
        P("hid", "node"),
    )
    return jax.shard_map(
        per_device,
        mesh=mesh,
        in_specs=placed,
        out_specs=(P("hid", "node"), P("hid", "node"), P("node", "hid"), P("hid")),
        check_vma=False,
    )
```

```python
import functools
import math

import jax
import jax.numpy as jnp
from jax import lax
from jax.experimental import pallas as pl
from jax.experimental.pallas import tpu as pltpu
from jax.sharding import PartitionSpec as P

F32 = jnp.float32
BF16 = jnp.bfloat16
ZN = 4
UNROLL = 4
QUARTER = 4
VMEM = pltpu.VMEM
MIB = 1024 * 1024


def shift_x(v, by, n):
    return lax.ppermute(v, "node", [(i, (i + ZN * by) % n) for i in range(n)])


def flip_z(v, by, n):
    return lax.ppermute(v, "node", [(i, i ^ by) for i in range(n)])


def split3(v):
    hi = lax.reduce_precision(v, 8, 7)
    mid = lax.reduce_precision(v - hi, 8, 7)
    return hi, mid, v - hi - mid


def load_rows(counts_ref, adj_hbm, adj, sems, begin):
    row_blocks, pieces = sems.shape

    def one(r, q):
        at = pl.ds((r * pieces + q) * QUARTER, QUARTER)
        return pltpu.make_async_copy(adj_hbm.at[at], adj.at[at], sems.at[r, q])

    def row(r, carry):
        for q in range(pieces):

            @pl.when(counts_ref[r] > q * QUARTER)
            def _():
                one(r, q).start() if begin else one(r, q).wait()

        return carry

    return row


def list_pairs(counts_ref, pairs_ref, none):
    row_blocks = counts_ref.shape[0]
    capacity = none // row_blocks

    def row(r, n):
        def one(p, n):
            pairs_ref[n] = r * capacity + 2 * p
            return n + 1

        return lax.fori_loop(0, (counts_ref[r] + 1) >> 1, one, n)

    used = lax.fori_loop(0, row_blocks, row, 0)
    for i in range(UNROLL):
        pairs_ref[used + i] = none
    return (used + UNROLL - 1) // UNROLL


def over_pairs(place_ref, counts_ref, adj_hbm, adj, pairs, sems, steps, work, add):
    row_blocks = counts_ref.shape[0]
    none = adj.shape[0]
    shift = (none // row_blocks).bit_length() - 1

    def step(i, ready):
        slots = [pairs[i * UNROLL + u] for u in range(UNROLL)]
        inside = [slot & (none - 1) for slot in slots]
        rows = [at >> shift for at in inside]
        last = functools.reduce(jnp.maximum, rows)
        lax.fori_loop(ready, last + 1, load_rows(counts_ref, adj_hbm, adj, sems, False), 0)
        parts = []
        for slot, at, r in zip(slots, inside, rows):
            both = jnp.concatenate([adj[at], adj[at + 1]], axis=1)
            parts.append((r, *work(r, both, (place_ref[slot], place_ref[slot + 1]))))
        for part in parts:
            add(*part)
        return jnp.maximum(ready, last + 1)

    lax.fori_loop(0, steps, step, 0)


def split_place(where, rows, block):
    return where >> (rows.bit_length() - 1), pl.ds(pl.multiple_of(where & (rows - 1), block), block)


def fwd_kernel(spots, place_ref, counts_ref, adj_hbm, cot_ref, *refs):
    srcs, (out_ref, xs, adj, acc, pairs, sems, rsems) = refs[:-7], refs[-7:]
    row_blocks, _, block = acc.shape
    nodes, rows = xs.shape[0] - 1, xs.shape[2]
    copies = []
    for ref, at in zip(srcs, spots):
        for n, q in enumerate(at):
            src = ref if len(at) == 1 else ref.at[n]
            copies.append(pltpu.make_async_copy(src, xs.at[q], sems.at[q]))
    for c in copies:
        c.start()
    lax.fori_loop(0, row_blocks, load_rows(counts_ref, adj_hbm, adj, rsems, True), 0)
    steps = list_pairs(counts_ref, pairs, adj.shape[0])
    acc[...] = jnp.zeros_like(acc)
    xs[nodes] = jnp.zeros_like(xs[nodes])
    for r in range(row_blocks):
        out_ref[r, :, block:] = cot_ref[:, r * block : (r + 1) * block]
    for c in copies:
        c.wait()

    def work(r, both, places):
        x = []
        for where in places:
            q, at = split_place(where, rows, block)
            x.append(xs[q, :, at])
        x = jnp.concatenate(x, axis=1)
        return (lax.dot_general(x, both, (((1,), (1,)), ((), ())), preferred_element_type=F32),)

    def add(r, got):
        acc[r] += got

    over_pairs(place_ref, counts_ref, adj_hbm, adj, pairs, rsems, steps, work, add)
    for r in range(row_blocks):
        out_ref[r, :, :block] = acc[r].astype(BF16)


def mid_kernel(order_ref, got_ref, near_ref, far_ref, out_ref, wt):
    hid, width, _ = got_ref.shape
    block = got_ref.shape[2] // 2
    total = hid * width
    half = hid // 2
    for n in range(half):
        wt[order_ref[n]] = near_ref[n]
        wt[order_ref[half + n]] = far_ref[n]
    wall = wt[...].reshape(total, wt.shape[2])
    w = wall[:, :total]
    bias = jnp.sum(wall[:, total:].astype(F32), axis=1, keepdims=True)
    got = got_ref[...].reshape(total, 2 * block)
    agg, cot = got[:, :block], got[:, block:].astype(F32)
    pre = jnp.dot(w, agg, preferred_element_type=F32) + bias
    sig = jax.nn.sigmoid(pre)
    hidden = (pre * sig).astype(BF16)
    slope = (cot * sig * (1.0 + pre * (1.0 - sig))).astype(BF16)
    ws = lax.dot_general(w, slope, (((0,), (0,)), ((), ())), preferred_element_type=F32)
    wg = lax.dot_general(slope, agg, (((1,), (1,)), ((), ())), preferred_element_type=F32)
    bsum = jnp.sum(slope.astype(F32), axis=1, keepdims=True)
    hi = bsum.astype(BF16).astype(F32)
    mid = (bsum - hi).astype(BF16).astype(F32)
    low = bsum - hi - mid
    lane = lax.broadcasted_iota(jnp.int32, (total, 128), 1)
    tail = jnp.where(lane == 0, hi, jnp.where(lane == 1, mid, jnp.where(lane == 2, low, 0.0)))
    out_ref[:, :, :block] = ws.astype(BF16).reshape(hid, width, block)
    out_ref[:, :, block : 2 * block] = hidden.reshape(hid, width, block)
    out_ref[:, :, 2 * block : 2 * block + total] = wg.astype(BF16).reshape(hid, width, total)
    out_ref[:, :, 2 * block + total :] = tail.astype(BF16).reshape(hid, width, 128)


def bwd_kernel(
    place_ref, counts_ref, dest_ref, adj_hbm, got_ref,
    hidden_ref, own_ref, d2p, d2m, r1, l1, r2, l2, acc, ext, adj, pairs, rsems,
):
    nodes, (width, rows) = acc.shape[0] - 1, acc.shape[1:]
    block = adj.shape[1]
    row_blocks = counts_ref.shape[0]
    total = nodes * width
    lax.fori_loop(0, row_blocks, load_rows(counts_ref, adj_hbm, adj, rsems, True), 0)
    steps = list_pairs(counts_ref, pairs, adj.shape[0])
    acc[...] = jnp.zeros_like(acc)

    def work(r, both, places):
        made = jnp.dot(got_ref[r, :, :block], both, preferred_element_type=F32)
        return made, places

    def add(r, made, places):
        for n, where in enumerate(places):
            q, at = split_place(where, rows, block)
            acc[q, :, at] += made[:, n * block : (n + 1) * block]

    over_pairs(place_ref, counts_ref, adj_hbm, adj, pairs, rsems, steps, work, add)

    wg = jnp.zeros((width, total), F32)
    tail = jnp.zeros((width, 128), F32)
    for b in range(row_blocks):
        hidden_ref[:, b * block : (b + 1) * block] = got_ref[b, :, block : 2 * block]
        wg = wg + got_ref[b, :, 2 * block : 2 * block + total].astype(F32)
        tail = tail + got_ref[b, :, 2 * block + total :].astype(F32)
    bsum = jnp.sum(tail, axis=1, keepdims=True)
    hi = bsum.astype(BF16).astype(F32)
    mid = (bsum - hi).astype(BF16).astype(F32)
    low = bsum - hi - mid
    lane = lax.broadcasted_iota(jnp.int32, (width, 128), 1)
    first = width + dest_ref[nodes]
    tail = jnp.where(lane == first, hi, 0.0)
    tail = jnp.where(lane == first + nodes, mid, tail)
    tail = jnp.where(lane == first + 2 * nodes, low, tail)
    for a in range(nodes):
        tile = wg[:, (a * width) // 128 * 128 : (a * width) // 128 * 128 + 128]
        start = (a * width) % 128
        if start:
            tile = pltpu.roll(tile, 128 - start, 1)
        ext[dest_ref[a]] = jnp.where(lane < width, tile, tail)

    def put(ref, n, q):
        ref[n, :, :rows] = acc[q].astype(BF16)
        ref[n, :, rows:] = ext[q].astype(BF16)

    for s in range(ZN):
        put(own_ref, s, s)
        right, left = (r2, l2) if s < 2 else (r1, l1)
        put(right, s % 2, ZN + s)
        put(left, s % 2, 3 * ZN + s)
    for n, s in enumerate((2, 0)):
        put(d2p, n, 2 * ZN + s)
        put(d2m, n, 2 * ZN + s + 1)


def relay_kernel(r1, l1, r2, l2, from_left, from_right, r1_out, l1_out, r2_out, l2_out):
    for n, (right, left, right_out, left_out) in enumerate(
        ((r1, l1, r1_out, l1_out), (r2, l2, r2_out, l2_out))
    ):
        right_out[0] = (right[0].astype(F32) + from_left[n].astype(F32)).astype(BF16)
        right_out[1] = right[1]
        left_out[0] = left[0]
        left_out[1] = (left[1].astype(F32) + from_right[n].astype(F32)).astype(BF16)


def joined(own_ref, right, left, s):
    n = s % 2
    return own_ref[s].astype(F32) + right[n].astype(F32) + left[n].astype(F32)


def join_far_kernel(own_ref, right, left, s2, s3):
    s2[...] = joined(own_ref, right, left, 2)
    s3[...] = joined(own_ref, right, left, 3).astype(BF16)


def join_near_kernel(own_ref, right, left, s1):
    s1[...] = joined(own_ref, right, left, 1).astype(BF16)


def last_kernel(scale, own_ref, right, left, near, far, feat_ref, wg_ref, bias_ref):
    total = joined(own_ref, right, left, 0) + near[...].astype(F32) + far[...].astype(F32)
    width, rows = feat_ref.shape
    feat_ref[...] = total[:, :rows].astype(BF16)
    tail = total[:, rows:]
    lane = lax.broadcasted_iota(jnp.int32, tail.shape, 1)
    bsum = jnp.sum(jnp.where(lane >= width, tail, 0.0), axis=1, keepdims=True)
    bias_ref[...] = jnp.broadcast_to(bsum * scale, (width, 128)).T[:1]
    wg_ref[...] = tail[:, :width].T * scale


def spec(space):
    return pl.BlockSpec(memory_space=space)


def params(mib):
    return pltpu.CompilerParams(vmem_limit_bytes=mib * MIB)


def per_device(feats, weight, bias, adjacency, columns, counts, cotangent):
    width, rows = feats.shape
    row_blocks, capacity, block, _ = adjacency.shape
    nodes, hid = lax.axis_size("node"), lax.axis_size("hid")
    total = weight.shape[0]
    scale = 1.0 / math.sqrt(nodes * rows)
    me, mine = lax.axis_index("node"), lax.axis_index("hid")
    x, z = me // ZN, me % ZN

    def rel(a):
        return ((a // ZN - x) % ZN) * ZN + ((a % ZN) ^ z)

    everyone = jnp.arange(nodes, dtype=jnp.int32)
    dest = jnp.concatenate([rel(everyone), me[None].astype(jnp.int32)])
    live = lax.broadcasted_iota(jnp.int32, columns.shape, 1) < counts[:, None]
    place = rel(columns // row_blocks) * rows + columns % row_blocks * block
    place = jnp.where(live, place, nodes * rows).reshape(-1)
    place = jnp.pad(place, (0, 2), constant_values=nodes * rows).astype(jnp.int32)
    blocks = adjacency.reshape(row_blocks * capacity, block, block)

    with jax.named_scope("node_gather"):
        z2 = flip_z(feats, 2, nodes)
        z1 = flip_z(feats, 1, nodes)
        z3 = flip_z(z2, 1, nodes)
        z12 = jnp.stack([z1, z2])
        left = [shift_x(v, 1, nodes) for v in (feats, z12, z3)]
        right = [shift_x(v, -1, nodes) for v in (feats, z12, z3)]
        across = [
            shift_x(left[0], 1, nodes),
            shift_x(right[1][0], -1, nodes),
            shift_x(left[1][1], 1, nodes),
            shift_x(right[2], -1, nodes),
        ]
    sources = [feats, z12, z3, *right, *across, *left]
    spots = ((0,), (1, 2), (3,), (4,), (5, 6), (7,), (8,), (9,), (10,), (11,), (12,), (13, 14), (15,))

    with jax.named_scope("weight_gather"):
        weight, bias, _ = lax.optimization_barrier((weight, bias, left[1]))
        lanes = jnp.stack(split3(bias), axis=1).astype(BF16)
        near = jnp.concatenate([weight.T, jnp.pad(lanes, ((0, 0), (0, 125)))], axis=1)[None]

        def hid_flip(v, by):
            return lax.ppermute(v, "hid", [(i, i ^ by) for i in range(hid)])

        masks = [0]
        for by in (hid // 2, 2, 4):
            near = jnp.concatenate([near, hid_flip(near, by)])
            masks += [m ^ by for m in masks]
        far = hid_flip(near, 1)
        masks += [m ^ 1 for m in masks]
        order = mine.astype(jnp.int32) ^ jnp.array(masks, jnp.int32)

    with jax.named_scope("aggregate"):
        agg = pl.pallas_call(
            functools.partial(fwd_kernel, spots),
            out_shape=jax.ShapeDtypeStruct((row_blocks, width, 2 * block), BF16),
            in_specs=[spec(pltpu.SMEM)] * 2
            + [spec(pl.ANY), spec(VMEM)]
            + [spec(pl.ANY)] * len(sources),
            out_specs=spec(VMEM),
            scratch_shapes=[
                VMEM((nodes + 1, width, rows), BF16),
                VMEM(blocks.shape, BF16),
                VMEM((row_blocks, width, block), F32),
                pltpu.SMEM((row_blocks * capacity // 2 + UNROLL,), jnp.int32),
                pltpu.SemaphoreType.DMA((nodes,)),
                pltpu.SemaphoreType.DMA((row_blocks, capacity // QUARTER)),
            ],
            compiler_params=params(16),
        )(place, counts, blocks, cotangent, *sources)
    got = lax.all_to_all(agg, "hid", 0, 0, tiled=True)

    with jax.named_scope("dense"):
        made = pl.pallas_call(
            mid_kernel,
            out_shape=jax.ShapeDtypeStruct((hid, width, 2 * block + total + 128), BF16),
            in_specs=[spec(pltpu.SMEM)] + [spec(VMEM)] * 3,
            out_specs=spec(VMEM),
            scratch_shapes=[VMEM((hid, width, total + 128), BF16)],
            compiler_params=params(16),
        )(order, got, near, far)
    back = lax.all_to_all(made, "hid", 0, 0, tiled=True)

    wide = rows + 128
    one = jax.ShapeDtypeStruct((width, wide), BF16)
    two = jax.ShapeDtypeStruct((2, width, wide), BF16)
    with jax.named_scope("spread"):
        hidden, own, d2p, d2m, r1, l1, r2, l2 = pl.pallas_call(
            bwd_kernel,
            out_shape=[
                jax.ShapeDtypeStruct((width, rows), BF16),
                jax.ShapeDtypeStruct((ZN, width, wide), BF16),
            ]
            + [two] * 6,
            in_specs=[spec(pltpu.SMEM)] * 3 + [spec(pl.ANY), spec(VMEM)],
            out_specs=[spec(VMEM)] * 8,
            scratch_shapes=[
                VMEM((nodes + 1, width, rows), F32),
                VMEM((nodes, width, 128), F32),
                VMEM(blocks.shape, BF16),
                pltpu.SMEM((row_blocks * capacity // 2 + UNROLL,), jnp.int32),
                pltpu.SemaphoreType.DMA((row_blocks, capacity // QUARTER)),
            ],
            compiler_params=params(24),
        )(place, counts, dest, blocks, back)

    def small(kernel, outs, *args):
        return pl.pallas_call(
            kernel,
            out_shape=outs,
            in_specs=[spec(VMEM)] * len(args),
            out_specs=[spec(VMEM)] * len(outs),
            compiler_params=params(8),
        )(*args)

    with jax.named_scope("node_sum"):
        from_left, from_right = shift_x(d2p, 1, nodes), shift_x(d2m, -1, nodes)
        r1, l1, r2, l2 = small(relay_kernel, [two] * 4, r1, l1, r2, l2, from_left, from_right)
        r1, l1 = shift_x(r1, 1, nodes), shift_x(l1, -1, nodes)
        r2, l2 = shift_x(r2, 1, nodes), shift_x(l2, -1, nodes)
        s2, s3 = small(join_far_kernel, [jax.ShapeDtypeStruct(one.shape, F32), one], own, r1, l1)
        far = (s2 + flip_z(s3, 1, nodes).astype(F32)).astype(BF16)
        far = flip_z(far, 2, nodes)
        (s1,) = small(join_near_kernel, [one], own, r2, l2)
        near = flip_z(s1, 1, nodes)
        feat_grad, weight_grad, bias_grad = small(
            functools.partial(last_kernel, scale),
            [
                jax.ShapeDtypeStruct((width, rows), BF16),
                jax.ShapeDtypeStruct((width, width), F32),
                jax.ShapeDtypeStruct((1, width), F32),
            ],
            own, r2, l2, near, far,
        )
    return hidden, feat_grad, weight_grad, bias_grad.reshape(width)


def solution(mesh):
    placed = (
        P("hid", "node"),
        P(None, "hid"),
        P("hid"),
        P("node", None, None, None),
        P("node", None),
        P("node"),
        P("hid", "node"),
    )
    return jax.shard_map(
        per_device,
        mesh=mesh,
        in_specs=placed,
        out_specs=(P("hid", "node"), P("hid", "node"), P("node", "hid"), P("hid")),
        check_vma=False,
    )
```

```python
import functools
import math

import jax
import jax.numpy as jnp
from jax import lax
from jax.experimental import pallas as pl
from jax.experimental.pallas import tpu as pltpu
from jax.sharding import PartitionSpec as P

F32 = jnp.float32
BF16 = jnp.bfloat16
ZN = 4
UNROLL = 4
QUARTER = 4
VMEM = pltpu.VMEM
MIB = 1024 * 1024
AGG, SPR = 56, 50


def shift_x(v, by, n):
    return lax.ppermute(v, "node", [(i, (i + ZN * by) % n) for i in range(n)])


def flip_z(v, by, n):
    return lax.ppermute(v, "node", [(i, i ^ by) for i in range(n)])


def split3(v):
    hi = lax.reduce_precision(v, 8, 7)
    mid = lax.reduce_precision(v - hi, 8, 7)
    return hi, mid, v - hi - mid


def load_rows(counts_ref, adj_hbm, adj, sems, begin):
    row_blocks, pieces = sems.shape

    def one(r, q):
        at = pl.ds((r * pieces + q) * QUARTER, QUARTER)
        return pltpu.make_async_copy(adj_hbm.at[at], adj.at[at], sems.at[r, q])

    def row(r, carry):
        for q in range(pieces):

            @pl.when(counts_ref[r] > q * QUARTER)
            def _():
                one(r, q).start() if begin else one(r, q).wait()

        return carry

    return row


def list_pairs(counts_ref, pairs_ref, none):
    row_blocks = counts_ref.shape[0]
    capacity = none // row_blocks

    def row(r, n):
        def one(p, n):
            pairs_ref[n] = r * capacity + 2 * p
            return n + 1

        return lax.fori_loop(0, (counts_ref[r] + 1) >> 1, one, n)

    used = lax.fori_loop(0, row_blocks, row, 0)
    for i in range(UNROLL):
        pairs_ref[used + i] = none
    return (used + UNROLL - 1) // UNROLL


def over_pairs(place_ref, counts_ref, adj_hbm, adj, pairs, sems, steps, work, add):
    row_blocks = counts_ref.shape[0]
    none = adj.shape[0]
    shift = (none // row_blocks).bit_length() - 1

    def step(i, ready):
        slots = [pairs[i * UNROLL + u] for u in range(UNROLL)]
        inside = [slot & (none - 1) for slot in slots]
        rows = [at >> shift for at in inside]
        last = functools.reduce(jnp.maximum, rows)
        lax.fori_loop(ready, last + 1, load_rows(counts_ref, adj_hbm, adj, sems, False), 0)
        parts = []
        for slot, at, r in zip(slots, inside, rows):
            both = jnp.concatenate([adj[at], adj[at + 1]], axis=1)
            parts.append((r, *work(r, both, (place_ref[slot], place_ref[slot + 1]))))
        for part in parts:
            add(*part)
        return jnp.maximum(ready, last + 1)

    lax.fori_loop(0, steps, step, 0)


def split_place(where, rows, block):
    return where >> (rows.bit_length() - 1), pl.ds(pl.multiple_of(where & (rows - 1), block), block)


def fwd_kernel(place_ref, counts_ref, adj_hbm, cot_ref, *refs):
    srcs, (out_ref, xs, adj, acc, pairs, sems, rsems) = refs[:-7], refs[-7:]
    row_blocks, _, block = acc.shape
    nodes, rows = xs.shape[0] - 1, xs.shape[2]
    copies = [pltpu.make_async_copy(srcs[q], xs.at[q], sems.at[q]) for q in range(nodes)]
    for c in copies:
        c.start()
    lax.fori_loop(0, row_blocks, load_rows(counts_ref, adj_hbm, adj, rsems, True), 0)
    steps = list_pairs(counts_ref, pairs, adj.shape[0])
    acc[...] = jnp.zeros_like(acc)
    xs[nodes] = jnp.zeros_like(xs[nodes])
    for r in range(row_blocks):
        out_ref[r, :, block:] = cot_ref[:, r * block : (r + 1) * block]
    for c in copies:
        c.wait()

    def work(r, both, places):
        x = []
        for where in places:
            q, at = split_place(where, rows, block)
            x.append(xs[q, :, at])
        x = jnp.concatenate(x, axis=1)
        return (lax.dot_general(x, both, (((1,), (1,)), ((), ())), preferred_element_type=F32),)

    def add(r, got):
        acc[r] += got

    over_pairs(place_ref, counts_ref, adj_hbm, adj, pairs, rsems, steps, work, add)
    for r in range(row_blocks):
        out_ref[r, :, :block] = acc[r].astype(BF16)


def mid_kernel(order_ref, got_ref, near_ref, far_ref, out_ref, wt):
    hid, width, _ = got_ref.shape
    block = got_ref.shape[2] // 2
    total = hid * width
    half = hid // 2
    for n in range(half):
        wt[order_ref[n]] = near_ref[n]
        wt[order_ref[half + n]] = far_ref[n]
    wall = wt[...].reshape(total, wt.shape[2])
    w = wall[:, :total]
    bias = jnp.sum(wall[:, total:].astype(F32), axis=1, keepdims=True)
    got = got_ref[...].reshape(total, 2 * block)
    agg, cot = got[:, :block], got[:, block:].astype(F32)
    pre = jnp.dot(w, agg, preferred_element_type=F32) + bias
    sig = jax.nn.sigmoid(pre)
    hidden = (pre * sig).astype(BF16)
    slope = (cot * sig * (1.0 + pre * (1.0 - sig))).astype(BF16)
    ws = lax.dot_general(w, slope, (((0,), (0,)), ((), ())), preferred_element_type=F32)
    wg = lax.dot_general(slope, agg, (((1,), (1,)), ((), ())), preferred_element_type=F32)
    bsum = jnp.sum(slope.astype(F32), axis=1, keepdims=True)
    hi = bsum.astype(BF16).astype(F32)
    mid = (bsum - hi).astype(BF16).astype(F32)
    low = bsum - hi - mid
    lane = lax.broadcasted_iota(jnp.int32, (total, 128), 1)
    tail = jnp.where(lane == 0, hi, jnp.where(lane == 1, mid, jnp.where(lane == 2, low, 0.0)))
    out_ref[:, :, :block] = ws.astype(BF16).reshape(hid, width, block)
    out_ref[:, :, block : 2 * block] = hidden.reshape(hid, width, block)
    out_ref[:, :, 2 * block : 2 * block + total] = wg.astype(BF16).reshape(hid, width, total)
    out_ref[:, :, 2 * block + total :] = tail.astype(BF16).reshape(hid, width, 128)


def bwd_kernel(
    place_ref, counts_ref, dest_ref, adj_hbm, got_ref,
    hidden_ref, own_ref, d2p, d2m, r1, l1, r2, l2, acc, ext, adj, pairs, rsems,
):
    nodes, (width, rows) = acc.shape[0] - 1, acc.shape[1:]
    block = adj.shape[1]
    row_blocks = counts_ref.shape[0]
    total = nodes * width
    lax.fori_loop(0, row_blocks, load_rows(counts_ref, adj_hbm, adj, rsems, True), 0)
    steps = list_pairs(counts_ref, pairs, adj.shape[0])
    acc[...] = jnp.zeros_like(acc)

    def work(r, both, places):
        made = jnp.dot(got_ref[r, :, :block], both, preferred_element_type=F32)
        return made, places

    def add(r, made, places):
        for n, where in enumerate(places):
            q, at = split_place(where, rows, block)
            acc[q, :, at] += made[:, n * block : (n + 1) * block]

    over_pairs(place_ref, counts_ref, adj_hbm, adj, pairs, rsems, steps, work, add)

    wg = jnp.zeros((width, total), F32)
    tail = jnp.zeros((width, 128), F32)
    for b in range(row_blocks):
        hidden_ref[:, b * block : (b + 1) * block] = got_ref[b, :, block : 2 * block]
        wg = wg + got_ref[b, :, 2 * block : 2 * block + total].astype(F32)
        tail = tail + got_ref[b, :, 2 * block + total :].astype(F32)
    bsum = jnp.sum(tail, axis=1, keepdims=True)
    hi = bsum.astype(BF16).astype(F32)
    mid = (bsum - hi).astype(BF16).astype(F32)
    low = bsum - hi - mid
    lane = lax.broadcasted_iota(jnp.int32, (width, 128), 1)
    first = width + dest_ref[nodes]
    tail = jnp.where(lane == first, hi, 0.0)
    tail = jnp.where(lane == first + nodes, mid, tail)
    tail = jnp.where(lane == first + 2 * nodes, low, tail)
    for a in range(nodes):
        tile = wg[:, (a * width) // 128 * 128 : (a * width) // 128 * 128 + 128]
        start = (a * width) % 128
        if start:
            tile = pltpu.roll(tile, 128 - start, 1)
        ext[dest_ref[a]] = jnp.where(lane < width, tile, tail)

    def put(ref, n, q):
        ref[n, :, :rows] = acc[q].astype(BF16)
        ref[n, :, rows:] = ext[q].astype(BF16)

    for s in range(ZN):
        put(own_ref, s, s)
        right, left = (r2, l2) if s < 2 else (r1, l1)
        put(right, s % 2, ZN + s)
        put(left, s % 2, 3 * ZN + s)
    for n, s in enumerate((2, 0)):
        put(d2p, n, 2 * ZN + s)
        put(d2m, n, 2 * ZN + s + 1)


def relay_kernel(r1, l1, r2, l2, from_left, from_right, r1_out, l1_out, r2_out, l2_out):
    for n, (right, left, right_out, left_out) in enumerate(
        ((r1, l1, r1_out, l1_out), (r2, l2, r2_out, l2_out))
    ):
        right_out[0] = (right[0].astype(F32) + from_left[n].astype(F32)).astype(BF16)
        right_out[1] = right[1]
        left_out[0] = left[0]
        left_out[1] = (left[1].astype(F32) + from_right[n].astype(F32)).astype(BF16)


def joined(own_ref, right, left, s):
    n = s % 2
    return own_ref[s].astype(F32) + right[n].astype(F32) + left[n].astype(F32)


def join_far_kernel(own_ref, right, left, s2, s3):
    s2[...] = joined(own_ref, right, left, 2)
    s3[...] = joined(own_ref, right, left, 3).astype(BF16)


def join_near_kernel(own_ref, right, left, s1):
    s1[...] = joined(own_ref, right, left, 1).astype(BF16)


def last_kernel(scale, own_ref, right, left, near, far, feat_ref, wg_ref, bias_ref):
    total = joined(own_ref, right, left, 0) + near[...].astype(F32) + far[...].astype(F32)
    width, rows = feat_ref.shape
    feat_ref[...] = total[:, :rows].astype(BF16)
    tail = total[:, rows:]
    lane = lax.broadcasted_iota(jnp.int32, tail.shape, 1)
    bsum = jnp.sum(jnp.where(lane >= width, tail, 0.0), axis=1, keepdims=True)
    bias_ref[...] = jnp.broadcast_to(bsum * scale, (width, 128)).T[:1]
    wg_ref[...] = tail[:, :width].T * scale


def spec(space):
    return pl.BlockSpec(memory_space=space)


def cost(us):
    return pl.CostEstimate(flops=0, bytes_accessed=int(us * 3e6), transcendentals=0)


def params(mib):
    return pltpu.CompilerParams(vmem_limit_bytes=mib * MIB)


def per_device(feats, weight, bias, adjacency, columns, counts, cotangent):
    width, rows = feats.shape
    row_blocks, capacity, block, _ = adjacency.shape
    nodes, hid = lax.axis_size("node"), lax.axis_size("hid")
    total = weight.shape[0]
    scale = 1.0 / math.sqrt(nodes * rows)
    me, mine = lax.axis_index("node"), lax.axis_index("hid")
    x, z = me // ZN, me % ZN

    def rel(a):
        return ((a // ZN - x) % ZN) * ZN + ((a % ZN) ^ z)

    everyone = jnp.arange(nodes, dtype=jnp.int32)
    dest = jnp.concatenate([rel(everyone), me[None].astype(jnp.int32)])
    live = lax.broadcasted_iota(jnp.int32, columns.shape, 1) < counts[:, None]
    place = rel(columns // row_blocks) * rows + columns % row_blocks * block
    place = jnp.where(live, place, nodes * rows).reshape(-1)
    place = jnp.pad(place, (0, 2), constant_values=nodes * rows).astype(jnp.int32)
    blocks = adjacency.reshape(row_blocks * capacity, block, block)

    with jax.named_scope("node_gather"):
        here = [feats] + [flip_z(feats, s, nodes) for s in range(1, ZN)]
        left = [shift_x(v, 1, nodes) for v in here]
        right = [shift_x(v, -1, nodes) for v in here]
        across = [shift_x(left[s], 1, nodes) for s in (0, 1)]
        across += [shift_x(right[s], -1, nodes) for s in (2, 3)]
    sources = here + right + across + left

    def hid_flip(v, by):
        return lax.ppermute(v, "hid", [(i, i ^ by) for i in range(hid)])

    with jax.named_scope("weight_gather"):
        weight, bias, _ = lax.optimization_barrier((weight, bias, here[1:]))
        lanes = jnp.stack(split3(bias), axis=1).astype(BF16)
        near = jnp.concatenate([weight.T, jnp.pad(lanes, ((0, 0), (0, 125)))], axis=1)[None]
        back = hid_flip(near, hid // 2)

    with jax.named_scope("aggregate"):
        agg = pl.pallas_call(
            fwd_kernel,
            out_shape=jax.ShapeDtypeStruct((row_blocks, width, 2 * block), BF16),
            in_specs=[spec(pltpu.SMEM)] * 2
            + [spec(pl.ANY), spec(VMEM)]
            + [spec(pl.ANY)] * len(sources),
            out_specs=spec(VMEM),
            scratch_shapes=[
                VMEM((nodes + 1, width, rows), BF16),
                VMEM(blocks.shape, BF16),
                VMEM((row_blocks, width, block), F32),
                pltpu.SMEM((row_blocks * capacity // 2 + UNROLL,), jnp.int32),
                pltpu.SemaphoreType.DMA((nodes,)),
                pltpu.SemaphoreType.DMA((row_blocks, capacity // QUARTER)),
            ],
            compiler_params=params(AGG),
            cost_estimate=cost(9),
        )(place, counts, blocks, cotangent, *sources)
    got = lax.all_to_all(agg, "hid", 0, 0, tiled=True)

    with jax.named_scope("weight_gather"):
        near, back, _ = lax.optimization_barrier((near, back, agg))
        near = jnp.concatenate([near, back])
        masks = [0, hid // 2]
        for by in (2, 4):
            near = jnp.concatenate([near, hid_flip(near, by)])
            masks += [m ^ by for m in masks]
        far = hid_flip(near, 1)
        masks += [m ^ 1 for m in masks]
        order = mine.astype(jnp.int32) ^ jnp.array(masks, jnp.int32)

    with jax.named_scope("dense"):
        made = pl.pallas_call(
            mid_kernel,
            out_shape=jax.ShapeDtypeStruct((hid, width, 2 * block + total + 128), BF16),
            in_specs=[spec(pltpu.SMEM)] + [spec(VMEM)] * 3,
            out_specs=spec(VMEM),
            scratch_shapes=[VMEM((hid, width, total + 128), BF16)],
            compiler_params=params(16),
        )(order, got, near, far)
    back = lax.all_to_all(made, "hid", 0, 0, tiled=True)

    wide = rows + 128
    one = jax.ShapeDtypeStruct((width, wide), BF16)
    two = jax.ShapeDtypeStruct((2, width, wide), BF16)
    with jax.named_scope("spread"):
        hidden, own, d2p, d2m, r1, l1, r2, l2 = pl.pallas_call(
            bwd_kernel,
            out_shape=[
                jax.ShapeDtypeStruct((width, rows), BF16),
                jax.ShapeDtypeStruct((ZN, width, wide), BF16),
            ]
            + [two] * 6,
            in_specs=[spec(pltpu.SMEM)] * 3 + [spec(pl.ANY), spec(VMEM)],
            out_specs=[spec(VMEM)] * 8,
            scratch_shapes=[
                VMEM((nodes + 1, width, rows), F32),
                VMEM((nodes, width, 128), F32),
                VMEM(blocks.shape, BF16),
                pltpu.SMEM((row_blocks * capacity // 2 + UNROLL,), jnp.int32),
                pltpu.SemaphoreType.DMA((row_blocks, capacity // QUARTER)),
            ],
            compiler_params=params(SPR),
            cost_estimate=cost(9),
        )(place, counts, dest, blocks, back)

    def small(kernel, outs, *args):
        return pl.pallas_call(
            kernel,
            out_shape=outs,
            in_specs=[spec(VMEM)] * len(args),
            out_specs=[spec(VMEM)] * len(outs),
            compiler_params=params(8),
        )(*args)

    with jax.named_scope("node_sum"):
        from_left, from_right = shift_x(d2p, 1, nodes), shift_x(d2m, -1, nodes)
        r1, l1, r2, l2 = small(relay_kernel, [two] * 4, r1, l1, r2, l2, from_left, from_right)
        r1, l1 = shift_x(r1, 1, nodes), shift_x(l1, -1, nodes)
        r2, l2 = shift_x(r2, 1, nodes), shift_x(l2, -1, nodes)
        s2, s3 = small(join_far_kernel, [jax.ShapeDtypeStruct(one.shape, F32), one], own, r1, l1)
        far = (s2 + flip_z(s3, 1, nodes).astype(F32)).astype(BF16)
        far = flip_z(far, 2, nodes)
        (s1,) = small(join_near_kernel, [one], own, r2, l2)
        near = flip_z(s1, 1, nodes)
        feat_grad, weight_grad, bias_grad = small(
            functools.partial(last_kernel, scale),
            [
                jax.ShapeDtypeStruct((width, rows), BF16),
                jax.ShapeDtypeStruct((width, width), F32),
                jax.ShapeDtypeStruct((1, width), F32),
            ],
            own, r2, l2, near, far,
        )
    return hidden, feat_grad, weight_grad, bias_grad.reshape(width)


def solution(mesh):
    placed = (
        P("hid", "node"),
        P(None, "hid"),
        P("hid"),
        P("node", None, None, None),
        P("node", None),
        P("node"),
        P("hid", "node"),
    )
    return jax.shard_map(
        per_device,
        mesh=mesh,
        in_specs=placed,
        out_specs=(P("hid", "node"), P("hid", "node"), P("node", "hid"), P("hid")),
        check_vma=False,
    )
```

```python
import functools
import math

import jax
import jax.numpy as jnp
from jax import lax
from jax.experimental import pallas as pl
from jax.experimental.pallas import tpu as pltpu
from jax.sharding import PartitionSpec as P

F32 = jnp.float32
BF16 = jnp.bfloat16
ZN = 4
UNROLL = 8
QUARTER = 4
VMEM = pltpu.VMEM
MIB = 1024 * 1024
AGG, SPR = 56, 50


def shift_x(v, by, n):
    return lax.ppermute(v, "node", [(i, (i + ZN * by) % n) for i in range(n)])


def flip_z(v, by, n):
    return lax.ppermute(v, "node", [(i, i ^ by) for i in range(n)])


def split3(v):
    hi = v.astype(BF16).astype(F32)
    mid = (v - hi).astype(BF16).astype(F32)
    low = v - hi - mid
    lane = lax.broadcasted_iota(jnp.int32, (v.shape[0], 128), 1)
    return jnp.where(lane == 0, hi, jnp.where(lane == 1, mid, jnp.where(lane == 2, low, 0.0)))


def load_rows(counts_ref, adj_hbm, adj, sems, begin):
    row_blocks, pieces = sems.shape

    def one(r, q):
        at = pl.ds((r * pieces + q) * QUARTER, QUARTER)
        return pltpu.make_async_copy(adj_hbm.at[at], adj.at[at], sems.at[r, q])

    def row(r, carry):
        for q in range(pieces):

            @pl.when(counts_ref[r] > q * QUARTER)
            def _():
                one(r, q).start() if begin else one(r, q).wait()

        return carry

    return row


def list_pairs(counts_ref, pairs_ref, none):
    row_blocks = counts_ref.shape[0]
    capacity = none // row_blocks

    def row(r, n):
        def one(p, n):
            pairs_ref[n] = r * capacity + 2 * p
            return n + 1

        return lax.fori_loop(0, (counts_ref[r] + 1) >> 1, one, n)

    used = lax.fori_loop(0, row_blocks, row, 0)
    for i in range(UNROLL):
        pairs_ref[used + i] = none
    return (used + UNROLL - 1) // UNROLL


def over_pairs(place_ref, counts_ref, adj_hbm, adj, pairs, sems, steps, work, add):
    row_blocks = counts_ref.shape[0]
    none = adj.shape[0]
    shift = (none // row_blocks).bit_length() - 1

    def step(i, ready):
        slots = [pairs[i * UNROLL + u] for u in range(UNROLL)]
        inside = [slot & (none - 1) for slot in slots]
        rows = [at >> shift for at in inside]
        last = functools.reduce(jnp.maximum, rows)
        lax.fori_loop(ready, last + 1, load_rows(counts_ref, adj_hbm, adj, sems, False), 0)
        parts = []
        for slot, at, r in zip(slots, inside, rows):
            both = jnp.concatenate([adj[at], adj[at + 1]], axis=1)
            parts.append((r, *work(r, both, (place_ref[slot], place_ref[slot + 1]))))
        for part in parts:
            add(*part)
        return jnp.maximum(ready, last + 1)

    lax.fori_loop(0, steps, step, 0)


def split_place(where, rows, block):
    return where >> (rows.bit_length() - 1), pl.ds(pl.multiple_of(where & (rows - 1), block), block)


def fwd_kernel(place_ref, counts_ref, adj_hbm, cot_ref, wt_ref, bias_ref, *refs):
    srcs, (out_ref, xs, adj, acc, pairs, sems, rsems) = refs[:-7], refs[-7:]
    row_blocks, _, block = acc.shape
    nodes, rows = xs.shape[0] - 1, xs.shape[2]
    copies = [pltpu.make_async_copy(srcs[q], xs.at[q], sems.at[q]) for q in range(nodes)]
    for c in copies:
        c.start()
    lax.fori_loop(0, row_blocks, load_rows(counts_ref, adj_hbm, adj, rsems, True), 0)
    steps = list_pairs(counts_ref, pairs, adj.shape[0])
    acc[...] = jnp.zeros_like(acc)
    xs[nodes] = jnp.zeros_like(xs[nodes])
    width, total = wt_ref.shape
    bias = jnp.broadcast_to(bias_ref[...], (width, width)).T[:, :1]
    tail = split3(bias).astype(BF16)
    for r in range(row_blocks):
        out_ref[r, :, block : 2 * block] = cot_ref[:, r * block : (r + 1) * block]
        out_ref[r, :, 2 * block : 2 * block + total] = wt_ref[...]
        out_ref[r, :, 2 * block + total :] = tail
    for c in copies:
        c.wait()

    def work(r, both, places):
        x = []
        for where in places:
            q, at = split_place(where, rows, block)
            x.append(xs[q, :, at])
        x = jnp.concatenate(x, axis=1)
        return (lax.dot_general(x, both, (((1,), (1,)), ((), ())), preferred_element_type=F32),)

    def add(r, got):
        acc[r] += got

    over_pairs(place_ref, counts_ref, adj_hbm, adj, pairs, rsems, steps, work, add)
    for r in range(row_blocks):
        out_ref[r, :, :block] = acc[r].astype(BF16)


def mid_kernel(got_ref, out_ref):
    hid, width, _ = got_ref.shape
    total = hid * width
    block = (got_ref.shape[2] - 128 - total) // 2
    got = got_ref[...].reshape(total, got_ref.shape[2])
    agg, cot = got[:, :block], got[:, block : 2 * block].astype(F32)
    w = got[:, 2 * block : 2 * block + total]
    bias = jnp.sum(got[:, 2 * block + total :].astype(F32), axis=1, keepdims=True)
    pre = jnp.dot(w, agg, preferred_element_type=F32) + bias
    sig = jax.nn.sigmoid(pre)
    hidden = (pre * sig).astype(BF16)
    slope = (cot * sig * (1.0 + pre * (1.0 - sig))).astype(BF16)
    ws = lax.dot_general(w, slope, (((0,), (0,)), ((), ())), preferred_element_type=F32)
    wg = lax.dot_general(slope, agg, (((1,), (1,)), ((), ())), preferred_element_type=F32)
    bsum = jnp.sum(slope.astype(F32), axis=1, keepdims=True)
    tail = split3(bsum)
    out_ref[:, :, :block] = ws.astype(BF16).reshape(hid, width, block)
    out_ref[:, :, block : 2 * block] = hidden.reshape(hid, width, block)
    out_ref[:, :, 2 * block : 2 * block + total] = wg.astype(BF16).reshape(hid, width, total)
    out_ref[:, :, 2 * block + total :] = tail.astype(BF16).reshape(hid, width, 128)


def bwd_kernel(
    place_ref, counts_ref, dest_ref, adj_hbm, got_ref,
    hidden_ref, own_ref, d2p, d2m, r1, l1, r2, l2, acc, ext, adj, pairs, rsems,
):
    nodes, (width, rows) = acc.shape[0] - 1, acc.shape[1:]
    block = adj.shape[1]
    row_blocks = counts_ref.shape[0]
    total = nodes * width
    lax.fori_loop(0, row_blocks, load_rows(counts_ref, adj_hbm, adj, rsems, True), 0)
    steps = list_pairs(counts_ref, pairs, adj.shape[0])
    acc[...] = jnp.zeros_like(acc)

    def work(r, both, places):
        made = jnp.dot(got_ref[r, :, :block], both, preferred_element_type=F32)
        return made, places

    def add(r, made, places):
        for n, where in enumerate(places):
            q, at = split_place(where, rows, block)
            acc[q, :, at] += made[:, n * block : (n + 1) * block]

    over_pairs(place_ref, counts_ref, adj_hbm, adj, pairs, rsems, steps, work, add)

    wg = jnp.zeros((width, total), F32)
    tail = jnp.zeros((width, 128), F32)
    for b in range(row_blocks):
        hidden_ref[:, b * block : (b + 1) * block] = got_ref[b, :, block : 2 * block]
        wg = wg + got_ref[b, :, 2 * block : 2 * block + total].astype(F32)
        tail = tail + got_ref[b, :, 2 * block + total :].astype(F32)
    bsum = jnp.sum(tail, axis=1, keepdims=True)
    hi = bsum.astype(BF16).astype(F32)
    mid = (bsum - hi).astype(BF16).astype(F32)
    low = bsum - hi - mid
    lane = lax.broadcasted_iota(jnp.int32, (width, 128), 1)
    first = width + dest_ref[nodes]
    tail = jnp.where(lane == first, hi, 0.0)
    tail = jnp.where(lane == first + nodes, mid, tail)
    tail = jnp.where(lane == first + 2 * nodes, low, tail)
    for a in range(nodes):
        tile = wg[:, (a * width) // 128 * 128 : (a * width) // 128 * 128 + 128]
        start = (a * width) % 128
        if start:
            tile = pltpu.roll(tile, 128 - start, 1)
        ext[dest_ref[a]] = jnp.where(lane < width, tile, tail)

    def put(ref, n, q):
        ref[n, :, :rows] = acc[q].astype(BF16)
        ref[n, :, rows:] = ext[q].astype(BF16)

    for s in range(ZN):
        put(own_ref, s, s)
        right, left = (r2, l2) if s < 2 else (r1, l1)
        put(right, s % 2, ZN + s)
        put(left, s % 2, 3 * ZN + s)
    for n, s in enumerate((2, 0)):
        put(d2p, n, 2 * ZN + s)
        put(d2m, n, 2 * ZN + s + 1)


def relay_kernel(r1, l1, r2, l2, from_left, from_right, r1_out, l1_out, r2_out, l2_out):
    for n, (right, left, right_out, left_out) in enumerate(
        ((r1, l1, r1_out, l1_out), (r2, l2, r2_out, l2_out))
    ):
        right_out[0] = (right[0].astype(F32) + from_left[n].astype(F32)).astype(BF16)
        right_out[1] = right[1]
        left_out[0] = left[0]
        left_out[1] = (left[1].astype(F32) + from_right[n].astype(F32)).astype(BF16)


def joined(own_ref, right, left, s):
    n = s % 2
    return own_ref[s].astype(F32) + right[n].astype(F32) + left[n].astype(F32)


def join_far_kernel(own_ref, right, left, s2, s3):
    s2[...] = joined(own_ref, right, left, 2)
    s3[...] = joined(own_ref, right, left, 3).astype(BF16)


def join_near_kernel(own_ref, right, left, s1):
    s1[...] = joined(own_ref, right, left, 1).astype(BF16)


def last_kernel(scale, own_ref, right, left, near, far, feat_ref, wg_ref, bias_ref):
    total = joined(own_ref, right, left, 0) + near[...].astype(F32) + far[...].astype(F32)
    width, rows = feat_ref.shape
    feat_ref[...] = total[:, :rows].astype(BF16)
    tail = total[:, rows:]
    lane = lax.broadcasted_iota(jnp.int32, tail.shape, 1)
    bsum = jnp.sum(jnp.where(lane >= width, tail, 0.0), axis=1, keepdims=True)
    bias_ref[...] = jnp.broadcast_to(bsum * scale, (width, 128)).T[:1]
    wg_ref[...] = tail[:, :width].T * scale


def spec(space):
    return pl.BlockSpec(memory_space=space)


def cost(us):
    return pl.CostEstimate(flops=0, bytes_accessed=int(us * 3e6), transcendentals=0)


def params(mib):
    return pltpu.CompilerParams(vmem_limit_bytes=mib * MIB)


def per_device(feats, weight, bias, adjacency, columns, counts, cotangent):
    width, rows = feats.shape
    row_blocks, capacity, block, _ = adjacency.shape
    nodes, hid = lax.axis_size("node"), lax.axis_size("hid")
    total = weight.shape[0]
    scale = 1.0 / math.sqrt(nodes * rows)
    me = lax.axis_index("node")
    x, z = me // ZN, me % ZN

    def rel(a):
        return ((a // ZN - x) % ZN) * ZN + ((a % ZN) ^ z)

    everyone = jnp.arange(nodes, dtype=jnp.int32)
    dest = jnp.concatenate([rel(everyone), me[None].astype(jnp.int32)])
    live = lax.broadcasted_iota(jnp.int32, columns.shape, 1) < counts[:, None]
    place = rel(columns // row_blocks) * rows + columns % row_blocks * block
    place = jnp.where(live, place, nodes * rows).reshape(-1)
    place = jnp.pad(place, (0, 2), constant_values=nodes * rows).astype(jnp.int32)
    blocks = adjacency.reshape(row_blocks * capacity, block, block)

    with jax.named_scope("node_gather"):
        here = [feats] + [flip_z(feats, s, nodes) for s in range(1, ZN)]
        left = [shift_x(v, 1, nodes) for v in here]
        right = [shift_x(v, -1, nodes) for v in here]
        across = [shift_x(left[s], 1, nodes) for s in (0, 1)]
        across += [shift_x(right[s], -1, nodes) for s in (2, 3)]
    sources = here + right + across + left

    with jax.named_scope("aggregate"):
        agg = pl.pallas_call(
            fwd_kernel,
            out_shape=jax.ShapeDtypeStruct((row_blocks, width, 2 * block + total + 128), BF16),
            in_specs=[spec(pltpu.SMEM)] * 2
            + [spec(pl.ANY)]
            + [spec(VMEM)] * 3
            + [spec(pl.ANY)] * len(sources),
            out_specs=spec(VMEM),
            scratch_shapes=[
                VMEM((nodes + 1, width, rows), BF16),
                VMEM(blocks.shape, BF16),
                VMEM((row_blocks, width, block), F32),
                pltpu.SMEM((row_blocks * capacity // 2 + UNROLL,), jnp.int32),
                pltpu.SemaphoreType.DMA((nodes,)),
                pltpu.SemaphoreType.DMA((row_blocks, capacity // QUARTER)),
            ],
            compiler_params=params(AGG),
            cost_estimate=cost(9),
        )(place, counts, blocks, cotangent, weight.T, bias.reshape(1, width), *sources)
    got = lax.all_to_all(agg, "hid", 0, 0, tiled=True)

    with jax.named_scope("dense"):
        made = pl.pallas_call(
            mid_kernel,
            out_shape=jax.ShapeDtypeStruct((hid, width, 2 * block + total + 128), BF16),
            in_specs=[spec(VMEM)],
            out_specs=spec(VMEM),
            compiler_params=params(16),
        )(got)
    back = lax.all_to_all(made, "hid", 0, 0, tiled=True)

    wide = rows + 128
    one = jax.ShapeDtypeStruct((width, wide), BF16)
    two = jax.ShapeDtypeStruct((2, width, wide), BF16)
    with jax.named_scope("spread"):
        hidden, own, d2p, d2m, r1, l1, r2, l2 = pl.pallas_call(
            bwd_kernel,
            out_shape=[
                jax.ShapeDtypeStruct((width, rows), BF16),
                jax.ShapeDtypeStruct((ZN, width, wide), BF16),
            ]
            + [two] * 6,
            in_specs=[spec(pltpu.SMEM)] * 3 + [spec(pl.ANY), spec(VMEM)],
            out_specs=[spec(VMEM)] * 8,
            scratch_shapes=[
                VMEM((nodes + 1, width, rows), F32),
                VMEM((nodes, width, 128), F32),
                VMEM(blocks.shape, BF16),
                pltpu.SMEM((row_blocks * capacity // 2 + UNROLL,), jnp.int32),
                pltpu.SemaphoreType.DMA((row_blocks, capacity // QUARTER)),
            ],
            compiler_params=params(SPR),
            cost_estimate=cost(9),
        )(place, counts, dest, blocks, back)

    def small(kernel, outs, *args):
        return pl.pallas_call(
            kernel,
            out_shape=outs,
            in_specs=[spec(VMEM)] * len(args),
            out_specs=[spec(VMEM)] * len(outs),
            compiler_params=params(8),
        )(*args)

    with jax.named_scope("node_sum"):
        from_left, from_right = shift_x(d2p, 1, nodes), shift_x(d2m, -1, nodes)
        r1, l1, r2, l2 = small(relay_kernel, [two] * 4, r1, l1, r2, l2, from_left, from_right)
        r1, l1 = shift_x(r1, 1, nodes), shift_x(l1, -1, nodes)
        r1, l1, r2, l2 = lax.optimization_barrier((r1, l1, r2, l2))
        r2, l2 = shift_x(r2, 1, nodes), shift_x(l2, -1, nodes)
        s2, s3 = small(join_far_kernel, [jax.ShapeDtypeStruct(one.shape, F32), one], own, r1, l1)
        far = (s2 + flip_z(s3, 1, nodes).astype(F32)).astype(BF16)
        far = flip_z(far, 2, nodes)
        (s1,) = small(join_near_kernel, [one], own, r2, l2)
        near = flip_z(s1, 1, nodes)
        feat_grad, weight_grad, bias_grad = small(
            functools.partial(last_kernel, scale),
            [
                jax.ShapeDtypeStruct((width, rows), BF16),
                jax.ShapeDtypeStruct((width, width), F32),
                jax.ShapeDtypeStruct((1, width), F32),
            ],
            own, r2, l2, near, far,
        )
    return hidden, feat_grad, weight_grad, bias_grad.reshape(width)


def solution(mesh):
    placed = (
        P("hid", "node"),
        P(None, "hid"),
        P("hid"),
        P("node", None, None, None),
        P("node", None),
        P("node"),
        P("hid", "node"),
    )
    return jax.shard_map(
        per_device,
        mesh=mesh,
        in_specs=placed,
        out_specs=(P("hid", "node"), P("hid", "node"), P("node", "hid"), P("hid")),
        check_vma=False,
    )
```

```python
import functools
import math

import jax
import jax.numpy as jnp
from jax import lax
from jax.experimental import pallas as pl
from jax.experimental.pallas import tpu as pltpu
from jax.sharding import PartitionSpec as P

F32 = jnp.float32
BF16 = jnp.bfloat16
ZN = 4
UNROLL = 8
QUARTER = 4
VMEM = pltpu.VMEM
MIB = 1024 * 1024
AGG, SPR = 56, 50


def shift_x(v, by, n):
    return lax.ppermute(v, "node", [(i, (i + ZN * by) % n) for i in range(n)])


def flip_z(v, by, n):
    return lax.ppermute(v, "node", [(i, i ^ by) for i in range(n)])


def split3(v):
    hi = v.astype(BF16).astype(F32)
    mid = (v - hi).astype(BF16).astype(F32)
    low = v - hi - mid
    lane = lax.broadcasted_iota(jnp.int32, (v.shape[0], 128), 1)
    return jnp.where(lane == 0, hi, jnp.where(lane == 1, mid, jnp.where(lane == 2, low, 0.0)))


def load_rows(counts_ref, adj_hbm, adj, sems, begin):
    row_blocks, pieces = sems.shape

    def one(r, q):
        at = pl.ds((r * pieces + q) * QUARTER, QUARTER)
        return pltpu.make_async_copy(adj_hbm.at[at], adj.at[at], sems.at[r, q])

    def row(r, carry):
        for q in range(pieces):

            @pl.when(counts_ref[r] > q * QUARTER)
            def _():
                one(r, q).start() if begin else one(r, q).wait()

        return carry

    return row


def list_pairs(counts_ref, pairs_ref, none):
    row_blocks = counts_ref.shape[0]
    capacity = none // row_blocks

    def row(r, n):
        def one(p, n):
            pairs_ref[n] = r * capacity + 2 * p
            return n + 1

        return lax.fori_loop(0, (counts_ref[r] + 1) >> 1, one, n)

    used = lax.fori_loop(0, row_blocks, row, 0)
    for i in range(UNROLL):
        pairs_ref[used + i] = none
    return (used + UNROLL - 1) // UNROLL


def over_pairs(place_ref, counts_ref, adj_hbm, adj, pairs, sems, steps, work, add):
    row_blocks = counts_ref.shape[0]
    none = adj.shape[0]
    shift = (none // row_blocks).bit_length() - 1

    def step(i, ready):
        slots = [pairs[i * UNROLL + u] for u in range(UNROLL)]
        inside = [slot & (none - 1) for slot in slots]
        rows = [at >> shift for at in inside]
        last = functools.reduce(jnp.maximum, rows)
        lax.fori_loop(ready, last + 1, load_rows(counts_ref, adj_hbm, adj, sems, False), 0)
        parts = []
        for slot, at, r in zip(slots, inside, rows):
            both = jnp.concatenate([adj[at], adj[at + 1]], axis=1)
            parts.append((r, *work(r, both, (place_ref[slot], place_ref[slot + 1]))))
        for part in parts:
            add(*part)
        return jnp.maximum(ready, last + 1)

    lax.fori_loop(0, steps, step, 0)


def split_place(where, rows, block):
    return where >> (rows.bit_length() - 1), pl.ds(pl.multiple_of(where & (rows - 1), block), block)


def pack_kernel(cot_ref, wt_ref, bias_ref, out_ref):
    parts = out_ref.shape[0]
    width, total = wt_ref.shape
    span = cot_ref.shape[1] // parts
    bias = jnp.broadcast_to(bias_ref[...], (width, width)).T[:, :1]
    tail = split3(bias).astype(BF16)
    for p in range(parts):
        out_ref[p, :, :span] = cot_ref[:, p * span : (p + 1) * span]
        out_ref[p, :, span : span + total] = wt_ref[...]
        out_ref[p, :, span + total :] = tail


def fwd_kernel(place_ref, counts_ref, adj_hbm, *refs):
    srcs, (out_ref, xs, adj, acc, pairs, sems, rsems) = refs[:-7], refs[-7:]
    row_blocks, _, block = acc.shape
    nodes, rows = xs.shape[0] - 1, xs.shape[2]
    copies = [pltpu.make_async_copy(srcs[q], xs.at[q], sems.at[q]) for q in range(nodes)]
    for c in copies:
        c.start()
    lax.fori_loop(0, row_blocks, load_rows(counts_ref, adj_hbm, adj, rsems, True), 0)
    steps = list_pairs(counts_ref, pairs, adj.shape[0])
    acc[...] = jnp.zeros_like(acc)
    xs[nodes] = jnp.zeros_like(xs[nodes])
    for c in copies:
        c.wait()

    def work(r, both, places):
        x = []
        for where in places:
            q, at = split_place(where, rows, block)
            x.append(xs[q, :, at])
        x = jnp.concatenate(x, axis=1)
        return (lax.dot_general(x, both, (((1,), (1,)), ((), ())), preferred_element_type=F32),)

    def add(r, got):
        acc[r] += got

    over_pairs(place_ref, counts_ref, adj_hbm, adj, pairs, rsems, steps, work, add)
    for r in range(row_blocks):
        done = acc[r].astype(BF16)
        for p in (r // 2, (row_blocks + r) // 2):
            out_ref[p, :, r % 2 * block : (r % 2 + 1) * block] = done


def mid_kernel(agg_ref, row_ref, cross_ref, stay_ref):
    hid, width, span = agg_ref.shape
    half = row_ref.shape[0]
    total = hid * width
    agg = agg_ref[...].reshape(total, span)
    row = row_ref[...].reshape(half * width, row_ref.shape[2])
    cot = row[:, :span].astype(F32)
    wt = row[:, span : span + total]
    bias = jnp.sum(row[:, span + total :].astype(F32), axis=1, keepdims=True)
    pre = jnp.dot(wt, agg, preferred_element_type=F32) + bias
    sig = jax.nn.sigmoid(pre)
    hidden = (pre * sig).astype(BF16)
    slope = (cot * sig * (1.0 + pre * (1.0 - sig))).astype(BF16)
    ws = lax.dot_general(wt, slope, (((0,), (0,)), ((), ())), preferred_element_type=F32)
    cross_ref[...] = ws.astype(BF16).reshape(hid, width, span)
    wg = lax.dot_general(slope, agg, (((1,), (1,)), ((), ())), preferred_element_type=F32)
    tail = split3(jnp.sum(slope.astype(F32), axis=1, keepdims=True))
    stay_ref[:, :, :span] = hidden.reshape(half, width, span)
    stay_ref[:, :, span : span + total] = wg.astype(BF16).reshape(half, width, total)
    stay_ref[:, :, span + total :] = tail.astype(BF16).reshape(half, width, 128)


def bwd_kernel(
    place_ref, counts_ref, adj_hbm, cross_ref,
    own_ref, d2p, d2m, r1, l1, r2, l2, acc, adj, ws, pairs, rsems,
):
    nodes, (width, rows) = acc.shape[0] - 1, acc.shape[1:]
    block = adj.shape[1]
    row_blocks = counts_ref.shape[0]
    lax.fori_loop(0, row_blocks, load_rows(counts_ref, adj_hbm, adj, rsems, True), 0)
    steps = list_pairs(counts_ref, pairs, adj.shape[0])
    acc[...] = jnp.zeros_like(acc)
    half = row_blocks // 2
    for p in range(half):
        both_halves = cross_ref[p].astype(F32) + cross_ref[half + p].astype(F32)
        ws[2 * p] = both_halves[:, :block].astype(BF16)
        ws[2 * p + 1] = both_halves[:, block:].astype(BF16)

    def work(r, both, places):
        made = jnp.dot(ws[r], both, preferred_element_type=F32)
        return made, places

    def add(r, made, places):
        for n, where in enumerate(places):
            q, at = split_place(where, rows, block)
            acc[q, :, at] += made[:, n * block : (n + 1) * block]

    over_pairs(place_ref, counts_ref, adj_hbm, adj, pairs, rsems, steps, work, add)

    def put(ref, n, q):
        ref[n] = acc[q].astype(BF16)

    for s in range(ZN):
        put(own_ref, s, s)
        right, left = (r2, l2) if s < 2 else (r1, l1)
        put(right, s % 2, ZN + s)
        put(left, s % 2, 3 * ZN + s)
    for n, s in enumerate((2, 0)):
        put(d2p, n, 2 * ZN + s)
        put(d2m, n, 2 * ZN + s + 1)


def fold_kernel(stay_ref, hidden_ref, out_ref):
    nodes, width, _ = out_ref.shape
    total = nodes * width
    half = stay_ref.shape[0]
    span = hidden_ref.shape[1] // half
    wg = jnp.zeros((width, total), F32)
    tail = jnp.zeros((width, 128), F32)
    for p in range(half):
        hidden_ref[:, p * span : (p + 1) * span] = stay_ref[p, :, :span]
        wg = wg + stay_ref[p, :, span : span + total].astype(F32)
        tail = tail + stay_ref[p, :, span + total :].astype(F32)
    tail = pltpu.roll(split3(jnp.sum(tail, axis=1, keepdims=True)), width, 1)
    lane = lax.broadcasted_iota(jnp.int32, (width, 128), 1)
    for a in range(nodes):
        tile = wg[:, (a * width) // 128 * 128 : (a * width) // 128 * 128 + 128]
        start = (a * width) % 128
        if start:
            tile = pltpu.roll(tile, 128 - start, 1)
        out_ref[a] = jnp.where(lane < width, tile, tail).astype(BF16)


def relay_kernel(r1, l1, r2, l2, from_left, from_right, r1_out, l1_out, r2_out, l2_out):
    for n, (right, left, right_out, left_out) in enumerate(
        ((r1, l1, r1_out, l1_out), (r2, l2, r2_out, l2_out))
    ):
        right_out[0] = (right[0].astype(F32) + from_left[n].astype(F32)).astype(BF16)
        right_out[1] = right[1]
        left_out[0] = left[0]
        left_out[1] = (left[1].astype(F32) + from_right[n].astype(F32)).astype(BF16)


def joined(own_ref, right, left, s):
    n = s % 2
    return own_ref[s].astype(F32) + right[n].astype(F32) + left[n].astype(F32)


def join_far_kernel(own_ref, right, left, s2, s3):
    s2[...] = joined(own_ref, right, left, 2)
    s3[...] = joined(own_ref, right, left, 3).astype(BF16)


def join_near_kernel(own_ref, right, left, s1):
    s1[...] = joined(own_ref, right, left, 1).astype(BF16)


def last_kernel(scale, own_ref, right, left, near, far, parts_ref, feat_ref, wg_ref, bias_ref):
    total = joined(own_ref, right, left, 0) + near[...].astype(F32) + far[...].astype(F32)
    feat_ref[...] = total.astype(BF16)
    width = feat_ref.shape[0]
    tail = parts_ref[0].astype(F32)
    for a in range(1, parts_ref.shape[0]):
        tail = tail + parts_ref[a].astype(F32)
    lane = lax.broadcasted_iota(jnp.int32, tail.shape, 1)
    bsum = jnp.sum(jnp.where(lane >= width, tail, 0.0), axis=1, keepdims=True)
    bias_ref[...] = jnp.broadcast_to(bsum * scale, (width, 128)).T[:1]
    wg_ref[...] = tail[:, :width].T * scale


def spec(space):
    return pl.BlockSpec(memory_space=space)


def cost(us):
    return pl.CostEstimate(flops=0, bytes_accessed=int(us * 3e6), transcendentals=0)


def params(mib):
    return pltpu.CompilerParams(vmem_limit_bytes=mib * MIB)


def per_device(feats, weight, bias, adjacency, columns, counts, cotangent):
    width, rows = feats.shape
    row_blocks, capacity, block, _ = adjacency.shape
    nodes, hid = lax.axis_size("node"), lax.axis_size("hid")
    total = weight.shape[0]
    scale = 1.0 / math.sqrt(nodes * rows)
    me = lax.axis_index("node")
    x, z = me // ZN, me % ZN

    def rel(a):
        return ((a // ZN - x) % ZN) * ZN + ((a % ZN) ^ z)

    live = lax.broadcasted_iota(jnp.int32, columns.shape, 1) < counts[:, None]
    place = rel(columns // row_blocks) * rows + columns % row_blocks * block
    place = jnp.where(live, place, nodes * rows).reshape(-1)
    place = jnp.pad(place, (0, 2), constant_values=nodes * rows).astype(jnp.int32)
    blocks = adjacency.reshape(row_blocks * capacity, block, block)

    with jax.named_scope("node_gather"):
        here = [feats] + [flip_z(feats, s, nodes) for s in range(1, ZN)]
        left = [shift_x(v, 1, nodes) for v in here]
        right = [shift_x(v, -1, nodes) for v in here]
        across = [shift_x(left[s], 1, nodes) for s in (0, 1)]
        across += [shift_x(right[s], -1, nodes) for s in (2, 3)]
    sources = here + right + across + left

    half = hid // 2
    span = rows // half
    halves = [list(range(half)), list(range(half, hid))]

    def exchange_half(v):
        return lax.all_to_all(v, "hid", 0, 0, axis_index_groups=halves, tiled=True)

    def exchange(v):
        return lax.all_to_all(v, "hid", 0, 0, tiled=True)

    with jax.named_scope("pack"):
        stay = jax.ShapeDtypeStruct((half, width, span + total + 128), BF16)
        row = pl.pallas_call(
            pack_kernel,
            out_shape=stay,
            in_specs=[spec(VMEM)] * 3,
            out_specs=spec(VMEM),
            compiler_params=params(8),
        )(cotangent, weight.T, bias.reshape(1, width))
        row, _ = lax.optimization_barrier((row, sources))
        row = exchange_half(row)

    with jax.named_scope("aggregate"):
        agg = pl.pallas_call(
            fwd_kernel,
            out_shape=jax.ShapeDtypeStruct((hid, width, span), BF16),
            in_specs=[spec(pltpu.SMEM)] * 2 + [spec(pl.ANY)] * (1 + len(sources)),
            out_specs=spec(VMEM),
            scratch_shapes=[
                VMEM((nodes + 1, width, rows), BF16),
                VMEM(blocks.shape, BF16),
                VMEM((row_blocks, width, block), F32),
                pltpu.SMEM((row_blocks * capacity // 2 + UNROLL,), jnp.int32),
                pltpu.SemaphoreType.DMA((nodes,)),
                pltpu.SemaphoreType.DMA((row_blocks, capacity // QUARTER)),
            ],
            compiler_params=params(AGG),
            cost_estimate=cost(9),
        )(place, counts, blocks, *sources)
    agg = exchange(agg)

    with jax.named_scope("dense"):
        cross, kept = pl.pallas_call(
            mid_kernel,
            out_shape=[jax.ShapeDtypeStruct((hid, width, span), BF16), stay],
            in_specs=[spec(VMEM)] * 2,
            out_specs=[spec(VMEM)] * 2,
            compiler_params=params(16),
        )(agg, row)
    cross = exchange(cross)
    kept, cross = lax.optimization_barrier((kept, cross))
    kept = exchange_half(kept)

    one = jax.ShapeDtypeStruct((width, rows), BF16)
    two = jax.ShapeDtypeStruct((2, width, rows), BF16)
    with jax.named_scope("spread"):
        own, d2p, d2m, r1, l1, r2, l2 = pl.pallas_call(
            bwd_kernel,
            out_shape=[jax.ShapeDtypeStruct((ZN, width, rows), BF16)] + [two] * 6,
            in_specs=[spec(pltpu.SMEM)] * 2 + [spec(pl.ANY), spec(VMEM)],
            out_specs=[spec(VMEM)] * 7,
            scratch_shapes=[
                VMEM((nodes + 1, width, rows), F32),
                VMEM(blocks.shape, BF16),
                VMEM((row_blocks, width, block), BF16),
                pltpu.SMEM((row_blocks * capacity // 2 + UNROLL,), jnp.int32),
                pltpu.SemaphoreType.DMA((row_blocks, capacity // QUARTER)),
            ],
            compiler_params=params(SPR),
            cost_estimate=cost(9),
        )(place, counts, blocks, cross)

    def small(kernel, outs, *args):
        return pl.pallas_call(
            kernel,
            out_shape=outs,
            in_specs=[spec(VMEM)] * len(args),
            out_specs=[spec(VMEM)] * len(outs),
            compiler_params=params(8),
        )(*args)

    with jax.named_scope("node_sum"):
        from_left, from_right = shift_x(d2p, 1, nodes), shift_x(d2m, -1, nodes)
        kept, _ = lax.optimization_barrier((kept, (from_left, from_right)))
        hidden, parts = small(
            fold_kernel, [one, jax.ShapeDtypeStruct((nodes, width, 128), BF16)], kept
        )
        parts = lax.all_to_all(parts, "node", 0, 0, tiled=True)
        r1, l1, r2, l2 = small(relay_kernel, [two] * 4, r1, l1, r2, l2, from_left, from_right)
        r1, l1 = shift_x(r1, 1, nodes), shift_x(l1, -1, nodes)
        r1, l1, r2, l2 = lax.optimization_barrier((r1, l1, r2, l2))
        r2, l2 = shift_x(r2, 1, nodes), shift_x(l2, -1, nodes)
        s2, s3 = small(join_far_kernel, [jax.ShapeDtypeStruct(one.shape, F32), one], own, r1, l1)
        far = (s2 + flip_z(s3, 1, nodes).astype(F32)).astype(BF16)
        far = flip_z(far, 2, nodes)
        (s1,) = small(join_near_kernel, [one], own, r2, l2)
        near = flip_z(s1, 1, nodes)
        feat_grad, weight_grad, bias_grad = small(
            functools.partial(last_kernel, scale),
            [
                jax.ShapeDtypeStruct((width, rows), BF16),
                jax.ShapeDtypeStruct((width, width), F32),
                jax.ShapeDtypeStruct((1, width), F32),
            ],
            own, r2, l2, near, far, parts,
        )
    return hidden, feat_grad, weight_grad, bias_grad.reshape(width)


def solution(mesh):
    placed = (
        P("hid", "node"),
        P(None, "hid"),
        P("hid"),
        P("node", None, None, None),
        P("node", None),
        P("node"),
        P("hid", "node"),
    )
    return jax.shard_map(
        per_device,
        mesh=mesh,
        in_specs=placed,
        out_specs=(P("hid", "node"), P("hid", "node"), P("node", "hid"), P("hid")),
        check_vma=False,
    )
```

```python
import functools
import math

import jax
import jax.numpy as jnp
from jax import lax
from jax.experimental import pallas as pl
from jax.experimental.pallas import tpu as pltpu
from jax.sharding import PartitionSpec as P

F32 = jnp.float32
BF16 = jnp.bfloat16
ZN = 4
UNROLL = 8
QUARTER = 4
VMEM = pltpu.VMEM
MIB = 1024 * 1024
AGG, SPR = 56, 50


def shift_x(v, by, n):
    return lax.ppermute(v, "node", [(i, (i + ZN * by) % n) for i in range(n)])


def flip_z(v, by, n):
    return lax.ppermute(v, "node", [(i, i ^ by) for i in range(n)])


def split3(v):
    hi = v.astype(BF16).astype(F32)
    mid = (v - hi).astype(BF16).astype(F32)
    low = v - hi - mid
    lane = lax.broadcasted_iota(jnp.int32, (v.shape[0], 128), 1)
    return jnp.where(lane == 0, hi, jnp.where(lane == 1, mid, jnp.where(lane == 2, low, 0.0)))


def load_rows(counts_ref, adj_hbm, adj, sems, begin):
    row_blocks, pieces = sems.shape

    def one(r, q):
        at = pl.ds((r * pieces + q) * QUARTER, QUARTER)
        return pltpu.make_async_copy(adj_hbm.at[at], adj.at[at], sems.at[r, q])

    def row(r, carry):
        for q in range(pieces):

            @pl.when(counts_ref[r] > q * QUARTER)
            def _():
                one(r, q).start() if begin else one(r, q).wait()

        return carry

    return row


def list_pairs(counts_ref, pairs_ref, none):
    row_blocks = counts_ref.shape[0]
    capacity = none // row_blocks

    def row(r, n):
        def one(p, n):
            pairs_ref[n] = r * capacity + 2 * p
            return n + 1

        return lax.fori_loop(0, (counts_ref[r] + 1) >> 1, one, n)

    used = lax.fori_loop(0, row_blocks, row, 0)
    for i in range(UNROLL):
        pairs_ref[used + i] = none
    return (used + UNROLL - 1) // UNROLL


def over_pairs(place_ref, counts_ref, adj_hbm, adj, pairs, sems, steps, work, add):
    row_blocks = counts_ref.shape[0]
    none = adj.shape[0]
    shift = (none // row_blocks).bit_length() - 1

    def step(i, ready):
        slots = [pairs[i * UNROLL + u] for u in range(UNROLL)]
        inside = [slot & (none - 1) for slot in slots]
        rows = [at >> shift for at in inside]
        last = functools.reduce(jnp.maximum, rows)
        lax.fori_loop(ready, last + 1, load_rows(counts_ref, adj_hbm, adj, sems, False), 0)
        parts = []
        for slot, at, r in zip(slots, inside, rows):
            k = slot & (none // row_blocks - 1)
            both = jnp.concatenate([adj[at], adj[at + 1]], axis=1)
            parts.append((r, *work(r, both, (place_ref[slot >> shift, k], place_ref[slot >> shift, k + 1]))))
        for part in parts:
            add(*part)
        return jnp.maximum(ready, last + 1)

    lax.fori_loop(0, steps, step, 0)


def split_place(where, rows, block):
    return where >> (rows.bit_length() - 1), pl.ds(pl.multiple_of(where & (rows - 1), block), block)


def pack_kernel(me_ref, counts_ref, columns_ref, cot_ref, wt_ref, bias_ref, out_ref, place_ref):
    row_blocks, capacity = columns_ref.shape
    rows, block = cot_ref.shape[1], cot_ref.shape[1] // row_blocks
    x, z = me_ref[0] >> 2, me_ref[0] & (ZN - 1)
    column = columns_ref[...]
    index = lax.div(column, row_blocks)
    plane = (((index >> 2) - x) & (ZN - 1)) * ZN + ((index & (ZN - 1)) ^ z)
    place = plane * rows + lax.rem(column, row_blocks) * block
    slot = lax.broadcasted_iota(jnp.int32, (1, capacity), 1)
    place_ref[...] = jnp.full(place_ref.shape, me_ref[1] * rows, jnp.int32)
    for r in range(row_blocks):
        place_ref[r : r + 1, :capacity] = jnp.where(
            slot < counts_ref[r], place[r : r + 1], me_ref[1] * rows
        )
    parts = out_ref.shape[0]
    width, total = wt_ref.shape
    span = cot_ref.shape[1] // parts
    bias = jnp.broadcast_to(bias_ref[...], (width, width)).T[:, :1]
    tail = split3(bias).astype(BF16)
    for p in range(parts):
        out_ref[p, :, :span] = cot_ref[:, p * span : (p + 1) * span]
        out_ref[p, :, span : span + total] = wt_ref[...]
        out_ref[p, :, span + total :] = tail


def fwd_kernel(place_ref, counts_ref, adj_hbm, *refs):
    srcs, (out_ref, xs, adj, acc, pairs, sems, rsems) = refs[:-7], refs[-7:]
    row_blocks, _, block = acc.shape
    nodes, rows = xs.shape[0] - 1, xs.shape[2]
    copies = [pltpu.make_async_copy(srcs[q], xs.at[q], sems.at[q]) for q in range(nodes)]
    for c in copies:
        c.start()
    lax.fori_loop(0, row_blocks, load_rows(counts_ref, adj_hbm, adj, rsems, True), 0)
    steps = list_pairs(counts_ref, pairs, adj.shape[0])
    acc[...] = jnp.zeros_like(acc)
    xs[nodes] = jnp.zeros_like(xs[nodes])
    for c in copies:
        c.wait()

    def work(r, both, places):
        x = []
        for where in places:
            q, at = split_place(where, rows, block)
            x.append(xs[q, :, at])
        x = jnp.concatenate(x, axis=1)
        return (lax.dot_general(x, both, (((1,), (1,)), ((), ())), preferred_element_type=F32),)

    def add(r, got):
        acc[r] += got

    over_pairs(place_ref, counts_ref, adj_hbm, adj, pairs, rsems, steps, work, add)
    for r in range(row_blocks):
        done = acc[r].astype(BF16)
        for p in (r // 2, (row_blocks + r) // 2):
            out_ref[p, :, r % 2 * block : (r % 2 + 1) * block] = done


def mid_kernel(agg_ref, row_ref, cross_ref, stay_ref):
    hid, width, span = agg_ref.shape
    half = row_ref.shape[0]
    total = hid * width
    agg = agg_ref[...].reshape(total, span)
    row = row_ref[...].reshape(half * width, row_ref.shape[2])
    cot = row[:, :span].astype(F32)
    wt = row[:, span : span + total]
    bias = jnp.sum(row[:, span + total :].astype(F32), axis=1, keepdims=True)
    pre = jnp.dot(wt, agg, preferred_element_type=F32) + bias
    sig = jax.nn.sigmoid(pre)
    hidden = (pre * sig).astype(BF16)
    slope = (cot * sig * (1.0 + pre * (1.0 - sig))).astype(BF16)
    ws = lax.dot_general(wt, slope, (((0,), (0,)), ((), ())), preferred_element_type=F32)
    cross_ref[...] = ws.astype(BF16).reshape(hid, width, span)
    wg = lax.dot_general(slope, agg, (((1,), (1,)), ((), ())), preferred_element_type=F32)
    tail = split3(jnp.sum(slope.astype(F32), axis=1, keepdims=True))
    stay_ref[:, :, :span] = hidden.reshape(half, width, span)
    stay_ref[:, :, span : span + total] = wg.astype(BF16).reshape(half, width, total)
    stay_ref[:, :, span + total :] = tail.astype(BF16).reshape(half, width, 128)


def bwd_kernel(
    place_ref, counts_ref, adj_hbm, cross_ref,
    own_ref, d2p, d2m, r1, l1, r2, l2, acc, adj, ws, pairs, rsems,
):
    nodes, (width, rows) = acc.shape[0] - 1, acc.shape[1:]
    block = adj.shape[1]
    row_blocks = counts_ref.shape[0]
    lax.fori_loop(0, row_blocks, load_rows(counts_ref, adj_hbm, adj, rsems, True), 0)
    steps = list_pairs(counts_ref, pairs, adj.shape[0])
    acc[...] = jnp.zeros_like(acc)
    half = row_blocks // 2
    for p in range(half):
        both_halves = cross_ref[p].astype(F32) + cross_ref[half + p].astype(F32)
        ws[2 * p] = both_halves[:, :block].astype(BF16)
        ws[2 * p + 1] = both_halves[:, block:].astype(BF16)

    def work(r, both, places):
        made = jnp.dot(ws[r], both, preferred_element_type=F32)
        return made, places

    def add(r, made, places):
        for n, where in enumerate(places):
            q, at = split_place(where, rows, block)
            acc[q, :, at] += made[:, n * block : (n + 1) * block]

    over_pairs(place_ref, counts_ref, adj_hbm, adj, pairs, rsems, steps, work, add)

    def put(ref, n, q):
        ref[n] = acc[q].astype(BF16)

    for s in range(ZN):
        put(own_ref, s, s)
        right, left = (r2, l2) if s < 2 else (r1, l1)
        put(right, s % 2, ZN + s)
        put(left, s % 2, 3 * ZN + s)
    for n, s in enumerate((2, 0)):
        put(d2p, n, 2 * ZN + s)
        put(d2m, n, 2 * ZN + s + 1)


def fold_kernel(stay_ref, hidden_ref, out_ref):
    nodes, width, _ = out_ref.shape
    total = nodes * width
    half = stay_ref.shape[0]
    span = hidden_ref.shape[1] // half
    wg = jnp.zeros((width, total), F32)
    tail = jnp.zeros((width, 128), F32)
    for p in range(half):
        hidden_ref[:, p * span : (p + 1) * span] = stay_ref[p, :, :span]
        wg = wg + stay_ref[p, :, span : span + total].astype(F32)
        tail = tail + stay_ref[p, :, span + total :].astype(F32)
    tail = pltpu.roll(split3(jnp.sum(tail, axis=1, keepdims=True)), width, 1)
    lane = lax.broadcasted_iota(jnp.int32, (width, 128), 1)
    for a in range(nodes):
        tile = wg[:, (a * width) // 128 * 128 : (a * width) // 128 * 128 + 128]
        start = (a * width) % 128
        if start:
            tile = pltpu.roll(tile, 128 - start, 1)
        out_ref[a] = jnp.where(lane < width, tile, tail).astype(BF16)


def relay_kernel(r1, l1, r2, l2, from_left, from_right, r1_out, l1_out, r2_out, l2_out):
    for n, (right, left, right_out, left_out) in enumerate(
        ((r1, l1, r1_out, l1_out), (r2, l2, r2_out, l2_out))
    ):
        right_out[0] = (right[0].astype(F32) + from_left[n].astype(F32)).astype(BF16)
        right_out[1] = right[1]
        left_out[0] = left[0]
        left_out[1] = (left[1].astype(F32) + from_right[n].astype(F32)).astype(BF16)


def joined(own_ref, right, left, s):
    n = s % 2
    return own_ref[s].astype(F32) + right[n].astype(F32) + left[n].astype(F32)


def join_far_kernel(own_ref, right, left, s2, s3):
    s2[...] = joined(own_ref, right, left, 2)
    s3[...] = joined(own_ref, right, left, 3).astype(BF16)


def join_near_kernel(own_ref, right, left, s1):
    s1[...] = joined(own_ref, right, left, 1).astype(BF16)


def last_kernel(scale, own_ref, right, left, near, far, parts_ref, feat_ref, wg_ref, bias_ref):
    total = joined(own_ref, right, left, 0) + near[...].astype(F32) + far[...].astype(F32)
    feat_ref[...] = total.astype(BF16)
    width = feat_ref.shape[0]
    tail = parts_ref[0].astype(F32)
    for a in range(1, parts_ref.shape[0]):
        tail = tail + parts_ref[a].astype(F32)
    lane = lax.broadcasted_iota(jnp.int32, tail.shape, 1)
    bsum = jnp.sum(jnp.where(lane >= width, tail, 0.0), axis=1, keepdims=True)
    bias_ref[...] = jnp.broadcast_to(bsum * scale, (width, 128)).T[:1]
    wg_ref[...] = tail[:, :width].T * scale


def spec(space):
    return pl.BlockSpec(memory_space=space)


def cost(us):
    return pl.CostEstimate(flops=0, bytes_accessed=int(us * 3e6), transcendentals=0)


def params(mib):
    return pltpu.CompilerParams(vmem_limit_bytes=mib * MIB)


def per_device(feats, weight, bias, adjacency, columns, counts, cotangent):
    width, rows = feats.shape
    row_blocks, capacity, block, _ = adjacency.shape
    nodes, hid = lax.axis_size("node"), lax.axis_size("hid")
    total = weight.shape[0]
    scale = 1.0 / math.sqrt(nodes * rows)
    me = lax.axis_index("node")
    blocks = adjacency.reshape(row_blocks * capacity, block, block)

    half = hid // 2
    span = rows // half
    halves = [list(range(half)), list(range(half, hid))]

    def exchange_half(v):
        return lax.all_to_all(v, "hid", 0, 0, axis_index_groups=halves, tiled=True)

    def exchange(v):
        return lax.all_to_all(v, "hid", 0, 0, tiled=True)

    with jax.named_scope("pack"):
        stay = jax.ShapeDtypeStruct((half, width, span + total + 128), BF16)
        row, place = pl.pallas_call(
            pack_kernel,
            out_shape=[stay, jax.ShapeDtypeStruct((row_blocks + 8, 128), jnp.int32)],
            in_specs=[spec(pltpu.SMEM)] * 2 + [spec(VMEM)] * 4,
            out_specs=[spec(VMEM)] * 2,
            compiler_params=params(57),
        )(
            jnp.stack([me, nodes]).astype(jnp.int32),
            counts, columns, cotangent, weight.T, bias.reshape(1, width),
        )

    with jax.named_scope("node_gather"):
        z1, z2 = flip_z(feats, 1, nodes), flip_z(feats, 2, nodes)
        here = [feats, z1, z2, flip_z(z2, 1, nodes)]
        here[1], row, place = lax.optimization_barrier((here[1], row, place))
        left = [shift_x(v, 1, nodes) for v in here]
        right = [shift_x(v, -1, nodes) for v in here]
        across = [shift_x(left[s], 1, nodes) for s in (0, 1)]
        across += [shift_x(right[s], -1, nodes) for s in (2, 3)]
    sources = here + right + across + left

    row = exchange_half(lax.optimization_barrier((row, sources))[0])

    with jax.named_scope("aggregate"):
        agg = pl.pallas_call(
            fwd_kernel,
            out_shape=jax.ShapeDtypeStruct((hid, width, span), BF16),
            in_specs=[spec(pltpu.SMEM)] * 2 + [spec(pl.ANY)] * (1 + len(sources)),
            out_specs=spec(VMEM),
            scratch_shapes=[
                VMEM((nodes + 1, width, rows), BF16),
                VMEM(blocks.shape, BF16),
                VMEM((row_blocks, width, block), F32),
                pltpu.SMEM((row_blocks * capacity // 2 + UNROLL,), jnp.int32),
                pltpu.SemaphoreType.DMA((nodes,)),
                pltpu.SemaphoreType.DMA((row_blocks, capacity // QUARTER)),
            ],
            compiler_params=params(AGG),
            cost_estimate=cost(9),
        )(place, counts, blocks, *sources)
    agg = exchange(agg)

    with jax.named_scope("dense"):
        cross, kept = pl.pallas_call(
            mid_kernel,
            out_shape=[jax.ShapeDtypeStruct((hid, width, span), BF16), stay],
            in_specs=[spec(VMEM)] * 2,
            out_specs=[spec(VMEM)] * 2,
            compiler_params=params(16),
        )(agg, row)
    cross = exchange(cross)
    kept, cross = lax.optimization_barrier((kept, cross))
    kept = exchange_half(kept)

    one = jax.ShapeDtypeStruct((width, rows), BF16)
    two = jax.ShapeDtypeStruct((2, width, rows), BF16)
    with jax.named_scope("spread"):
        own, d2p, d2m, r1, l1, r2, l2 = pl.pallas_call(
            bwd_kernel,
            out_shape=[jax.ShapeDtypeStruct((ZN, width, rows), BF16)] + [two] * 6,
            in_specs=[spec(pltpu.SMEM)] * 2 + [spec(pl.ANY), spec(VMEM)],
            out_specs=[spec(VMEM)] * 7,
            scratch_shapes=[
                VMEM((nodes + 1, width, rows), F32),
                VMEM(blocks.shape, BF16),
                VMEM((row_blocks, width, block), BF16),
                pltpu.SMEM((row_blocks * capacity // 2 + UNROLL,), jnp.int32),
                pltpu.SemaphoreType.DMA((row_blocks, capacity // QUARTER)),
            ],
            compiler_params=params(SPR),
            cost_estimate=cost(9),
        )(place, counts, blocks, cross)

    def small(kernel, outs, *args):
        return pl.pallas_call(
            kernel,
            out_shape=outs,
            in_specs=[spec(VMEM)] * len(args),
            out_specs=[spec(VMEM)] * len(outs),
            compiler_params=params(8),
        )(*args)

    with jax.named_scope("node_sum"):
        from_left, from_right = shift_x(d2p, 1, nodes), shift_x(d2m, -1, nodes)
        r1, l1, r2, l2 = small(relay_kernel, [two] * 4, r1, l1, r2, l2, from_left, from_right)
        r1, l1 = shift_x(r1, 1, nodes), shift_x(l1, -1, nodes)
        r1, l1, r2, l2 = lax.optimization_barrier((r1, l1, r2, l2))
        r2, l2 = shift_x(r2, 1, nodes), shift_x(l2, -1, nodes)
        s2, s3 = small(join_far_kernel, [jax.ShapeDtypeStruct(one.shape, F32), one], own, r1, l1)
        s3 = flip_z(s3, 1, nodes)
        kept, _ = lax.optimization_barrier((kept, s3))
        hidden, parts = small(
            fold_kernel, [one, jax.ShapeDtypeStruct((nodes, width, 128), BF16)], kept
        )
        parts = lax.all_to_all(parts, "node", 0, 0, tiled=True)
        far = (s2 + s3.astype(F32)).astype(BF16)
        far = flip_z(far, 2, nodes)
        (s1,) = small(join_near_kernel, [one], own, r2, l2)
        near = flip_z(s1, 1, nodes)
        feat_grad, weight_grad, bias_grad = small(
            functools.partial(last_kernel, scale),
            [
                jax.ShapeDtypeStruct((width, rows), BF16),
                jax.ShapeDtypeStruct((width, width), F32),
                jax.ShapeDtypeStruct((1, width), F32),
            ],
            own, r2, l2, near, far, parts,
        )
    return hidden, feat_grad, weight_grad, bias_grad.reshape(width)


def solution(mesh):
    placed = (
        P("hid", "node"),
        P(None, "hid"),
        P("hid"),
        P("node", None, None, None),
        P("node", None),
        P("node"),
        P("hid", "node"),
    )
    return jax.shard_map(
        per_device,
        mesh=mesh,
        in_specs=placed,
        out_specs=(P("hid", "node"), P("hid", "node"), P("node", "hid"), P("hid")),
        check_vma=False,
    )
```

```python
import functools
import math

import jax
import jax.numpy as jnp
from jax import lax
from jax.experimental import pallas as pl
from jax.experimental.pallas import tpu as pltpu
from jax.sharding import PartitionSpec as P

F32 = jnp.float32
BF16 = jnp.bfloat16
ZN = 4
UNROLL = 8
QUARTER = 4
VMEM = pltpu.VMEM
MIB = 1024 * 1024
AGG, SPR = 56, 50


def shift_x(v, by, n):
    return lax.ppermute(v, "node", [(i, (i + ZN * by) % n) for i in range(n)])


def flip_z(v, by, n):
    return lax.ppermute(v, "node", [(i, i ^ by) for i in range(n)])


def split3(v):
    hi = v.astype(BF16).astype(F32)
    mid = (v - hi).astype(BF16).astype(F32)
    low = v - hi - mid
    lane = lax.broadcasted_iota(jnp.int32, (v.shape[0], 128), 1)
    return jnp.where(lane == 0, hi, jnp.where(lane == 1, mid, jnp.where(lane == 2, low, 0.0)))


def load_rows(counts_ref, adj_hbm, adj, sems, begin):
    row_blocks, pieces = sems.shape

    def one(r, q):
        at = pl.ds((r * pieces + q) * QUARTER, QUARTER)
        return pltpu.make_async_copy(adj_hbm.at[at], adj.at[at], sems.at[r, q])

    def row(r, carry):
        for q in range(pieces):

            @pl.when(counts_ref[r] > q * QUARTER)
            def _():
                one(r, q).start() if begin else one(r, q).wait()

        return carry

    return row


def list_pairs(counts_ref, pairs_ref, none):
    row_blocks = counts_ref.shape[0]
    capacity = none // row_blocks

    def row(r, n):
        def one(p, n):
            pairs_ref[n] = r * capacity + 2 * p
            return n + 1

        return lax.fori_loop(0, (counts_ref[r] + 1) >> 1, one, n)

    used = lax.fori_loop(0, row_blocks, row, 0)
    for i in range(UNROLL):
        pairs_ref[used + i] = none
    return (used + UNROLL - 1) // UNROLL


def over_pairs(place_ref, counts_ref, adj_hbm, adj, pairs, sems, steps, work, add):
    row_blocks = counts_ref.shape[0]
    none = adj.shape[0]
    shift = (none // row_blocks).bit_length() - 1

    def step(i, ready):
        slots = [pairs[i * UNROLL + u] for u in range(UNROLL)]
        inside = [slot & (none - 1) for slot in slots]
        rows = [at >> shift for at in inside]
        last = functools.reduce(jnp.maximum, rows)
        lax.fori_loop(ready, last + 1, load_rows(counts_ref, adj_hbm, adj, sems, False), 0)
        parts = []
        for slot, at, r in zip(slots, inside, rows):
            k = slot & (none // row_blocks - 1)
            both = jnp.concatenate([adj[at], adj[at + 1]], axis=1)
            parts.append((r, *work(r, both, (place_ref[slot >> shift, k], place_ref[slot >> shift, k + 1]))))
        for part in parts:
            add(*part)
        return jnp.maximum(ready, last + 1)

    lax.fori_loop(0, steps, step, 0)


def split_place(where, rows, block):
    return where >> (rows.bit_length() - 1), pl.ds(pl.multiple_of(where & (rows - 1), block), block)


def pack_kernel(me_ref, counts_ref, columns_ref, cot_ref, wt_ref, bias_ref, out_ref, place_ref):
    row_blocks, capacity = columns_ref.shape
    rows, block = cot_ref.shape[1], cot_ref.shape[1] // row_blocks
    x, z = me_ref[0] >> 2, me_ref[0] & (ZN - 1)
    column = columns_ref[...]
    index = lax.div(column, row_blocks)
    plane = (((index >> 2) - x) & (ZN - 1)) * ZN + ((index & (ZN - 1)) ^ z)
    place = plane * rows + lax.rem(column, row_blocks) * block
    slot = lax.broadcasted_iota(jnp.int32, (1, capacity), 1)
    place_ref[...] = jnp.full(place_ref.shape, me_ref[1] * rows, jnp.int32)
    for r in range(row_blocks):
        place_ref[r : r + 1, :capacity] = jnp.where(
            slot < counts_ref[r], place[r : r + 1], me_ref[1] * rows
        )
    width, total = wt_ref.shape
    bias = jnp.broadcast_to(bias_ref[...], (width, width)).T[:, :1]
    out_ref[:, :rows] = cot_ref[...]
    out_ref[:, rows : rows + total] = wt_ref[...]
    out_ref[:, rows + total :] = split3(bias).astype(BF16)


def fwd_kernel(place_ref, counts_ref, adj_hbm, *refs):
    srcs, (out_ref, xs, adj, acc, pairs, sems, rsems) = refs[:-7], refs[-7:]
    row_blocks, _, block = acc.shape
    nodes, rows = xs.shape[0] - 1, xs.shape[2]
    copies = [pltpu.make_async_copy(srcs[q], xs.at[q], sems.at[q]) for q in range(nodes)]
    for c in copies:
        c.start()
    lax.fori_loop(0, row_blocks, load_rows(counts_ref, adj_hbm, adj, rsems, True), 0)
    steps = list_pairs(counts_ref, pairs, adj.shape[0])
    acc[...] = jnp.zeros_like(acc)
    xs[nodes] = jnp.zeros_like(xs[nodes])
    for c in copies:
        c.wait()

    def work(r, both, places):
        x = []
        for where in places:
            q, at = split_place(where, rows, block)
            x.append(xs[q, :, at])
        x = jnp.concatenate(x, axis=1)
        return (lax.dot_general(x, both, (((1,), (1,)), ((), ())), preferred_element_type=F32),)

    def add(r, got):
        acc[r] += got

    over_pairs(place_ref, counts_ref, adj_hbm, adj, pairs, rsems, steps, work, add)
    for r in range(row_blocks):
        done = acc[r].astype(BF16)
        for p in (r // 2, (row_blocks + r) // 2):
            out_ref[p, :, r % 2 * block : (r % 2 + 1) * block] = done


def mid_kernel(at_ref, agg_ref, row_hbm, cross_ref, stay_ref, row, cots, sems):
    hid, width, span = agg_ref.shape
    half = stay_ref.shape[0]
    total = hid * width
    rows = row_hbm.shape[1] - row.shape[1]
    copies = [
        pltpu.make_async_copy(row_hbm.at[:, pl.ds(rows, row.shape[1])], row, sems.at[0]),
        pltpu.make_async_copy(
            row_hbm.at[:, pl.ds(pl.multiple_of(at_ref[0] * span, span), span)], cots, sems.at[1]
        ),
    ]
    for c in copies:
        c.start()
    agg = agg_ref[...].reshape(total, span)
    for c in copies:
        c.wait()
    cot = cots[...].astype(F32)
    wt = row[:, :total]
    bias = jnp.sum(row[:, total:].astype(F32), axis=1, keepdims=True)
    pre = jnp.dot(wt, agg, preferred_element_type=F32) + bias
    sig = jax.nn.sigmoid(pre)
    hidden = (pre * sig).astype(BF16)
    slope = (cot * sig * (1.0 + pre * (1.0 - sig))).astype(BF16)
    ws = lax.dot_general(wt, slope, (((0,), (0,)), ((), ())), preferred_element_type=F32)
    cross_ref[...] = ws.astype(BF16).reshape(hid, width, span)
    wg = lax.dot_general(slope, agg, (((1,), (1,)), ((), ())), preferred_element_type=F32)
    tail = split3(jnp.sum(slope.astype(F32), axis=1, keepdims=True))
    stay_ref[:, :, :span] = hidden.reshape(half, width, span)
    stay_ref[:, :, span : span + total] = wg.astype(BF16).reshape(half, width, total)
    stay_ref[:, :, span + total :] = tail.astype(BF16).reshape(half, width, 128)


def bwd_kernel(
    place_ref, counts_ref, adj_hbm, cross_ref,
    own_ref, d2p, d2m, r1, l1, r2, l2, acc, adj, ws, pairs, rsems,
):
    nodes, (width, rows) = acc.shape[0] - 1, acc.shape[1:]
    block = adj.shape[1]
    row_blocks = counts_ref.shape[0]
    lax.fori_loop(0, row_blocks, load_rows(counts_ref, adj_hbm, adj, rsems, True), 0)
    steps = list_pairs(counts_ref, pairs, adj.shape[0])
    acc[...] = jnp.zeros_like(acc)
    half = row_blocks // 2
    for p in range(half):
        both_halves = cross_ref[p].astype(F32) + cross_ref[half + p].astype(F32)
        ws[2 * p] = both_halves[:, :block].astype(BF16)
        ws[2 * p + 1] = both_halves[:, block:].astype(BF16)

    def work(r, both, places):
        made = jnp.dot(ws[r], both, preferred_element_type=F32)
        return made, places

    def add(r, made, places):
        for n, where in enumerate(places):
            q, at = split_place(where, rows, block)
            acc[q, :, at] += made[:, n * block : (n + 1) * block]

    over_pairs(place_ref, counts_ref, adj_hbm, adj, pairs, rsems, steps, work, add)

    def put(ref, n, q):
        ref[n] = acc[q].astype(BF16)

    for s in range(ZN):
        put(own_ref, s, s)
        right, left = (r2, l2) if s < 2 else (r1, l1)
        put(right, s % 2, ZN + s)
        put(left, s % 2, 3 * ZN + s)
    for n, s in enumerate((2, 0)):
        put(d2p, n, 2 * ZN + s)
        put(d2m, n, 2 * ZN + s + 1)


def fold_kernel(stay_ref, hidden_ref, out_ref):
    nodes, width, _ = out_ref.shape
    total = nodes * width
    half = stay_ref.shape[0]
    span = hidden_ref.shape[1] // half
    wg = jnp.zeros((width, total), F32)
    tail = jnp.zeros((width, 128), F32)
    for p in range(half):
        hidden_ref[:, p * span : (p + 1) * span] = stay_ref[p, :, :span]
        wg = wg + stay_ref[p, :, span : span + total].astype(F32)
        tail = tail + stay_ref[p, :, span + total :].astype(F32)
    tail = pltpu.roll(split3(jnp.sum(tail, axis=1, keepdims=True)), width, 1)
    lane = lax.broadcasted_iota(jnp.int32, (width, 128), 1)
    for a in range(nodes):
        tile = wg[:, (a * width) // 128 * 128 : (a * width) // 128 * 128 + 128]
        start = (a * width) % 128
        if start:
            tile = pltpu.roll(tile, 128 - start, 1)
        out_ref[a] = jnp.where(lane < width, tile, tail).astype(BF16)


def relay_kernel(r1, l1, r2, l2, from_left, from_right, r1_out, l1_out, r2_out, l2_out):
    for n, (right, left, right_out, left_out) in enumerate(
        ((r1, l1, r1_out, l1_out), (r2, l2, r2_out, l2_out))
    ):
        right_out[0] = (right[0].astype(F32) + from_left[n].astype(F32)).astype(BF16)
        right_out[1] = right[1]
        left_out[0] = left[0]
        left_out[1] = (left[1].astype(F32) + from_right[n].astype(F32)).astype(BF16)


def joined(own_ref, right, left, s):
    n = s % 2
    return own_ref[s].astype(F32) + right[n].astype(F32) + left[n].astype(F32)


def join_far_kernel(own_ref, right, left, s2, s3):
    s2[...] = joined(own_ref, right, left, 2)
    s3[...] = joined(own_ref, right, left, 3).astype(BF16)


def join_near_kernel(own_ref, right, left, s1):
    s1[...] = joined(own_ref, right, left, 1).astype(BF16)


def last_kernel(scale, own_ref, right, left, near, far, parts_ref, feat_ref, wg_ref, bias_ref):
    total = joined(own_ref, right, left, 0) + near[...].astype(F32) + far[...].astype(F32)
    feat_ref[...] = total.astype(BF16)
    width = feat_ref.shape[0]
    tail = parts_ref[0].astype(F32)
    for a in range(1, parts_ref.shape[0]):
        tail = tail + parts_ref[a].astype(F32)
    lane = lax.broadcasted_iota(jnp.int32, tail.shape, 1)
    bsum = jnp.sum(jnp.where(lane >= width, tail, 0.0), axis=1, keepdims=True)
    bias_ref[...] = jnp.broadcast_to(bsum * scale, (width, 128)).T[:1]
    wg_ref[...] = tail[:, :width].T * scale


def spec(space):
    return pl.BlockSpec(memory_space=space)


def cost(us):
    return pl.CostEstimate(flops=0, bytes_accessed=int(us * 3e6), transcendentals=0)


def params(mib):
    return pltpu.CompilerParams(vmem_limit_bytes=mib * MIB)


def per_device(feats, weight, bias, adjacency, columns, counts, cotangent):
    width, rows = feats.shape
    row_blocks, capacity, block, _ = adjacency.shape
    nodes, hid = lax.axis_size("node"), lax.axis_size("hid")
    total = weight.shape[0]
    scale = 1.0 / math.sqrt(nodes * rows)
    me, mine = lax.axis_index("node"), lax.axis_index("hid")
    blocks = adjacency.reshape(row_blocks * capacity, block, block)

    half = hid // 2
    span = rows // half
    halves = [list(range(half)), list(range(half, hid))]

    def exchange_half(v):
        return lax.all_to_all(v, "hid", 0, 0, axis_index_groups=halves, tiled=True)

    def exchange(v):
        return lax.all_to_all(v, "hid", 0, 0, tiled=True)

    with jax.named_scope("pack"):
        stay = jax.ShapeDtypeStruct((half, width, span + total + 128), BF16)
        row, place = pl.pallas_call(
            pack_kernel,
            out_shape=[
                jax.ShapeDtypeStruct((width, rows + total + 128), BF16),
                jax.ShapeDtypeStruct((row_blocks + 8, 128), jnp.int32),
            ],
            in_specs=[spec(pltpu.SMEM)] * 2 + [spec(VMEM)] * 4,
            out_specs=[spec(VMEM)] * 2,
            compiler_params=params(57),
        )(
            jnp.stack([me, nodes]).astype(jnp.int32),
            counts, columns, cotangent, weight.T, bias.reshape(1, width),
        )

        row = lax.all_gather(row, "hid", axis=0, axis_index_groups=halves, tiled=True)

    with jax.named_scope("node_gather"):
        z1, z2 = flip_z(feats, 1, nodes), flip_z(feats, 2, nodes)
        here = [feats, z1, z2, flip_z(z2, 1, nodes)]
        left = [shift_x(v, 1, nodes) for v in here]
        right = [shift_x(v, -1, nodes) for v in here]
        across = [shift_x(left[s], 1, nodes) for s in (0, 1)]
        across += [shift_x(right[s], -1, nodes) for s in (2, 3)]
    sources = here + right + across + left

    with jax.named_scope("aggregate"):
        agg = pl.pallas_call(
            fwd_kernel,
            out_shape=jax.ShapeDtypeStruct((hid, width, span), BF16),
            in_specs=[spec(pltpu.SMEM)] * 2 + [spec(pl.ANY)] * (1 + len(sources)),
            out_specs=spec(VMEM),
            scratch_shapes=[
                VMEM((nodes + 1, width, rows), BF16),
                VMEM(blocks.shape, BF16),
                VMEM((row_blocks, width, block), F32),
                pltpu.SMEM((row_blocks * capacity // 2 + UNROLL,), jnp.int32),
                pltpu.SemaphoreType.DMA((nodes,)),
                pltpu.SemaphoreType.DMA((row_blocks, capacity // QUARTER)),
            ],
            compiler_params=params(AGG),
            cost_estimate=cost(9),
        )(place, counts, blocks, *sources)
    agg = exchange(agg)

    with jax.named_scope("dense"):
        cross, kept = pl.pallas_call(
            mid_kernel,
            out_shape=[jax.ShapeDtypeStruct((hid, width, span), BF16), stay],
            in_specs=[spec(pltpu.SMEM), spec(VMEM), spec(pl.ANY)],
            out_specs=[spec(VMEM)] * 2,
            scratch_shapes=[
                VMEM((half * width, total + 128), BF16),
                VMEM((half * width, span), BF16),
                pltpu.SemaphoreType.DMA((2,)),
            ],
            compiler_params=params(57),
        )((mine % half)[None].astype(jnp.int32), agg, row)
    cross = exchange(cross)
    kept, cross = lax.optimization_barrier((kept, cross))
    kept = exchange_half(kept)

    one = jax.ShapeDtypeStruct((width, rows), BF16)
    two = jax.ShapeDtypeStruct((2, width, rows), BF16)
    with jax.named_scope("spread"):
        own, d2p, d2m, r1, l1, r2, l2 = pl.pallas_call(
            bwd_kernel,
            out_shape=[jax.ShapeDtypeStruct((ZN, width, rows), BF16)] + [two] * 6,
            in_specs=[spec(pltpu.SMEM)] * 2 + [spec(pl.ANY), spec(VMEM)],
            out_specs=[spec(VMEM)] * 7,
            scratch_shapes=[
                VMEM((nodes + 1, width, rows), F32),
                VMEM(blocks.shape, BF16),
                VMEM((row_blocks, width, block), BF16),
                pltpu.SMEM((row_blocks * capacity // 2 + UNROLL,), jnp.int32),
                pltpu.SemaphoreType.DMA((row_blocks, capacity // QUARTER)),
            ],
            compiler_params=params(SPR),
            cost_estimate=cost(9),
        )(place, counts, blocks, cross)

    def small(kernel, outs, *args):
        return pl.pallas_call(
            kernel,
            out_shape=outs,
            in_specs=[spec(VMEM)] * len(args),
            out_specs=[spec(VMEM)] * len(outs),
            compiler_params=params(8),
        )(*args)

    with jax.named_scope("node_sum"):
        from_left, from_right = shift_x(d2p, 1, nodes), shift_x(d2m, -1, nodes)
        r1, l1, r2, l2 = small(relay_kernel, [two] * 4, r1, l1, r2, l2, from_left, from_right)
        r1, l1 = shift_x(r1, 1, nodes), shift_x(l1, -1, nodes)
        r1, l1, r2, l2 = lax.optimization_barrier((r1, l1, r2, l2))
        r2, l2 = shift_x(r2, 1, nodes), shift_x(l2, -1, nodes)
        s2, s3 = small(join_far_kernel, [jax.ShapeDtypeStruct(one.shape, F32), one], own, r1, l1)
        s3 = flip_z(s3, 1, nodes)
        kept, _ = lax.optimization_barrier((kept, s3))
        hidden, parts = small(
            fold_kernel, [one, jax.ShapeDtypeStruct((nodes, width, 128), BF16)], kept
        )
        parts = lax.all_to_all(parts, "node", 0, 0, tiled=True)
        far = (s2 + s3.astype(F32)).astype(BF16)
        far = flip_z(far, 2, nodes)
        (s1,) = small(join_near_kernel, [one], own, r2, l2)
        near = flip_z(s1, 1, nodes)
        feat_grad, weight_grad, bias_grad = small(
            functools.partial(last_kernel, scale),
            [
                jax.ShapeDtypeStruct((width, rows), BF16),
                jax.ShapeDtypeStruct((width, width), F32),
                jax.ShapeDtypeStruct((1, width), F32),
            ],
            own, r2, l2, near, far, parts,
        )
    return hidden, feat_grad, weight_grad, bias_grad.reshape(width)


def solution(mesh):
    placed = (
        P("hid", "node"),
        P(None, "hid"),
        P("hid"),
        P("node", None, None, None),
        P("node", None),
        P("node"),
        P("hid", "node"),
    )
    return jax.shard_map(
        per_device,
        mesh=mesh,
        in_specs=placed,
        out_specs=(P("hid", "node"), P("hid", "node"), P("node", "hid"), P("hid")),
        check_vma=False,
    )
```

```python
import functools
import math

import jax
import jax.numpy as jnp
from jax import lax
from jax.experimental import pallas as pl
from jax.experimental.pallas import tpu as pltpu
from jax.sharding import PartitionSpec as P

F32 = jnp.float32
BF16 = jnp.bfloat16
ZN = 4
UNROLL = 8
QUARTER = 4
VMEM = pltpu.VMEM
MIB = 1024 * 1024
AGG, SPR = 56, 50


def shift_x(v, by, n):
    return lax.ppermute(v, "node", [(i, (i + ZN * by) % n) for i in range(n)])


def flip_z(v, by, n):
    return lax.ppermute(v, "node", [(i, i ^ by) for i in range(n)])


def split3(v):
    hi = v.astype(BF16).astype(F32)
    mid = (v - hi).astype(BF16).astype(F32)
    low = v - hi - mid
    lane = lax.broadcasted_iota(jnp.int32, (v.shape[0], 128), 1)
    return jnp.where(lane == 0, hi, jnp.where(lane == 1, mid, jnp.where(lane == 2, low, 0.0)))


def load_rows(counts_ref, adj_hbm, adj, sems, begin):
    row_blocks, pieces = sems.shape

    def one(r, q):
        at = pl.ds((r * pieces + q) * QUARTER, QUARTER)
        return pltpu.make_async_copy(adj_hbm.at[at], adj.at[at], sems.at[r, q])

    def row(r, carry):
        for q in range(pieces):

            @pl.when(counts_ref[r] > q * QUARTER)
            def _():
                one(r, q).start() if begin else one(r, q).wait()

        return carry

    return row


def list_pairs(counts_ref, pairs_ref, none):
    row_blocks = counts_ref.shape[0]
    capacity = none // row_blocks

    def row(r, n):
        def one(p, n):
            pairs_ref[n] = r * capacity + 2 * p
            return n + 1

        return lax.fori_loop(0, (counts_ref[r] + 1) >> 1, one, n)

    used = lax.fori_loop(0, row_blocks, row, 0)
    for i in range(UNROLL):
        pairs_ref[used + i] = none
    return (used + UNROLL - 1) // UNROLL


def over_pairs(place_ref, counts_ref, adj_hbm, adj, pairs, sems, steps, work, add):
    row_blocks = counts_ref.shape[0]
    none = adj.shape[0]
    shift = (none // row_blocks).bit_length() - 1

    def step(i, ready):
        slots = [pairs[i * UNROLL + u] for u in range(UNROLL)]
        inside = [slot & (none - 1) for slot in slots]
        rows = [at >> shift for at in inside]
        last = functools.reduce(jnp.maximum, rows)
        lax.fori_loop(ready, last + 1, load_rows(counts_ref, adj_hbm, adj, sems, False), 0)
        parts = []
        for slot, at, r in zip(slots, inside, rows):
            k = slot & (none // row_blocks - 1)
            both = jnp.concatenate([adj[at], adj[at + 1]], axis=1)
            parts.append((r, *work(r, both, (place_ref[slot >> shift, k], place_ref[slot >> shift, k + 1]))))
        for part in parts:
            add(*part)
        return jnp.maximum(ready, last + 1)

    lax.fori_loop(0, steps, step, 0)


def split_place(where, rows, block):
    return where >> (rows.bit_length() - 1), pl.ds(pl.multiple_of(where & (rows - 1), block), block)


def pack_kernel(me_ref, counts_ref, columns_ref, cot_ref, wt_ref, bias_ref, out_ref, place_ref):
    row_blocks, capacity = columns_ref.shape
    rows, block = cot_ref.shape[1], cot_ref.shape[1] // row_blocks
    x, z = me_ref[0] >> 2, me_ref[0] & (ZN - 1)
    column = columns_ref[...]
    index = lax.div(column, row_blocks)
    plane = (((index >> 2) - x) & (ZN - 1)) * ZN + ((index & (ZN - 1)) ^ z)
    place = plane * rows + lax.rem(column, row_blocks) * block
    slot = lax.broadcasted_iota(jnp.int32, (1, capacity), 1)
    place_ref[...] = jnp.full(place_ref.shape, me_ref[1] * rows, jnp.int32)
    for r in range(row_blocks):
        place_ref[r : r + 1, :capacity] = jnp.where(
            slot < counts_ref[r], place[r : r + 1], me_ref[1] * rows
        )
    parts = out_ref.shape[0]
    width, total = wt_ref.shape
    span = cot_ref.shape[1] // parts
    bias = jnp.broadcast_to(bias_ref[...], (width, width)).T[:, :1]
    tail = split3(bias).astype(BF16)
    for p in range(parts):
        out_ref[p, :, :span] = cot_ref[:, p * span : (p + 1) * span]
        out_ref[p, :, span : span + total] = wt_ref[...]
        out_ref[p, :, span + total :] = tail


def fwd_kernel(place_ref, counts_ref, adj_hbm, *refs):
    srcs, (out_ref, xs, adj, acc, pairs, sems, rsems) = refs[:-7], refs[-7:]
    row_blocks, _, block = acc.shape
    nodes, rows = xs.shape[0] - 1, xs.shape[2]
    copies, q = [], 0
    for n, ref in enumerate(srcs):
        blocks = ref.shape[0] if len(ref.shape) == 3 else 1
        to = xs.at[pl.ds(q, blocks)] if blocks > 1 else xs.at[q]
        copies.append(pltpu.make_async_copy(ref, to, sems.at[n]))
        q += blocks
    for c in copies:
        c.start()
    lax.fori_loop(0, row_blocks, load_rows(counts_ref, adj_hbm, adj, rsems, True), 0)
    steps = list_pairs(counts_ref, pairs, adj.shape[0])
    acc[...] = jnp.zeros_like(acc)
    xs[nodes] = jnp.zeros_like(xs[nodes])
    for c in copies:
        c.wait()

    def work(r, both, places):
        x = []
        for where in places:
            q, at = split_place(where, rows, block)
            x.append(xs[q, :, at])
        x = jnp.concatenate(x, axis=1)
        return (lax.dot_general(x, both, (((1,), (1,)), ((), ())), preferred_element_type=F32),)

    def add(r, got):
        acc[r] += got

    over_pairs(place_ref, counts_ref, adj_hbm, adj, pairs, rsems, steps, work, add)
    for r in range(row_blocks):
        done = acc[r].astype(BF16)
        for p in (r // 2, (row_blocks + r) // 2):
            out_ref[p, :, r % 2 * block : (r % 2 + 1) * block] = done


def mid_kernel(agg_ref, row_ref, cross_ref, stay_ref):
    hid, width, span = agg_ref.shape
    half = row_ref.shape[0]
    total = hid * width
    agg = agg_ref[...].reshape(total, span)
    row = row_ref[...].reshape(half * width, row_ref.shape[2])
    cot = row[:, :span].astype(F32)
    wt = row[:, span : span + total]
    bias = jnp.sum(row[:, span + total :].astype(F32), axis=1, keepdims=True)
    pre = jnp.dot(wt, agg, preferred_element_type=F32) + bias
    sig = jax.nn.sigmoid(pre)
    hidden = (pre * sig).astype(BF16)
    slope = (cot * sig * (1.0 + pre * (1.0 - sig))).astype(BF16)
    ws = lax.dot_general(wt, slope, (((0,), (0,)), ((), ())), preferred_element_type=F32)
    cross_ref[...] = ws.astype(BF16).reshape(hid, width, span)
    wg = lax.dot_general(slope, agg, (((1,), (1,)), ((), ())), preferred_element_type=F32)
    tail = split3(jnp.sum(slope.astype(F32), axis=1, keepdims=True))
    stay_ref[:, :, :span] = hidden.reshape(half, width, span)
    stay_ref[:, :, span : span + total] = wg.astype(BF16).reshape(half, width, total)
    stay_ref[:, :, span + total :] = tail.astype(BF16).reshape(half, width, 128)


def bwd_kernel(
    place_ref, counts_ref, adj_hbm, cross_ref,
    own_ref, d2p, d2m, r1, l1, r2, l2, acc, adj, ws, pairs, rsems,
):
    nodes, (width, rows) = acc.shape[0] - 1, acc.shape[1:]
    block = adj.shape[1]
    row_blocks = counts_ref.shape[0]
    lax.fori_loop(0, row_blocks, load_rows(counts_ref, adj_hbm, adj, rsems, True), 0)
    steps = list_pairs(counts_ref, pairs, adj.shape[0])
    acc[...] = jnp.zeros_like(acc)
    half = row_blocks // 2
    for p in range(half):
        both_halves = cross_ref[p].astype(F32) + cross_ref[half + p].astype(F32)
        ws[2 * p] = both_halves[:, :block].astype(BF16)
        ws[2 * p + 1] = both_halves[:, block:].astype(BF16)

    def work(r, both, places):
        made = jnp.dot(ws[r], both, preferred_element_type=F32)
        return made, places

    def add(r, made, places):
        for n, where in enumerate(places):
            q, at = split_place(where, rows, block)
            acc[q, :, at] += made[:, n * block : (n + 1) * block]

    over_pairs(place_ref, counts_ref, adj_hbm, adj, pairs, rsems, steps, work, add)

    def put(ref, n, q):
        ref[n] = acc[q].astype(BF16)

    for s in range(ZN):
        put(own_ref, s, s)
        right, left = (r2, l2) if s < 2 else (r1, l1)
        put(right, s % 2, ZN + s)
        put(left, s % 2, 3 * ZN + s)
    for n, s in enumerate((2, 0)):
        put(d2p, n, 2 * ZN + s)
        put(d2m, n, 2 * ZN + s + 1)


def fold_kernel(stay_ref, hidden_ref, out_ref):
    nodes, width, _ = out_ref.shape
    total = nodes * width
    half = stay_ref.shape[0]
    span = hidden_ref.shape[1] // half
    wg = jnp.zeros((width, total), F32)
    tail = jnp.zeros((width, 128), F32)
    for p in range(half):
        hidden_ref[:, p * span : (p + 1) * span] = stay_ref[p, :, :span]
        wg = wg + stay_ref[p, :, span : span + total].astype(F32)
        tail = tail + stay_ref[p, :, span + total :].astype(F32)
    tail = pltpu.roll(split3(jnp.sum(tail, axis=1, keepdims=True)), width, 1)
    lane = lax.broadcasted_iota(jnp.int32, (width, 128), 1)
    for a in range(nodes):
        tile = wg[:, (a * width) // 128 * 128 : (a * width) // 128 * 128 + 128]
        start = (a * width) % 128
        if start:
            tile = pltpu.roll(tile, 128 - start, 1)
        out_ref[a] = jnp.where(lane < width, tile, tail).astype(BF16)


def relay_kernel(r1, l1, r2, l2, from_left, from_right, r1_out, l1_out, r2_out, l2_out):
    for n, (right, left, right_out, left_out) in enumerate(
        ((r1, l1, r1_out, l1_out), (r2, l2, r2_out, l2_out))
    ):
        right_out[0] = (right[0].astype(F32) + from_left[n].astype(F32)).astype(BF16)
        right_out[1] = right[1]
        left_out[0] = left[0]
        left_out[1] = (left[1].astype(F32) + from_right[n].astype(F32)).astype(BF16)


def joined(own_ref, right, left, s):
    n = s % 2
    return own_ref[s].astype(F32) + right[n].astype(F32) + left[n].astype(F32)


def join_far_kernel(own_ref, right, left, s2, s3):
    s2[...] = joined(own_ref, right, left, 2)
    s3[...] = joined(own_ref, right, left, 3).astype(BF16)


def join_near_kernel(own_ref, right, left, s1):
    s1[...] = joined(own_ref, right, left, 1).astype(BF16)


def last_kernel(scale, own_ref, right, left, near, far, parts_ref, feat_ref, wg_ref, bias_ref):
    total = joined(own_ref, right, left, 0) + near[...].astype(F32) + far[...].astype(F32)
    feat_ref[...] = total.astype(BF16)
    width = feat_ref.shape[0]
    tail = parts_ref[0].astype(F32)
    for a in range(1, parts_ref.shape[0]):
        tail = tail + parts_ref[a].astype(F32)
    lane = lax.broadcasted_iota(jnp.int32, tail.shape, 1)
    bsum = jnp.sum(jnp.where(lane >= width, tail, 0.0), axis=1, keepdims=True)
    bias_ref[...] = jnp.broadcast_to(bsum * scale, (width, 128)).T[:1]
    wg_ref[...] = tail[:, :width].T * scale


def spec(space):
    return pl.BlockSpec(memory_space=space)


def cost(us):
    return pl.CostEstimate(flops=0, bytes_accessed=int(us * 3e6), transcendentals=0)


def params(mib):
    return pltpu.CompilerParams(vmem_limit_bytes=mib * MIB)


def per_device(feats, weight, bias, adjacency, columns, counts, cotangent):
    width, rows = feats.shape
    row_blocks, capacity, block, _ = adjacency.shape
    nodes, hid = lax.axis_size("node"), lax.axis_size("hid")
    total = weight.shape[0]
    scale = 1.0 / math.sqrt(nodes * rows)
    me = lax.axis_index("node")
    blocks = adjacency.reshape(row_blocks * capacity, block, block)

    half = hid // 2
    span = rows // half
    halves = [list(range(half)), list(range(half, hid))]

    def exchange_half(v):
        return lax.all_to_all(v, "hid", 0, 0, axis_index_groups=halves, tiled=True)

    def exchange(v):
        return lax.all_to_all(v, "hid", 0, 0, tiled=True)

    with jax.named_scope("pack"):
        stay = jax.ShapeDtypeStruct((half, width, span + total + 128), BF16)
        row, place = pl.pallas_call(
            pack_kernel,
            out_shape=[stay, jax.ShapeDtypeStruct((row_blocks + 8, 128), jnp.int32)],
            in_specs=[spec(pltpu.SMEM)] * 2 + [spec(VMEM)] * 4,
            out_specs=[spec(VMEM)] * 2,
            compiler_params=params(57),
        )(
            jnp.stack([me, nodes]).astype(jnp.int32),
            counts, columns, cotangent, weight.T, bias.reshape(1, width),
        )

    with jax.named_scope("node_gather"):
        z1, z2 = flip_z(feats, 1, nodes), flip_z(feats, 2, nodes)
        z3 = flip_z(z2, 1, nodes)
        left0, right0 = shift_x(feats, 1, nodes), shift_x(feats, -1, nodes)
        z1, left0, right0, row, place = lax.optimization_barrier((z1, left0, right0, row, place))
        here = [feats, jnp.stack([z1, z2]), z3]
        left = [left0] + [shift_x(v, 1, nodes) for v in here[1:]]
        right = [right0] + [shift_x(v, -1, nodes) for v in here[1:]]
        across = [
            shift_x(right[0], -1, nodes),
            shift_x(left[1][0], 1, nodes),
            shift_x(right[1][1], -1, nodes),
            shift_x(left[2], 1, nodes),
        ]
    sources = here + right + across + left

    row = exchange_half(lax.optimization_barrier((row, sources))[0])

    with jax.named_scope("aggregate"):
        agg = pl.pallas_call(
            fwd_kernel,
            out_shape=jax.ShapeDtypeStruct((hid, width, span), BF16),
            in_specs=[spec(pltpu.SMEM)] * 2 + [spec(pl.ANY)] * (1 + len(sources)),
            out_specs=spec(VMEM),
            scratch_shapes=[
                VMEM((nodes + 1, width, rows), BF16),
                VMEM(blocks.shape, BF16),
                VMEM((row_blocks, width, block), F32),
                pltpu.SMEM((row_blocks * capacity // 2 + UNROLL,), jnp.int32),
                pltpu.SemaphoreType.DMA((len(sources),)),
                pltpu.SemaphoreType.DMA((row_blocks, capacity // QUARTER)),
            ],
            compiler_params=params(AGG),
            cost_estimate=cost(9),
        )(place, counts, blocks, *sources)
    agg = exchange(agg)

    with jax.named_scope("dense"):
        cross, kept = pl.pallas_call(
            mid_kernel,
            out_shape=[jax.ShapeDtypeStruct((hid, width, span), BF16), stay],
            in_specs=[spec(VMEM)] * 2,
            out_specs=[spec(VMEM)] * 2,
            compiler_params=params(16),
        )(agg, row)
    cross = exchange(cross)
    kept, cross = lax.optimization_barrier((kept, cross))
    kept = exchange_half(kept)

    one = jax.ShapeDtypeStruct((width, rows), BF16)
    two = jax.ShapeDtypeStruct((2, width, rows), BF16)
    with jax.named_scope("spread"):
        own, d2p, d2m, r1, l1, r2, l2 = pl.pallas_call(
            bwd_kernel,
            out_shape=[jax.ShapeDtypeStruct((ZN, width, rows), BF16)] + [two] * 6,
            in_specs=[spec(pltpu.SMEM)] * 2 + [spec(pl.ANY), spec(VMEM)],
            out_specs=[spec(VMEM)] * 7,
            scratch_shapes=[
                VMEM((nodes + 1, width, rows), F32),
                VMEM(blocks.shape, BF16),
                VMEM((row_blocks, width, block), BF16),
                pltpu.SMEM((row_blocks * capacity // 2 + UNROLL,), jnp.int32),
                pltpu.SemaphoreType.DMA((row_blocks, capacity // QUARTER)),
            ],
            compiler_params=params(SPR),
            cost_estimate=cost(9),
        )(place, counts, blocks, cross)

    def small(kernel, outs, *args):
        return pl.pallas_call(
            kernel,
            out_shape=outs,
            in_specs=[spec(VMEM)] * len(args),
            out_specs=[spec(VMEM)] * len(outs),
            compiler_params=params(8),
        )(*args)

    with jax.named_scope("node_sum"):
        from_left, from_right = shift_x(d2p, 1, nodes), shift_x(d2m, -1, nodes)
        r1, l1, r2, l2 = small(relay_kernel, [two] * 4, r1, l1, r2, l2, from_left, from_right)
        r1, l1 = shift_x(r1, 1, nodes), shift_x(l1, -1, nodes)
        r1, l1, r2, l2 = lax.optimization_barrier((r1, l1, r2, l2))
        r2, l2 = shift_x(r2, 1, nodes), shift_x(l2, -1, nodes)
        s2, s3 = small(join_far_kernel, [jax.ShapeDtypeStruct(one.shape, F32), one], own, r1, l1)
        s3 = flip_z(s3, 1, nodes)
        kept, _ = lax.optimization_barrier((kept, s3))
        hidden, parts = small(
            fold_kernel, [one, jax.ShapeDtypeStruct((nodes, width, 128), BF16)], kept
        )
        parts = lax.all_to_all(parts, "node", 0, 0, tiled=True)
        far = (s2 + s3.astype(F32)).astype(BF16)
        far = flip_z(far, 2, nodes)
        (s1,) = small(join_near_kernel, [one], own, r2, l2)
        near = flip_z(s1, 1, nodes)
        feat_grad, weight_grad, bias_grad = small(
            functools.partial(last_kernel, scale),
            [
                jax.ShapeDtypeStruct((width, rows), BF16),
                jax.ShapeDtypeStruct((width, width), F32),
                jax.ShapeDtypeStruct((1, width), F32),
            ],
            own, r2, l2, near, far, parts,
        )
    return hidden, feat_grad, weight_grad, bias_grad.reshape(width)


def solution(mesh):
    placed = (
        P("hid", "node"),
        P(None, "hid"),
        P("hid"),
        P("node", None, None, None),
        P("node", None),
        P("node"),
        P("hid", "node"),
    )
    return jax.shard_map(
        per_device,
        mesh=mesh,
        in_specs=placed,
        out_specs=(P("hid", "node"), P("hid", "node"), P("node", "hid"), P("hid")),
        check_vma=False,
    )
```

```python
import functools
import math

import jax
import jax.numpy as jnp
from jax import lax
from jax.experimental import pallas as pl
from jax.experimental.pallas import tpu as pltpu
from jax.sharding import PartitionSpec as P

F32 = jnp.float32
BF16 = jnp.bfloat16
ZN = 4
UNROLL = 8
QUARTER = 4
VMEM = pltpu.VMEM
MIB = 1024 * 1024
AGG, SPR = 56, 50


def shift_x(v, by, n):
    return lax.ppermute(v, "node", [(i, (i + ZN * by) % n) for i in range(n)])


def flip_z(v, by, n):
    return lax.ppermute(v, "node", [(i, i ^ by) for i in range(n)])


def split3(v):
    hi = v.astype(BF16).astype(F32)
    mid = (v - hi).astype(BF16).astype(F32)
    low = v - hi - mid
    lane = lax.broadcasted_iota(jnp.int32, (v.shape[0], 128), 1)
    return jnp.where(lane == 0, hi, jnp.where(lane == 1, mid, jnp.where(lane == 2, low, 0.0)))


def load_rows(counts_ref, adj_hbm, adj, sems, begin):
    row_blocks, pieces = sems.shape

    def one(r, q):
        at = pl.ds((r * pieces + q) * QUARTER, QUARTER)
        return pltpu.make_async_copy(adj_hbm.at[at], adj.at[at], sems.at[r, q])

    def row(r, carry):
        for q in range(pieces):

            @pl.when(counts_ref[r] > q * QUARTER)
            def _():
                one(r, q).start() if begin else one(r, q).wait()

        return carry

    return row


def list_pairs(counts_ref, pairs_ref, none):
    row_blocks = counts_ref.shape[0]
    capacity = none // row_blocks

    def row(r, n):
        def one(p, n):
            pairs_ref[n] = r * capacity + 2 * p
            return n + 1

        return lax.fori_loop(0, (counts_ref[r] + 1) >> 1, one, n)

    used = lax.fori_loop(0, row_blocks, row, 0)
    for i in range(UNROLL):
        pairs_ref[used + i] = none
    return (used + UNROLL - 1) // UNROLL


def over_pairs(place_ref, counts_ref, adj_hbm, adj, pairs, sems, steps, work, add):
    row_blocks = counts_ref.shape[0]
    none = adj.shape[0]
    shift = (none // row_blocks).bit_length() - 1

    def step(i, ready):
        slots = [pairs[i * UNROLL + u] for u in range(UNROLL)]
        inside = [slot & (none - 1) for slot in slots]
        rows = [at >> shift for at in inside]
        last = functools.reduce(jnp.maximum, rows)
        lax.fori_loop(ready, last + 1, load_rows(counts_ref, adj_hbm, adj, sems, False), 0)
        parts = []
        for slot, at, r in zip(slots, inside, rows):
            k = slot & (none // row_blocks - 1)
            both = jnp.concatenate([adj[at], adj[at + 1]], axis=1)
            parts.append((r, *work(r, both, (place_ref[slot >> shift, k], place_ref[slot >> shift, k + 1]))))
        for part in parts:
            add(*part)
        return jnp.maximum(ready, last + 1)

    lax.fori_loop(0, steps, step, 0)


def split_place(where, rows, block):
    return where >> (rows.bit_length() - 1), pl.ds(pl.multiple_of(where & (rows - 1), block), block)


def pack_kernel(me_ref, counts_ref, columns_ref, cot_ref, wt_ref, bias_ref, out_ref, place_ref):
    row_blocks, capacity = columns_ref.shape
    rows, block = cot_ref.shape[1], cot_ref.shape[1] // row_blocks
    x, z = me_ref[0] >> 2, me_ref[0] & (ZN - 1)
    column = columns_ref[...]
    index = lax.div(column, row_blocks)
    plane = (((index >> 2) - x) & (ZN - 1)) * ZN + ((index & (ZN - 1)) ^ z)
    place = plane * rows + lax.rem(column, row_blocks) * block
    slot = lax.broadcasted_iota(jnp.int32, (1, capacity), 1)
    place_ref[...] = jnp.full(place_ref.shape, me_ref[1] * rows, jnp.int32)
    for r in range(row_blocks):
        place_ref[r : r + 1, :capacity] = jnp.where(
            slot < counts_ref[r], place[r : r + 1], me_ref[1] * rows
        )
    parts = out_ref.shape[0]
    width, total = wt_ref.shape
    span = cot_ref.shape[1] // parts
    bias = jnp.broadcast_to(bias_ref[...], (width, width)).T[:, :1]
    tail = split3(bias).astype(BF16)
    for p in range(parts):
        out_ref[p, :, :span] = cot_ref[:, p * span : (p + 1) * span]
        out_ref[p, :, span : span + total] = wt_ref[...]
        out_ref[p, :, span + total :] = tail


def fwd_kernel(place_ref, counts_ref, adj_hbm, *refs):
    srcs, (out_ref, xs, adj, acc, pairs, sems, rsems) = refs[:-7], refs[-7:]
    row_blocks, _, block = acc.shape
    nodes, rows = xs.shape[0] - 1, xs.shape[2]
    copies, q = [], 0
    for n, ref in enumerate(srcs):
        blocks = ref.shape[0] if len(ref.shape) == 3 else 1
        to = xs.at[pl.ds(q, blocks)] if blocks > 1 else xs.at[q]
        copies.append(pltpu.make_async_copy(ref, to, sems.at[n]))
        q += blocks
    for c in copies:
        c.start()
    lax.fori_loop(0, row_blocks, load_rows(counts_ref, adj_hbm, adj, rsems, True), 0)
    steps = list_pairs(counts_ref, pairs, adj.shape[0])
    acc[...] = jnp.zeros_like(acc)
    xs[nodes] = jnp.zeros_like(xs[nodes])
    for c in copies:
        c.wait()

    def work(r, both, places):
        x = []
        for where in places:
            q, at = split_place(where, rows, block)
            x.append(xs[q, :, at])
        x = jnp.concatenate(x, axis=1)
        return (lax.dot_general(x, both, (((1,), (1,)), ((), ())), preferred_element_type=F32),)

    def add(r, got):
        acc[r] += got

    over_pairs(place_ref, counts_ref, adj_hbm, adj, pairs, rsems, steps, work, add)
    for r in range(row_blocks):
        done = acc[r].astype(BF16)
        for p in (r // 2, (row_blocks + r) // 2):
            out_ref[p, :, r % 2 * block : (r % 2 + 1) * block] = done


def mid_kernel(agg_ref, row_ref, cross_ref, stay_ref):
    hid, width, span = agg_ref.shape
    half = row_ref.shape[0]
    total = hid * width
    agg = agg_ref[...].reshape(total, span)
    row = row_ref[...].reshape(half * width, row_ref.shape[2])
    cot = row[:, :span].astype(F32)
    wt = row[:, span : span + total]
    bias = jnp.sum(row[:, span + total :].astype(F32), axis=1, keepdims=True)
    pre = jnp.dot(wt, agg, preferred_element_type=F32) + bias
    sig = jax.nn.sigmoid(pre)
    hidden = (pre * sig).astype(BF16)
    slope = (cot * sig * (1.0 + pre * (1.0 - sig))).astype(BF16)
    ws = lax.dot_general(wt, slope, (((0,), (0,)), ((), ())), preferred_element_type=F32)
    cross_ref[...] = ws.astype(BF16).reshape(hid, width, span)
    wg = lax.dot_general(slope, agg, (((1,), (1,)), ((), ())), preferred_element_type=F32)
    tail = split3(jnp.sum(slope.astype(F32), axis=1, keepdims=True))
    stay_ref[:, :, :span] = hidden.reshape(half, width, span)
    stay_ref[:, :, span : span + total] = wg.astype(BF16).reshape(half, width, total)
    stay_ref[:, :, span + total :] = tail.astype(BF16).reshape(half, width, 128)


def bwd_kernel(
    place_ref, counts_ref, adj_hbm, cross_ref,
    own_ref, r1, c1, l1, r2, c2, l2, acc, adj, ws, pairs, rsems,
):
    nodes, (width, rows) = acc.shape[0] - 1, acc.shape[1:]
    block = adj.shape[1]
    row_blocks = counts_ref.shape[0]
    lax.fori_loop(0, row_blocks, load_rows(counts_ref, adj_hbm, adj, rsems, True), 0)
    steps = list_pairs(counts_ref, pairs, adj.shape[0])
    acc[...] = jnp.zeros_like(acc)
    half = row_blocks // 2
    for p in range(half):
        both_halves = cross_ref[p].astype(F32) + cross_ref[half + p].astype(F32)
        ws[2 * p] = both_halves[:, :block].astype(BF16)
        ws[2 * p + 1] = both_halves[:, block:].astype(BF16)

    def work(r, both, places):
        made = jnp.dot(ws[r], both, preferred_element_type=F32)
        return made, places

    def add(r, made, places):
        for n, where in enumerate(places):
            q, at = split_place(where, rows, block)
            acc[q, :, at] += made[:, n * block : (n + 1) * block]

    over_pairs(place_ref, counts_ref, adj_hbm, adj, pairs, rsems, steps, work, add)

    def put(ref, n, q):
        ref[n] = acc[q].astype(BF16)

    for s in range(ZN):
        put(own_ref, s, s)
        for dx, ref in enumerate((r2, c2, l2) if s < 2 else (r1, c1, l1), 1):
            put(ref, s % 2, dx * ZN + s)


def fold_kernel(stay_ref, hidden_ref, out_ref):
    nodes, width, _ = out_ref.shape
    total = nodes * width
    half = stay_ref.shape[0]
    span = hidden_ref.shape[1] // half
    wg = jnp.zeros((width, total), F32)
    tail = jnp.zeros((width, 128), F32)
    for p in range(half):
        hidden_ref[:, p * span : (p + 1) * span] = stay_ref[p, :, :span]
        wg = wg + stay_ref[p, :, span : span + total].astype(F32)
        tail = tail + stay_ref[p, :, span + total :].astype(F32)
    tail = pltpu.roll(split3(jnp.sum(tail, axis=1, keepdims=True)), width, 1)
    lane = lax.broadcasted_iota(jnp.int32, (width, 128), 1)
    for a in range(nodes):
        tile = wg[:, (a * width) // 128 * 128 : (a * width) // 128 * 128 + 128]
        start = (a * width) % 128
        if start:
            tile = pltpu.roll(tile, 128 - start, 1)
        out_ref[a] = jnp.where(lane < width, tile, tail).astype(BF16)


def joined(own_ref, parts, s):
    total = own_ref[s].astype(F32)
    for part in parts:
        total = total + part[s % 2].astype(F32)
    return total


def join_far_kernel(own_ref, a, b, c, s2, s3):
    s2[...] = joined(own_ref, (a, b, c), 2)
    s3[...] = joined(own_ref, (a, b, c), 3).astype(BF16)


def join_near_kernel(own_ref, a, b, c, s1):
    s1[...] = joined(own_ref, (a, b, c), 1).astype(BF16)


def last_kernel(scale, own_ref, a, b, c, near, far, parts_ref, feat_ref, wg_ref, bias_ref):
    total = joined(own_ref, (a, b, c), 0) + near[...].astype(F32) + far[...].astype(F32)
    feat_ref[...] = total.astype(BF16)
    width = feat_ref.shape[0]
    tail = parts_ref[0].astype(F32)
    for a in range(1, parts_ref.shape[0]):
        tail = tail + parts_ref[a].astype(F32)
    lane = lax.broadcasted_iota(jnp.int32, tail.shape, 1)
    bsum = jnp.sum(jnp.where(lane >= width, tail, 0.0), axis=1, keepdims=True)
    bias_ref[...] = jnp.broadcast_to(bsum * scale, (width, 128)).T[:1]
    wg_ref[...] = tail[:, :width].T * scale


def spec(space):
    return pl.BlockSpec(memory_space=space)


def cost(us):
    return pl.CostEstimate(flops=0, bytes_accessed=int(us * 3e6), transcendentals=0)


def params(mib):
    return pltpu.CompilerParams(vmem_limit_bytes=mib * MIB)


def per_device(feats, weight, bias, adjacency, columns, counts, cotangent):
    width, rows = feats.shape
    row_blocks, capacity, block, _ = adjacency.shape
    nodes, hid = lax.axis_size("node"), lax.axis_size("hid")
    total = weight.shape[0]
    scale = 1.0 / math.sqrt(nodes * rows)
    me = lax.axis_index("node")
    blocks = adjacency.reshape(row_blocks * capacity, block, block)

    half = hid // 2
    span = rows // half
    halves = [list(range(half)), list(range(half, hid))]

    def exchange_half(v):
        return lax.all_to_all(v, "hid", 0, 0, axis_index_groups=halves, tiled=True)

    def exchange(v):
        return lax.all_to_all(v, "hid", 0, 0, tiled=True)

    with jax.named_scope("pack"):
        stay = jax.ShapeDtypeStruct((half, width, span + total + 128), BF16)
        row, place = pl.pallas_call(
            pack_kernel,
            out_shape=[stay, jax.ShapeDtypeStruct((row_blocks + 8, 128), jnp.int32)],
            in_specs=[spec(pltpu.SMEM)] * 2 + [spec(VMEM)] * 4,
            out_specs=[spec(VMEM)] * 2,
            compiler_params=params(57),
        )(
            jnp.stack([me, nodes]).astype(jnp.int32),
            counts, columns, cotangent, weight.T, bias.reshape(1, width),
        )

    with jax.named_scope("node_gather"):
        z1, z2 = flip_z(feats, 1, nodes), flip_z(feats, 2, nodes)
        first = [shift_x(feats, by, nodes) for by in (1, 2, 3)]
        z1, z2, first, row, place = lax.optimization_barrier((z1, z2, first, row, place))
        z3 = flip_z(z2, 1, nodes)
        here = [feats, jnp.stack([z1, z2]), z3]
        left, across, right = [
            [first[by - 1]] + [shift_x(v, by, nodes) for v in here[1:]] for by in (1, 2, 3)
        ]
    sources = here + right + across + left

    row = exchange_half(lax.optimization_barrier((row, sources))[0])

    with jax.named_scope("aggregate"):
        agg = pl.pallas_call(
            fwd_kernel,
            out_shape=jax.ShapeDtypeStruct((hid, width, span), BF16),
            in_specs=[spec(pltpu.SMEM)] * 2 + [spec(pl.ANY)] * (1 + len(sources)),
            out_specs=spec(VMEM),
            scratch_shapes=[
                VMEM((nodes + 1, width, rows), BF16),
                VMEM(blocks.shape, BF16),
                VMEM((row_blocks, width, block), F32),
                pltpu.SMEM((row_blocks * capacity // 2 + UNROLL,), jnp.int32),
                pltpu.SemaphoreType.DMA((len(sources),)),
                pltpu.SemaphoreType.DMA((row_blocks, capacity // QUARTER)),
            ],
            compiler_params=params(AGG),
            cost_estimate=cost(9),
        )(place, counts, blocks, *sources)
    agg = exchange(agg)

    with jax.named_scope("dense"):
        cross, kept = pl.pallas_call(
            mid_kernel,
            out_shape=[jax.ShapeDtypeStruct((hid, width, span), BF16), stay],
            in_specs=[spec(VMEM)] * 2,
            out_specs=[spec(VMEM)] * 2,
            compiler_params=params(16),
        )(agg, row)
    cross = exchange(cross)
    kept, cross = lax.optimization_barrier((kept, cross))
    kept = exchange_half(kept)

    one = jax.ShapeDtypeStruct((width, rows), BF16)
    two = jax.ShapeDtypeStruct((2, width, rows), BF16)
    with jax.named_scope("spread"):
        own, *sums = pl.pallas_call(
            bwd_kernel,
            out_shape=[jax.ShapeDtypeStruct((ZN, width, rows), BF16)] + [two] * 6,
            in_specs=[spec(pltpu.SMEM)] * 2 + [spec(pl.ANY), spec(VMEM)],
            out_specs=[spec(VMEM)] * 7,
            scratch_shapes=[
                VMEM((nodes + 1, width, rows), F32),
                VMEM(blocks.shape, BF16),
                VMEM((row_blocks, width, block), BF16),
                pltpu.SMEM((row_blocks * capacity // 2 + UNROLL,), jnp.int32),
                pltpu.SemaphoreType.DMA((row_blocks, capacity // QUARTER)),
            ],
            compiler_params=params(SPR),
            cost_estimate=cost(9),
        )(place, counts, blocks, cross)

    def small(kernel, outs, *args):
        return pl.pallas_call(
            kernel,
            out_shape=outs,
            in_specs=[spec(VMEM)] * len(args),
            out_specs=[spec(VMEM)] * len(outs),
            compiler_params=params(8),
        )(*args)

    with jax.named_scope("node_sum"):
        set1 = [shift_x(v, by, nodes) for by, v in enumerate(sums[:3], 1)]
        set1, set2 = lax.optimization_barrier((set1, sums[3:]))
        set2 = [shift_x(v, by, nodes) for by, v in enumerate(set2, 1)]
        s2, s3 = small(join_far_kernel, [jax.ShapeDtypeStruct(one.shape, F32), one], own, *set1)
        s3 = flip_z(s3, 1, nodes)
        kept, _ = lax.optimization_barrier((kept, s3))
        hidden, parts = small(
            fold_kernel, [one, jax.ShapeDtypeStruct((nodes, width, 128), BF16)], kept
        )
        parts = lax.all_to_all(parts, "node", 0, 0, tiled=True)
        far = (s2 + s3.astype(F32)).astype(BF16)
        far = flip_z(far, 2, nodes)
        (s1,) = small(join_near_kernel, [one], own, *set2)
        near = flip_z(s1, 1, nodes)
        feat_grad, weight_grad, bias_grad = small(
            functools.partial(last_kernel, scale),
            [
                jax.ShapeDtypeStruct((width, rows), BF16),
                jax.ShapeDtypeStruct((width, width), F32),
                jax.ShapeDtypeStruct((1, width), F32),
            ],
            own, *set2, near, far, parts,
        )
    return hidden, feat_grad, weight_grad, bias_grad.reshape(width)


def solution(mesh):
    placed = (
        P("hid", "node"),
        P(None, "hid"),
        P("hid"),
        P("node", None, None, None),
        P("node", None),
        P("node"),
        P("hid", "node"),
    )
    return jax.shard_map(
        per_device,
        mesh=mesh,
        in_specs=placed,
        out_specs=(P("hid", "node"), P("hid", "node"), P("node", "hid"), P("hid")),
        check_vma=False,
    )
```

```python
import functools
import math

import jax
import jax.numpy as jnp
from jax import lax
from jax.experimental import pallas as pl
from jax.experimental.pallas import tpu as pltpu
from jax.sharding import PartitionSpec as P

F32 = jnp.float32
BF16 = jnp.bfloat16
ZN = 4
UNROLL = 8
QUARTER = 4
VMEM = pltpu.VMEM
MIB = 1024 * 1024
AGG, SPR = 56, 50


def shift_x(v, by, n):
    return lax.ppermute(v, "node", [(i, (i + ZN * by) % n) for i in range(n)])


def flip_z(v, by, n):
    return lax.ppermute(v, "node", [(i, i ^ by) for i in range(n)])


def split3(v):
    hi = v.astype(BF16).astype(F32)
    mid = (v - hi).astype(BF16).astype(F32)
    low = v - hi - mid
    lane = lax.broadcasted_iota(jnp.int32, (v.shape[0], 128), 1)
    return jnp.where(lane == 0, hi, jnp.where(lane == 1, mid, jnp.where(lane == 2, low, 0.0)))


def load_rows(counts_ref, adj_hbm, adj, sems, begin):
    row_blocks, pieces = sems.shape

    def one(r, q):
        at = pl.ds((r * pieces + q) * QUARTER, QUARTER)
        return pltpu.make_async_copy(adj_hbm.at[at], adj.at[at], sems.at[r, q])

    def row(r, carry):
        for q in range(pieces):

            @pl.when(counts_ref[r] > q * QUARTER)
            def _():
                one(r, q).start() if begin else one(r, q).wait()

        return carry

    return row


def list_pairs(counts_ref, pairs_ref, none):
    row_blocks = counts_ref.shape[0]
    capacity = none // row_blocks

    def row(r, n):
        def one(p, n):
            pairs_ref[n] = r * capacity + 2 * p
            return n + 1

        return lax.fori_loop(0, (counts_ref[r] + 1) >> 1, one, n)

    used = lax.fori_loop(0, row_blocks, row, 0)
    for i in range(UNROLL):
        pairs_ref[used + i] = none
    return (used + UNROLL - 1) // UNROLL


def over_pairs(place_ref, counts_ref, adj_hbm, adj, pairs, sems, steps, work, add):
    row_blocks = counts_ref.shape[0]
    none = adj.shape[0]
    shift = (none // row_blocks).bit_length() - 1

    def step(i, ready):
        slots = [pairs[i * UNROLL + u] for u in range(UNROLL)]
        inside = [slot & (none - 1) for slot in slots]
        rows = [at >> shift for at in inside]
        last = functools.reduce(jnp.maximum, rows)
        lax.fori_loop(ready, last + 1, load_rows(counts_ref, adj_hbm, adj, sems, False), 0)
        parts = []
        for slot, at, r in zip(slots, inside, rows):
            k = slot & (none // row_blocks - 1)
            both = jnp.concatenate([adj[at], adj[at + 1]], axis=1)
            parts.append((r, *work(r, both, (place_ref[slot >> shift, k], place_ref[slot >> shift, k + 1]))))
        for part in parts:
            add(*part)
        return jnp.maximum(ready, last + 1)

    lax.fori_loop(0, steps, step, 0)


def split_place(where, rows, block):
    return where >> (rows.bit_length() - 1), pl.ds(pl.multiple_of(where & (rows - 1), block), block)


def pack_kernel(me_ref, counts_ref, columns_ref, cot_ref, wt_ref, bias_ref, out_ref, place_ref):
    row_blocks, capacity = columns_ref.shape
    rows, block = cot_ref.shape[1], cot_ref.shape[1] // row_blocks
    x, z = me_ref[0] >> 2, me_ref[0] & (ZN - 1)
    column = columns_ref[...]
    index = lax.div(column, row_blocks)
    plane = (((index >> 2) - x) & (ZN - 1)) * ZN + ((index & (ZN - 1)) ^ z)
    place = plane * rows + lax.rem(column, row_blocks) * block
    slot = lax.broadcasted_iota(jnp.int32, (1, capacity), 1)
    place_ref[...] = jnp.full(place_ref.shape, me_ref[1] * rows, jnp.int32)
    for r in range(row_blocks):
        place_ref[r : r + 1, :capacity] = jnp.where(
            slot < counts_ref[r], place[r : r + 1], me_ref[1] * rows
        )
    parts = out_ref.shape[0]
    width, total = wt_ref.shape
    span = cot_ref.shape[1] // parts
    bias = jnp.broadcast_to(bias_ref[...], (width, width)).T[:, :1]
    tail = split3(bias).astype(BF16)
    for p in range(parts):
        out_ref[p, :, :span] = cot_ref[:, p * span : (p + 1) * span]
        out_ref[p, :, span : span + total] = wt_ref[...]
        out_ref[p, :, span + total :] = tail


def fwd_kernel(place_ref, counts_ref, adj_hbm, *refs):
    srcs, (out_ref, xs, adj, acc, pairs, sems, rsems) = refs[:-7], refs[-7:]
    row_blocks, _, block = acc.shape
    nodes, rows = xs.shape[0] - 1, xs.shape[2]
    copies, q = [], 0
    for n, ref in enumerate(srcs):
        blocks = ref.shape[0] if len(ref.shape) == 3 else 1
        to = xs.at[pl.ds(q, blocks)] if blocks > 1 else xs.at[q]
        copies.append(pltpu.make_async_copy(ref, to, sems.at[n]))
        q += blocks
    for c in copies:
        c.start()
    lax.fori_loop(0, row_blocks, load_rows(counts_ref, adj_hbm, adj, rsems, True), 0)
    steps = list_pairs(counts_ref, pairs, adj.shape[0])
    acc[...] = jnp.zeros_like(acc)
    xs[nodes] = jnp.zeros_like(xs[nodes])
    for c in copies:
        c.wait()

    def work(r, both, places):
        x = []
        for where in places:
            q, at = split_place(where, rows, block)
            x.append(xs[q, :, at])
        x = jnp.concatenate(x, axis=1)
        return (lax.dot_general(x, both, (((1,), (1,)), ((), ())), preferred_element_type=F32),)

    def add(r, got):
        acc[r] += got

    over_pairs(place_ref, counts_ref, adj_hbm, adj, pairs, rsems, steps, work, add)
    for r in range(row_blocks):
        done = acc[r].astype(BF16)
        for p in (r // 2, (row_blocks + r) // 2):
            out_ref[p, :, r % 2 * block : (r % 2 + 1) * block] = done


def mid_kernel(agg_ref, row_ref, cross_ref, stay_ref):
    hid, width, span = agg_ref.shape
    half = row_ref.shape[0]
    total = hid * width
    agg = agg_ref[...].reshape(total, span)
    row = row_ref[...].reshape(half * width, row_ref.shape[2])
    cot = row[:, :span].astype(F32)
    wt = row[:, span : span + total]
    bias = jnp.sum(row[:, span + total :].astype(F32), axis=1, keepdims=True)
    pre = jnp.dot(wt, agg, preferred_element_type=F32) + bias
    sig = jax.nn.sigmoid(pre)
    hidden = (pre * sig).astype(BF16)
    slope = (cot * sig * (1.0 + pre * (1.0 - sig))).astype(BF16)
    ws = lax.dot_general(wt, slope, (((0,), (0,)), ((), ())), preferred_element_type=F32)
    cross_ref[...] = ws.astype(BF16).reshape(hid, width, span)
    wg = lax.dot_general(slope, agg, (((1,), (1,)), ((), ())), preferred_element_type=F32)
    tail = split3(jnp.sum(slope.astype(F32), axis=1, keepdims=True))
    stay_ref[:, :, :span] = hidden.reshape(half, width, span)
    stay_ref[:, :, span : span + total] = wg.astype(BF16).reshape(half, width, total)
    stay_ref[:, :, span + total :] = tail.astype(BF16).reshape(half, width, 128)


def bwd_kernel(
    place_ref, counts_ref, adj_hbm, cross_ref,
    own_ref, d2p, d2m, r1, l1, r2, l2, acc, adj, ws, pairs, rsems,
):
    nodes, (width, rows) = acc.shape[0] - 1, acc.shape[1:]
    block = adj.shape[1]
    row_blocks = counts_ref.shape[0]
    lax.fori_loop(0, row_blocks, load_rows(counts_ref, adj_hbm, adj, rsems, True), 0)
    steps = list_pairs(counts_ref, pairs, adj.shape[0])
    acc[...] = jnp.zeros_like(acc)
    half = row_blocks // 2
    for p in range(half):
        both_halves = cross_ref[p].astype(F32) + cross_ref[half + p].astype(F32)
        ws[2 * p] = both_halves[:, :block].astype(BF16)
        ws[2 * p + 1] = both_halves[:, block:].astype(BF16)

    def work(r, both, places):
        made = jnp.dot(ws[r], both, preferred_element_type=F32)
        return made, places

    def add(r, made, places):
        for n, where in enumerate(places):
            q, at = split_place(where, rows, block)
            acc[q, :, at] += made[:, n * block : (n + 1) * block]

    over_pairs(place_ref, counts_ref, adj_hbm, adj, pairs, rsems, steps, work, add)

    def put(ref, n, q):
        ref[n] = acc[q].astype(BF16)

    for s in range(ZN):
        put(own_ref, s, s)
        right, left = (r2, l2) if s < 2 else (r1, l1)
        put(right, s % 2, ZN + s)
        put(left, s % 2, 3 * ZN + s)
    for n, s in enumerate((2, 0)):
        put(d2p, n, 2 * ZN + s)
        put(d2m, n, 2 * ZN + s + 1)


def fold_kernel(stay_ref, hidden_ref, out_ref):
    nodes, width, _ = out_ref.shape
    total = nodes * width
    half = stay_ref.shape[0]
    span = hidden_ref.shape[1] // half
    wg = jnp.zeros((width, total), F32)
    tail = jnp.zeros((width, 128), F32)
    for p in range(half):
        hidden_ref[:, p * span : (p + 1) * span] = stay_ref[p, :, :span]
        wg = wg + stay_ref[p, :, span : span + total].astype(F32)
        tail = tail + stay_ref[p, :, span + total :].astype(F32)
    tail = pltpu.roll(split3(jnp.sum(tail, axis=1, keepdims=True)), width, 1)
    lane = lax.broadcasted_iota(jnp.int32, (width, 128), 1)
    for a in range(nodes):
        tile = wg[:, (a * width) // 128 * 128 : (a * width) // 128 * 128 + 128]
        start = (a * width) % 128
        if start:
            tile = pltpu.roll(tile, 128 - start, 1)
        out_ref[a] = jnp.where(lane < width, tile, tail).astype(BF16)


def relay_kernel(r1, l1, r2, l2, from_left, from_right, r1_out, l1_out, r2_out, l2_out):
    for n, (right, left, right_out, left_out) in enumerate(
        ((r1, l1, r1_out, l1_out), (r2, l2, r2_out, l2_out))
    ):
        right_out[0] = (right[0].astype(F32) + from_left[n].astype(F32)).astype(BF16)
        right_out[1] = right[1]
        left_out[0] = left[0]
        left_out[1] = (left[1].astype(F32) + from_right[n].astype(F32)).astype(BF16)


def joined(own_ref, right, left, s):
    n = s % 2
    return own_ref[s].astype(F32) + right[n].astype(F32) + left[n].astype(F32)


def join_far_kernel(own_ref, right, left, s2, s3):
    s2[...] = joined(own_ref, right, left, 2)
    s3[...] = joined(own_ref, right, left, 3).astype(BF16)


def join_near_kernel(own_ref, right, left, s1):
    s1[...] = joined(own_ref, right, left, 1).astype(BF16)


def last_kernel(scale, own_ref, right, left, near, far, parts_ref, feat_ref, wg_ref, bias_ref):
    total = joined(own_ref, right, left, 0) + near[...].astype(F32) + far[...].astype(F32)
    feat_ref[...] = total.astype(BF16)
    width = feat_ref.shape[0]
    tail = parts_ref[0].astype(F32)
    for a in range(1, parts_ref.shape[0]):
        tail = tail + parts_ref[a].astype(F32)
    lane = lax.broadcasted_iota(jnp.int32, tail.shape, 1)
    bsum = jnp.sum(jnp.where(lane >= width, tail, 0.0), axis=1, keepdims=True)
    bias_ref[...] = jnp.broadcast_to(bsum * scale, (width, 128)).T[:1]
    wg_ref[...] = tail[:, :width].T * scale


def spec(space):
    return pl.BlockSpec(memory_space=space)


def cost(us):
    return pl.CostEstimate(flops=0, bytes_accessed=int(us * 3e6), transcendentals=0)


def params(mib):
    return pltpu.CompilerParams(vmem_limit_bytes=mib * MIB)


def per_device(feats, weight, bias, adjacency, columns, counts, cotangent):
    width, rows = feats.shape
    row_blocks, capacity, block, _ = adjacency.shape
    nodes, hid = lax.axis_size("node"), lax.axis_size("hid")
    total = weight.shape[0]
    scale = 1.0 / math.sqrt(nodes * rows)
    me = lax.axis_index("node")
    blocks = adjacency.reshape(row_blocks * capacity, block, block)

    half = hid // 2
    span = rows // half
    halves = [list(range(half)), list(range(half, hid))]

    def exchange_half(v):
        return lax.all_to_all(v, "hid", 0, 0, axis_index_groups=halves, tiled=True)

    def exchange(v):
        return lax.all_to_all(v, "hid", 0, 0, tiled=True)

    with jax.named_scope("pack"):
        stay = jax.ShapeDtypeStruct((half, width, span + total + 128), BF16)
        row, place = pl.pallas_call(
            pack_kernel,
            out_shape=[stay, jax.ShapeDtypeStruct((row_blocks + 8, 128), jnp.int32)],
            in_specs=[spec(pltpu.SMEM)] * 2 + [spec(VMEM)] * 4,
            out_specs=[spec(VMEM)] * 2,
            compiler_params=params(57),
        )(
            jnp.stack([me, nodes]).astype(jnp.int32),
            counts, columns, cotangent, weight.T, bias.reshape(1, width),
        )

    with jax.named_scope("node_gather"):
        z1, z2 = flip_z(feats, 1, nodes), flip_z(feats, 2, nodes)
        z3 = flip_z(z2, 1, nodes)
        left0, right0 = shift_x(feats, 1, nodes), shift_x(feats, -1, nodes)
        z1, left0, right0, place = lax.optimization_barrier((z1, left0, right0, place))
        row = exchange_half(row)
        here = [feats, jnp.stack([z1, z2]), z3]
        left = [left0] + [shift_x(v, 1, nodes) for v in here[1:]]
        right = [right0] + [shift_x(v, -1, nodes) for v in here[1:]]
        row, left[1], right[1] = lax.optimization_barrier((row, left[1], right[1]))
        across = [
            shift_x(right[0], -1, nodes),
            shift_x(left[1][0], 1, nodes),
            shift_x(right[1][1], -1, nodes),
            shift_x(left[2], 1, nodes),
        ]
    sources = here + right + across + left


    with jax.named_scope("aggregate"):
        agg = pl.pallas_call(
            fwd_kernel,
            out_shape=jax.ShapeDtypeStruct((hid, width, span), BF16),
            in_specs=[spec(pltpu.SMEM)] * 2 + [spec(pl.ANY)] * (1 + len(sources)),
            out_specs=spec(VMEM),
            scratch_shapes=[
                VMEM((nodes + 1, width, rows), BF16),
                VMEM(blocks.shape, BF16),
                VMEM((row_blocks, width, block), F32),
                pltpu.SMEM((row_blocks * capacity // 2 + UNROLL,), jnp.int32),
                pltpu.SemaphoreType.DMA((len(sources),)),
                pltpu.SemaphoreType.DMA((row_blocks, capacity // QUARTER)),
            ],
            compiler_params=params(AGG),
            cost_estimate=cost(9),
        )(place, counts, blocks, *sources)
    agg = exchange(agg)

    with jax.named_scope("dense"):
        cross, kept = pl.pallas_call(
            mid_kernel,
            out_shape=[jax.ShapeDtypeStruct((hid, width, span), BF16), stay],
            in_specs=[spec(VMEM)] * 2,
            out_specs=[spec(VMEM)] * 2,
            compiler_params=params(16),
        )(agg, row)
    cross = exchange(cross)
    kept, cross = lax.optimization_barrier((kept, cross))
    kept = exchange_half(kept)

    one = jax.ShapeDtypeStruct((width, rows), BF16)
    two = jax.ShapeDtypeStruct((2, width, rows), BF16)
    with jax.named_scope("spread"):
        own, d2p, d2m, r1, l1, r2, l2 = pl.pallas_call(
            bwd_kernel,
            out_shape=[jax.ShapeDtypeStruct((ZN, width, rows), BF16)] + [two] * 6,
            in_specs=[spec(pltpu.SMEM)] * 2 + [spec(pl.ANY), spec(VMEM)],
            out_specs=[spec(VMEM)] * 7,
            scratch_shapes=[
                VMEM((nodes + 1, width, rows), F32),
                VMEM(blocks.shape, BF16),
                VMEM((row_blocks, width, block), BF16),
                pltpu.SMEM((row_blocks * capacity // 2 + UNROLL,), jnp.int32),
                pltpu.SemaphoreType.DMA((row_blocks, capacity // QUARTER)),
            ],
            compiler_params=params(SPR),
            cost_estimate=cost(9),
        )(place, counts, blocks, cross)

    def small(kernel, outs, *args):
        return pl.pallas_call(
            kernel,
            out_shape=outs,
            in_specs=[spec(VMEM)] * len(args),
            out_specs=[spec(VMEM)] * len(outs),
            compiler_params=params(8),
        )(*args)

    with jax.named_scope("node_sum"):
        from_left, from_right = shift_x(d2p, 1, nodes), shift_x(d2m, -1, nodes)
        r1, l1, r2, l2 = small(relay_kernel, [two] * 4, r1, l1, r2, l2, from_left, from_right)
        r1, l1 = shift_x(r1, 1, nodes), shift_x(l1, -1, nodes)
        r1, l1, r2, l2 = lax.optimization_barrier((r1, l1, r2, l2))
        r2, l2 = shift_x(r2, 1, nodes), shift_x(l2, -1, nodes)
        s2, s3 = small(join_far_kernel, [jax.ShapeDtypeStruct(one.shape, F32), one], own, r1, l1)
        s3 = flip_z(s3, 1, nodes)
        kept, _ = lax.optimization_barrier((kept, s3))
        hidden, parts = small(
            fold_kernel, [one, jax.ShapeDtypeStruct((nodes, width, 128), BF16)], kept
        )
        parts = lax.all_to_all(parts, "node", 0, 0, tiled=True)
        far = (s2 + s3.astype(F32)).astype(BF16)
        far = flip_z(far, 2, nodes)
        (s1,) = small(join_near_kernel, [one], own, r2, l2)
        near = flip_z(s1, 1, nodes)
        feat_grad, weight_grad, bias_grad = small(
            functools.partial(last_kernel, scale),
            [
                jax.ShapeDtypeStruct((width, rows), BF16),
                jax.ShapeDtypeStruct((width, width), F32),
                jax.ShapeDtypeStruct((1, width), F32),
            ],
            own, r2, l2, near, far, parts,
        )
    return hidden, feat_grad, weight_grad, bias_grad.reshape(width)


def solution(mesh):
    placed = (
        P("hid", "node"),
        P(None, "hid"),
        P("hid"),
        P("node", None, None, None),
        P("node", None),
        P("node"),
        P("hid", "node"),
    )
    return jax.shard_map(
        per_device,
        mesh=mesh,
        in_specs=placed,
        out_specs=(P("hid", "node"), P("hid", "node"), P("node", "hid"), P("hid")),
        check_vma=False,
    )
```

```python
import functools
import math

import jax
import jax.numpy as jnp
from jax import lax
from jax.experimental import pallas as pl
from jax.experimental.pallas import tpu as pltpu
from jax.sharding import PartitionSpec as P

F32 = jnp.float32
BF16 = jnp.bfloat16
ZN = 4
UNROLL = 8
QUARTER = 4
VMEM = pltpu.VMEM
MIB = 1024 * 1024
AGG, SPR = 56, 50


def shift_x(v, by, n):
    return lax.ppermute(v, "node", [(i, (i + ZN * by) % n) for i in range(n)])


def flip_z(v, by, n):
    return lax.ppermute(v, "node", [(i, i ^ by) for i in range(n)])


def split3(v):
    hi = v.astype(BF16).astype(F32)
    mid = (v - hi).astype(BF16).astype(F32)
    low = v - hi - mid
    lane = lax.broadcasted_iota(jnp.int32, (v.shape[0], 128), 1)
    return jnp.where(lane == 0, hi, jnp.where(lane == 1, mid, jnp.where(lane == 2, low, 0.0)))


def load_rows(counts_ref, adj_hbm, adj, sems, begin):
    row_blocks, pieces = sems.shape

    def one(r, q):
        at = pl.ds((r * pieces + q) * QUARTER, QUARTER)
        return pltpu.make_async_copy(adj_hbm.at[at], adj.at[at], sems.at[r, q])

    def row(r, carry):
        for q in range(pieces):

            @pl.when(counts_ref[r] > q * QUARTER)
            def _():
                one(r, q).start() if begin else one(r, q).wait()

        return carry

    return row


def list_pairs(counts_ref, pairs_ref, none):
    row_blocks = counts_ref.shape[0]
    capacity = none // row_blocks

    def row(r, n):
        def one(p, n):
            pairs_ref[n] = r * capacity + 2 * p
            return n + 1

        return lax.fori_loop(0, (counts_ref[r] + 1) >> 1, one, n)

    used = lax.fori_loop(0, row_blocks, row, 0)
    for i in range(UNROLL):
        pairs_ref[used + i] = none
    return (used + UNROLL - 1) // UNROLL


def over_pairs(place_ref, counts_ref, adj_hbm, adj, pairs, sems, steps, work, add):
    row_blocks = counts_ref.shape[0]
    none = adj.shape[0]
    shift = (none // row_blocks).bit_length() - 1

    def step(i, ready):
        slots = [pairs[i * UNROLL + u] for u in range(UNROLL)]
        inside = [slot & (none - 1) for slot in slots]
        rows = [at >> shift for at in inside]
        last = functools.reduce(jnp.maximum, rows)
        lax.fori_loop(ready, last + 1, load_rows(counts_ref, adj_hbm, adj, sems, False), 0)
        parts = []
        for slot, at, r in zip(slots, inside, rows):
            k = slot & (none // row_blocks - 1)
            both = jnp.concatenate([adj[at], adj[at + 1]], axis=1)
            parts.append((r, *work(r, both, (place_ref[slot >> shift, k], place_ref[slot >> shift, k + 1]))))
        for part in parts:
            add(*part)
        return jnp.maximum(ready, last + 1)

    lax.fori_loop(0, steps, step, 0)


def split_place(where, rows, block):
    return where >> (rows.bit_length() - 1), pl.ds(pl.multiple_of(where & (rows - 1), block), block)


def pack_kernel(me_ref, counts_ref, columns_ref, cot_ref, wt_ref, bias_ref, out_ref, place_ref):
    row_blocks, capacity = columns_ref.shape
    rows, block = cot_ref.shape[1], cot_ref.shape[1] // row_blocks
    x, z = me_ref[0] >> 2, me_ref[0] & (ZN - 1)
    column = columns_ref[...]
    index = lax.div(column, row_blocks)
    plane = (((index >> 2) - x) & (ZN - 1)) * ZN + ((index & (ZN - 1)) ^ z)
    place = plane * rows + lax.rem(column, row_blocks) * block
    slot = lax.broadcasted_iota(jnp.int32, (1, capacity), 1)
    place_ref[...] = jnp.full(place_ref.shape, me_ref[1] * rows, jnp.int32)
    for r in range(row_blocks):
        place_ref[r : r + 1, :capacity] = jnp.where(
            slot < counts_ref[r], place[r : r + 1], me_ref[1] * rows
        )
    parts = out_ref.shape[0]
    width, total = wt_ref.shape
    span = cot_ref.shape[1] // parts
    bias = jnp.broadcast_to(bias_ref[...], (width, width)).T[:, :1]
    tail = split3(bias).astype(BF16)
    for p in range(parts):
        out_ref[p, :, :span] = cot_ref[:, p * span : (p + 1) * span]
        out_ref[p, :, span : span + total] = wt_ref[...]
        out_ref[p, :, span + total :] = tail


def fwd_kernel(place_ref, counts_ref, adj_hbm, *refs):
    srcs, (out_ref, xs, adj, acc, pairs, sems, rsems) = refs[:-7], refs[-7:]
    row_blocks, _, block = acc.shape
    nodes, rows = xs.shape[0] - 1, xs.shape[2]
    copies, q = [], 0
    for n, ref in enumerate(srcs):
        blocks = ref.shape[0] if len(ref.shape) == 3 else 1
        to = xs.at[pl.ds(q, blocks)] if blocks > 1 else xs.at[q]
        copies.append(pltpu.make_async_copy(ref, to, sems.at[n]))
        q += blocks
    for c in copies:
        c.start()
    lax.fori_loop(0, row_blocks, load_rows(counts_ref, adj_hbm, adj, rsems, True), 0)
    steps = list_pairs(counts_ref, pairs, adj.shape[0])
    acc[...] = jnp.zeros_like(acc)
    xs[nodes] = jnp.zeros_like(xs[nodes])
    for c in copies:
        c.wait()

    def work(r, both, places):
        x = []
        for where in places:
            q, at = split_place(where, rows, block)
            x.append(xs[q, :, at])
        x = jnp.concatenate(x, axis=1)
        return (lax.dot_general(x, both, (((1,), (1,)), ((), ())), preferred_element_type=F32),)

    def add(r, got):
        acc[r] += got

    over_pairs(place_ref, counts_ref, adj_hbm, adj, pairs, rsems, steps, work, add)
    for r in range(row_blocks):
        done = acc[r].astype(BF16)
        for p in (r // 2, (row_blocks + r) // 2):
            out_ref[p, :, r % 2 * block : (r % 2 + 1) * block] = done


def mid_kernel(agg_ref, row_ref, cross_ref, stay_ref):
    hid, width, span = agg_ref.shape
    half = row_ref.shape[0]
    total = hid * width
    agg = agg_ref[...].reshape(total, span)
    row = row_ref[...].reshape(half * width, row_ref.shape[2])
    cot = row[:, :span].astype(F32)
    wt = row[:, span : span + total]
    bias = jnp.sum(row[:, span + total :].astype(F32), axis=1, keepdims=True)
    pre = jnp.dot(wt, agg, preferred_element_type=F32) + bias
    sig = jax.nn.sigmoid(pre)
    hidden = (pre * sig).astype(BF16)
    slope = (cot * sig * (1.0 + pre * (1.0 - sig))).astype(BF16)
    ws = lax.dot_general(wt, slope, (((0,), (0,)), ((), ())), preferred_element_type=F32)
    cross_ref[...] = ws.astype(BF16).reshape(hid, width, span)
    wg = lax.dot_general(slope, agg, (((1,), (1,)), ((), ())), preferred_element_type=F32)
    tail = split3(jnp.sum(slope.astype(F32), axis=1, keepdims=True))
    stay_ref[:, :, :span] = hidden.reshape(half, width, span)
    stay_ref[:, :, span : span + total] = wg.astype(BF16).reshape(half, width, total)
    stay_ref[:, :, span + total :] = tail.astype(BF16).reshape(half, width, 128)


def bwd_kernel(
    place_ref, counts_ref, adj_hbm, cross_ref,
    own_ref, d2p, d2m, r1, l1, r2, l2, acc, adj, ws, pairs, rsems,
):
    nodes, (width, rows) = acc.shape[0] - 1, acc.shape[1:]
    block = adj.shape[1]
    row_blocks = counts_ref.shape[0]
    lax.fori_loop(0, row_blocks, load_rows(counts_ref, adj_hbm, adj, rsems, True), 0)
    steps = list_pairs(counts_ref, pairs, adj.shape[0])
    acc[...] = jnp.zeros_like(acc)
    half = row_blocks // 2
    for p in range(half):
        both_halves = cross_ref[p].astype(F32) + cross_ref[half + p].astype(F32)
        ws[2 * p] = both_halves[:, :block].astype(BF16)
        ws[2 * p + 1] = both_halves[:, block:].astype(BF16)

    def work(r, both, places):
        made = jnp.dot(ws[r], both, preferred_element_type=F32)
        return made, places

    def add(r, made, places):
        for n, where in enumerate(places):
            q, at = split_place(where, rows, block)
            acc[q, :, at] += made[:, n * block : (n + 1) * block]

    over_pairs(place_ref, counts_ref, adj_hbm, adj, pairs, rsems, steps, work, add)

    def put(ref, n, q):
        ref[n] = acc[q].astype(BF16)

    for s in range(ZN):
        put(own_ref, s, s)
        right, left = (r2, l2) if s < 2 else (r1, l1)
        put(right, s % 2, ZN + s)
        put(left, s % 2, 3 * ZN + s)
    for n, s in enumerate((2, 0)):
        put(d2p, n, 2 * ZN + s)
        put(d2m, n, 2 * ZN + s + 1)


def fold_kernel(stay_ref, hidden_ref, out_ref):
    nodes, width, _ = out_ref.shape
    total = nodes * width
    half = stay_ref.shape[0]
    span = hidden_ref.shape[1] // half
    wg = jnp.zeros((width, total), F32)
    tail = jnp.zeros((width, 128), F32)
    for p in range(half):
        hidden_ref[:, p * span : (p + 1) * span] = stay_ref[p, :, :span]
        wg = wg + stay_ref[p, :, span : span + total].astype(F32)
        tail = tail + stay_ref[p, :, span + total :].astype(F32)
    tail = pltpu.roll(split3(jnp.sum(tail, axis=1, keepdims=True)), width, 1)
    lane = lax.broadcasted_iota(jnp.int32, (width, 128), 1)
    for a in range(nodes):
        tile = wg[:, (a * width) // 128 * 128 : (a * width) // 128 * 128 + 128]
        start = (a * width) % 128
        if start:
            tile = pltpu.roll(tile, 128 - start, 1)
        out_ref[a] = jnp.where(lane < width, tile, tail).astype(BF16)


def relay_kernel(r1, l1, r2, l2, from_left, from_right, r1_out, l1_out, r2_out, l2_out):
    for n, (right, left, right_out, left_out) in enumerate(
        ((r1, l1, r1_out, l1_out), (r2, l2, r2_out, l2_out))
    ):
        right_out[0] = (right[0].astype(F32) + from_left[n].astype(F32)).astype(BF16)
        right_out[1] = right[1]
        left_out[0] = left[0]
        left_out[1] = (left[1].astype(F32) + from_right[n].astype(F32)).astype(BF16)


def joined(own_ref, right, left, s):
    n = s % 2
    return own_ref[s].astype(F32) + right[n].astype(F32) + left[n].astype(F32)


def join_far_kernel(own_ref, right, left, s2, s3):
    s2[...] = joined(own_ref, right, left, 2)
    s3[...] = joined(own_ref, right, left, 3).astype(BF16)


def join_near_kernel(own_ref, right, left, s1):
    s1[...] = joined(own_ref, right, left, 1).astype(BF16)


def last_kernel(scale, own_ref, right, left, near, far, parts_ref, feat_ref, wg_ref, bias_ref):
    total = joined(own_ref, right, left, 0) + near[...].astype(F32) + far[...].astype(F32)
    feat_ref[...] = total.astype(BF16)
    width = feat_ref.shape[0]
    tail = parts_ref[0].astype(F32)
    for a in range(1, parts_ref.shape[0]):
        tail = tail + parts_ref[a].astype(F32)
    lane = lax.broadcasted_iota(jnp.int32, tail.shape, 1)
    bsum = jnp.sum(jnp.where(lane >= width, tail, 0.0), axis=1, keepdims=True)
    bias_ref[...] = jnp.broadcast_to(bsum * scale, (width, 128)).T[:1]
    wg_ref[...] = tail[:, :width].T * scale


def spec(space):
    return pl.BlockSpec(memory_space=space)


def cost(us):
    return pl.CostEstimate(flops=0, bytes_accessed=int(us * 3e6), transcendentals=0)


def params(mib):
    return pltpu.CompilerParams(vmem_limit_bytes=mib * MIB)


def per_device(feats, weight, bias, adjacency, columns, counts, cotangent):
    width, rows = feats.shape
    row_blocks, capacity, block, _ = adjacency.shape
    nodes, hid = lax.axis_size("node"), lax.axis_size("hid")
    total = weight.shape[0]
    scale = 1.0 / math.sqrt(nodes * rows)
    me = lax.axis_index("node")
    blocks = adjacency.reshape(row_blocks * capacity, block, block)

    half = hid // 2
    span = rows // half
    halves = [list(range(half)), list(range(half, hid))]

    def exchange_half(v):
        return lax.all_to_all(v, "hid", 0, 0, axis_index_groups=halves, tiled=True)

    def exchange(v):
        return lax.all_to_all(v, "hid", 0, 0, tiled=True)

    with jax.named_scope("pack"):
        stay = jax.ShapeDtypeStruct((half, width, span + total + 128), BF16)
        row, place = pl.pallas_call(
            pack_kernel,
            out_shape=[stay, jax.ShapeDtypeStruct((row_blocks + 8, 128), jnp.int32)],
            in_specs=[spec(pltpu.SMEM)] * 2 + [spec(VMEM)] * 4,
            out_specs=[spec(VMEM)] * 2,
            compiler_params=params(57),
        )(
            jnp.stack([me, nodes]).astype(jnp.int32),
            counts, columns, cotangent, weight.T, bias.reshape(1, width),
        )

    with jax.named_scope("node_gather"):
        z1, z2 = flip_z(feats, 1, nodes), flip_z(feats, 2, nodes)
        z3 = flip_z(z2, 1, nodes)
        left0, right0 = shift_x(feats, 1, nodes), shift_x(feats, -1, nodes)
        z1, left0, right0, place = lax.optimization_barrier((z1, left0, right0, place))
        row = exchange_half(row)
        here = [feats, jnp.stack([z1, z2]), z3]
        left = [left0] + [shift_x(v, 1, nodes) for v in here[1:]]
        right = [right0] + [shift_x(v, -1, nodes) for v in here[1:]]
        across = [
            shift_x(right[0], -1, nodes),
            shift_x(left[1][0], 1, nodes),
            shift_x(right[1][1], -1, nodes),
            shift_x(left[2], 1, nodes),
        ]
    sources = here + right + across + left
    row, sources = lax.optimization_barrier((row, sources))


    with jax.named_scope("aggregate"):
        agg = pl.pallas_call(
            fwd_kernel,
            out_shape=jax.ShapeDtypeStruct((hid, width, span), BF16),
            in_specs=[spec(pltpu.SMEM)] * 2 + [spec(pl.ANY)] * (1 + len(sources)),
            out_specs=spec(VMEM),
            scratch_shapes=[
                VMEM((nodes + 1, width, rows), BF16),
                VMEM(blocks.shape, BF16),
                VMEM((row_blocks, width, block), F32),
                pltpu.SMEM((row_blocks * capacity // 2 + UNROLL,), jnp.int32),
                pltpu.SemaphoreType.DMA((len(sources),)),
                pltpu.SemaphoreType.DMA((row_blocks, capacity // QUARTER)),
            ],
            compiler_params=params(AGG),
            cost_estimate=cost(9),
        )(place, counts, blocks, *sources)
    agg = exchange(agg)

    with jax.named_scope("dense"):
        cross, kept = pl.pallas_call(
            mid_kernel,
            out_shape=[jax.ShapeDtypeStruct((hid, width, span), BF16), stay],
            in_specs=[spec(VMEM)] * 2,
            out_specs=[spec(VMEM)] * 2,
            compiler_params=params(16),
        )(agg, row)
    cross = exchange(cross)
    kept, cross = lax.optimization_barrier((kept, cross))
    kept = exchange_half(kept)

    one = jax.ShapeDtypeStruct((width, rows), BF16)
    two = jax.ShapeDtypeStruct((2, width, rows), BF16)
    with jax.named_scope("spread"):
        own, d2p, d2m, r1, l1, r2, l2 = pl.pallas_call(
            bwd_kernel,
            out_shape=[jax.ShapeDtypeStruct((ZN, width, rows), BF16)] + [two] * 6,
            in_specs=[spec(pltpu.SMEM)] * 2 + [spec(pl.ANY), spec(VMEM)],
            out_specs=[spec(VMEM)] * 7,
            scratch_shapes=[
                VMEM((nodes + 1, width, rows), F32),
                VMEM(blocks.shape, BF16),
                VMEM((row_blocks, width, block), BF16),
                pltpu.SMEM((row_blocks * capacity // 2 + UNROLL,), jnp.int32),
                pltpu.SemaphoreType.DMA((row_blocks, capacity // QUARTER)),
            ],
            compiler_params=params(SPR),
            cost_estimate=cost(9),
        )(place, counts, blocks, cross)

    def small(kernel, outs, *args):
        return pl.pallas_call(
            kernel,
            out_shape=outs,
            in_specs=[spec(VMEM)] * len(args),
            out_specs=[spec(VMEM)] * len(outs),
            compiler_params=params(8),
        )(*args)

    with jax.named_scope("node_sum"):
        from_left, from_right = shift_x(d2p, 1, nodes), shift_x(d2m, -1, nodes)
        r1, l1, r2, l2 = small(relay_kernel, [two] * 4, r1, l1, r2, l2, from_left, from_right)
        r1, l1 = shift_x(r1, 1, nodes), shift_x(l1, -1, nodes)
        r1, l1, r2, l2 = lax.optimization_barrier((r1, l1, r2, l2))
        r2, l2 = shift_x(r2, 1, nodes), shift_x(l2, -1, nodes)
        s2, s3 = small(join_far_kernel, [jax.ShapeDtypeStruct(one.shape, F32), one], own, r1, l1)
        s3 = flip_z(s3, 1, nodes)
        kept, _ = lax.optimization_barrier((kept, s3))
        hidden, parts = small(
            fold_kernel, [one, jax.ShapeDtypeStruct((nodes, width, 128), BF16)], kept
        )
        parts = lax.all_to_all(parts, "node", 0, 0, tiled=True)
        far = (s2 + s3.astype(F32)).astype(BF16)
        far = flip_z(far, 2, nodes)
        (s1,) = small(join_near_kernel, [one], own, r2, l2)
        near = flip_z(s1, 1, nodes)
        feat_grad, weight_grad, bias_grad = small(
            functools.partial(last_kernel, scale),
            [
                jax.ShapeDtypeStruct((width, rows), BF16),
                jax.ShapeDtypeStruct((width, width), F32),
                jax.ShapeDtypeStruct((1, width), F32),
            ],
            own, r2, l2, near, far, parts,
        )
    return hidden, feat_grad, weight_grad, bias_grad.reshape(width)


def solution(mesh):
    placed = (
        P("hid", "node"),
        P(None, "hid"),
        P("hid"),
        P("node", None, None, None),
        P("node", None),
        P("node"),
        P("hid", "node"),
    )
    return jax.shard_map(
        per_device,
        mesh=mesh,
        in_specs=placed,
        out_specs=(P("hid", "node"), P("hid", "node"), P("node", "hid"), P("hid")),
        check_vma=False,
    )
```

```python
import functools
import math

import jax
import jax.numpy as jnp
from jax import lax
from jax.experimental import pallas as pl
from jax.experimental.pallas import tpu as pltpu
from jax.sharding import PartitionSpec as P

F32 = jnp.float32
BF16 = jnp.bfloat16
ZN = 4
UNROLL = 16
QUARTER = 4
VMEM = pltpu.VMEM
MIB = 1024 * 1024
AGG, SPR = 56, 50


def shift_x(v, by, n):
    return lax.ppermute(v, "node", [(i, (i + ZN * by) % n) for i in range(n)])


def flip_z(v, by, n):
    return lax.ppermute(v, "node", [(i, i ^ by) for i in range(n)])


def split3(v):
    hi = v.astype(BF16).astype(F32)
    mid = (v - hi).astype(BF16).astype(F32)
    low = v - hi - mid
    lane = lax.broadcasted_iota(jnp.int32, (v.shape[0], 128), 1)
    return jnp.where(lane == 0, hi, jnp.where(lane == 1, mid, jnp.where(lane == 2, low, 0.0)))


def load_rows(counts_ref, adj_hbm, adj, sems, begin):
    row_blocks, pieces = sems.shape

    def one(r, q):
        at = pl.ds((r * pieces + q) * QUARTER, QUARTER)
        return pltpu.make_async_copy(adj_hbm.at[at], adj.at[at], sems.at[r, q])

    def row(r, carry):
        for q in range(pieces):

            @pl.when(counts_ref[r] > q * QUARTER)
            def _():
                one(r, q).start() if begin else one(r, q).wait()

        return carry

    return row


def list_pairs(counts_ref, pairs_ref, none):
    row_blocks = counts_ref.shape[0]
    capacity = none // row_blocks

    def row(r, n):
        def one(p, n):
            pairs_ref[n] = r * capacity + 2 * p
            return n + 1

        return lax.fori_loop(0, (counts_ref[r] + 1) >> 1, one, n)

    used = lax.fori_loop(0, row_blocks, row, 0)
    for i in range(UNROLL):
        pairs_ref[used + i] = none
    return (used + UNROLL - 1) // UNROLL


def over_pairs(place_ref, counts_ref, adj_hbm, adj, pairs, sems, steps, work, add):
    row_blocks = counts_ref.shape[0]
    none = adj.shape[0]
    shift = (none // row_blocks).bit_length() - 1

    def step(i, ready):
        slots = [pairs[i * UNROLL + u] for u in range(UNROLL)]
        inside = [slot & (none - 1) for slot in slots]
        rows = [at >> shift for at in inside]
        last = functools.reduce(jnp.maximum, rows)
        lax.fori_loop(ready, last + 1, load_rows(counts_ref, adj_hbm, adj, sems, False), 0)
        for slot, at, r in zip(slots, inside, rows):
            k = slot & (none // row_blocks - 1)
            both = jnp.concatenate([adj[at], adj[at + 1]], axis=1)
            add(r, *work(r, both, (place_ref[slot >> shift, k], place_ref[slot >> shift, k + 1])))
        return jnp.maximum(ready, last + 1)

    lax.fori_loop(0, steps, step, 0)


def split_place(where, rows, block):
    return where >> (rows.bit_length() - 1), pl.ds(pl.multiple_of(where & (rows - 1), block), block)


def pack_kernel(me_ref, counts_ref, columns_ref, cot_ref, wt_ref, bias_ref, out_ref, place_ref):
    row_blocks, capacity = columns_ref.shape
    rows, block = cot_ref.shape[1], cot_ref.shape[1] // row_blocks
    x, z = me_ref[0] >> 2, me_ref[0] & (ZN - 1)
    column = columns_ref[...]
    index = lax.div(column, row_blocks)
    plane = (((index >> 2) - x) & (ZN - 1)) * ZN + ((index & (ZN - 1)) ^ z)
    place = plane * rows + lax.rem(column, row_blocks) * block
    slot = lax.broadcasted_iota(jnp.int32, (1, capacity), 1)
    place_ref[...] = jnp.full(place_ref.shape, me_ref[1] * rows, jnp.int32)
    for r in range(row_blocks):
        place_ref[r : r + 1, :capacity] = jnp.where(
            slot < counts_ref[r], place[r : r + 1], me_ref[1] * rows
        )
    parts = out_ref.shape[0]
    width, total = wt_ref.shape
    span = cot_ref.shape[1] // parts
    bias = jnp.broadcast_to(bias_ref[...], (width, width)).T[:, :1]
    tail = split3(bias).astype(BF16)
    for p in range(parts):
        out_ref[p, :, :span] = cot_ref[:, p * span : (p + 1) * span]
        out_ref[p, :, span : span + total] = wt_ref[...]
        out_ref[p, :, span + total :] = tail


def fwd_kernel(place_ref, counts_ref, adj_hbm, *refs):
    srcs, (out_ref, xs, adj, acc, pairs, sems, rsems) = refs[:-7], refs[-7:]
    row_blocks, _, block = acc.shape
    nodes, rows = xs.shape[0] - 1, xs.shape[2]
    copies, q = [], 0
    for n, ref in enumerate(srcs):
        blocks = ref.shape[0] if len(ref.shape) == 3 else 1
        to = xs.at[pl.ds(q, blocks)] if blocks > 1 else xs.at[q]
        copies.append(pltpu.make_async_copy(ref, to, sems.at[n]))
        q += blocks
    for c in copies:
        c.start()
    lax.fori_loop(0, row_blocks, load_rows(counts_ref, adj_hbm, adj, rsems, True), 0)
    steps = list_pairs(counts_ref, pairs, adj.shape[0])
    acc[...] = jnp.zeros_like(acc)
    xs[nodes] = jnp.zeros_like(xs[nodes])
    for c in copies:
        c.wait()

    def work(r, both, places):
        x = []
        for where in places:
            q, at = split_place(where, rows, block)
            x.append(xs[q, :, at])
        x = jnp.concatenate(x, axis=1)
        return (lax.dot_general(x, both, (((1,), (1,)), ((), ())), preferred_element_type=F32),)

    def add(r, got):
        acc[r] += got

    over_pairs(place_ref, counts_ref, adj_hbm, adj, pairs, rsems, steps, work, add)
    for r in range(row_blocks):
        done = acc[r].astype(BF16)
        for p in (r // 2, (row_blocks + r) // 2):
            out_ref[p, :, r % 2 * block : (r % 2 + 1) * block] = done


def mid_kernel(agg_ref, row_ref, cross_ref, stay_ref):
    hid, width, span = agg_ref.shape
    half = row_ref.shape[0]
    total = hid * width
    agg = agg_ref[...].reshape(total, span)
    row = row_ref[...].reshape(half * width, row_ref.shape[2])
    cot = row[:, :span].astype(F32)
    wt = row[:, span : span + total]
    bias = jnp.sum(row[:, span + total :].astype(F32), axis=1, keepdims=True)
    pre = jnp.dot(wt, agg, preferred_element_type=F32) + bias
    sig = jax.nn.sigmoid(pre)
    hidden = (pre * sig).astype(BF16)
    slope = (cot * sig * (1.0 + pre * (1.0 - sig))).astype(BF16)
    ws = lax.dot_general(wt, slope, (((0,), (0,)), ((), ())), preferred_element_type=F32)
    cross_ref[...] = ws.astype(BF16).reshape(hid, width, span)
    wg = lax.dot_general(slope, agg, (((1,), (1,)), ((), ())), preferred_element_type=F32)
    tail = split3(jnp.sum(slope.astype(F32), axis=1, keepdims=True))
    stay_ref[:, :, :span] = hidden.reshape(half, width, span)
    stay_ref[:, :, span : span + total] = wg.astype(BF16).reshape(half, width, total)
    stay_ref[:, :, span + total :] = tail.astype(BF16).reshape(half, width, 128)


def bwd_kernel(
    place_ref, counts_ref, adj_hbm, cross_ref,
    own_ref, d2p, d2m, r1, l1, r2, l2, acc, adj, ws, pairs, rsems,
):
    nodes, (width, rows) = acc.shape[0] - 1, acc.shape[1:]
    block = adj.shape[1]
    row_blocks = counts_ref.shape[0]
    lax.fori_loop(0, row_blocks, load_rows(counts_ref, adj_hbm, adj, rsems, True), 0)
    steps = list_pairs(counts_ref, pairs, adj.shape[0])
    acc[...] = jnp.zeros_like(acc)
    half = row_blocks // 2
    for p in range(half):
        both_halves = cross_ref[p].astype(F32) + cross_ref[half + p].astype(F32)
        ws[2 * p] = both_halves[:, :block].astype(BF16)
        ws[2 * p + 1] = both_halves[:, block:].astype(BF16)

    def work(r, both, places):
        made = jnp.dot(ws[r], both, preferred_element_type=F32)
        return made, places

    def add(r, made, places):
        for n, where in enumerate(places):
            q, at = split_place(where, rows, block)
            acc[q, :, at] += made[:, n * block : (n + 1) * block]

    over_pairs(place_ref, counts_ref, adj_hbm, adj, pairs, rsems, steps, work, add)

    def put(ref, n, q):
        ref[n] = acc[q].astype(BF16)

    for s in range(ZN):
        put(own_ref, s, s)
        right, left = (r2, l2) if s < 2 else (r1, l1)
        put(right, s % 2, ZN + s)
        put(left, s % 2, 3 * ZN + s)
    for n, s in enumerate((2, 0)):
        put(d2p, n, 2 * ZN + s)
        put(d2m, n, 2 * ZN + s + 1)


def fold_kernel(stay_ref, hidden_ref, out_ref):
    nodes, width, _ = out_ref.shape
    total = nodes * width
    half = stay_ref.shape[0]
    span = hidden_ref.shape[1] // half
    wg = jnp.zeros((width, total), F32)
    tail = jnp.zeros((width, 128), F32)
    for p in range(half):
        hidden_ref[:, p * span : (p + 1) * span] = stay_ref[p, :, :span]
        wg = wg + stay_ref[p, :, span : span + total].astype(F32)
        tail = tail + stay_ref[p, :, span + total :].astype(F32)
    tail = pltpu.roll(split3(jnp.sum(tail, axis=1, keepdims=True)), width, 1)
    lane = lax.broadcasted_iota(jnp.int32, (width, 128), 1)
    for a in range(nodes):
        tile = wg[:, (a * width) // 128 * 128 : (a * width) // 128 * 128 + 128]
        start = (a * width) % 128
        if start:
            tile = pltpu.roll(tile, 128 - start, 1)
        out_ref[a] = jnp.where(lane < width, tile, tail).astype(BF16)


def relay_kernel(r1, l1, r2, l2, from_left, from_right, r1_out, l1_out, r2_out, l2_out):
    for n, (right, left, right_out, left_out) in enumerate(
        ((r1, l1, r1_out, l1_out), (r2, l2, r2_out, l2_out))
    ):
        right_out[0] = (right[0].astype(F32) + from_left[n].astype(F32)).astype(BF16)
        right_out[1] = right[1]
        left_out[0] = left[0]
        left_out[1] = (left[1].astype(F32) + from_right[n].astype(F32)).astype(BF16)


def joined(own_ref, right, left, s):
    n = s % 2
    return own_ref[s].astype(F32) + right[n].astype(F32) + left[n].astype(F32)


def join_far_kernel(own_ref, right, left, s2, s3):
    s2[...] = joined(own_ref, right, left, 2)
    s3[...] = joined(own_ref, right, left, 3).astype(BF16)


def join_near_kernel(own_ref, right, left, s1):
    s1[...] = joined(own_ref, right, left, 1).astype(BF16)


def last_kernel(scale, own_ref, right, left, near, far, parts_ref, feat_ref, wg_ref, bias_ref):
    total = joined(own_ref, right, left, 0) + near[...].astype(F32) + far[...].astype(F32)
    feat_ref[...] = total.astype(BF16)
    width = feat_ref.shape[0]
    tail = parts_ref[0].astype(F32)
    for a in range(1, parts_ref.shape[0]):
        tail = tail + parts_ref[a].astype(F32)
    lane = lax.broadcasted_iota(jnp.int32, tail.shape, 1)
    bsum = jnp.sum(jnp.where(lane >= width, tail, 0.0), axis=1, keepdims=True)
    bias_ref[...] = jnp.broadcast_to(bsum * scale, (width, 128)).T[:1]
    wg_ref[...] = tail[:, :width].T * scale


def spec(space):
    return pl.BlockSpec(memory_space=space)


def cost(us):
    return pl.CostEstimate(flops=0, bytes_accessed=int(us * 3e6), transcendentals=0)


def params(mib):
    return pltpu.CompilerParams(vmem_limit_bytes=mib * MIB)


def per_device(feats, weight, bias, adjacency, columns, counts, cotangent):
    width, rows = feats.shape
    row_blocks, capacity, block, _ = adjacency.shape
    nodes, hid = lax.axis_size("node"), lax.axis_size("hid")
    total = weight.shape[0]
    scale = 1.0 / math.sqrt(nodes * rows)
    me = lax.axis_index("node")
    blocks = adjacency.reshape(row_blocks * capacity, block, block)

    half = hid // 2
    span = rows // half
    halves = [list(range(half)), list(range(half, hid))]

    def exchange_half(v):
        return lax.all_to_all(v, "hid", 0, 0, axis_index_groups=halves, tiled=True)

    def exchange(v):
        return lax.all_to_all(v, "hid", 0, 0, tiled=True)

    with jax.named_scope("pack"):
        stay = jax.ShapeDtypeStruct((half, width, span + total + 128), BF16)
        row, place = pl.pallas_call(
            pack_kernel,
            out_shape=[stay, jax.ShapeDtypeStruct((row_blocks + 8, 128), jnp.int32)],
            in_specs=[spec(pltpu.SMEM)] * 2 + [spec(VMEM)] * 4,
            out_specs=[spec(VMEM)] * 2,
            compiler_params=params(57),
        )(
            jnp.stack([me, nodes]).astype(jnp.int32),
            counts, columns, cotangent, weight.T, bias.reshape(1, width),
        )

    with jax.named_scope("node_gather"):
        z1, z2 = flip_z(feats, 1, nodes), flip_z(feats, 2, nodes)
        z3 = flip_z(z2, 1, nodes)
        left0, right0 = shift_x(feats, 1, nodes), shift_x(feats, -1, nodes)
        z1, left0, right0, place = lax.optimization_barrier((z1, left0, right0, place))
        row = exchange_half(row)
        here = [feats, jnp.stack([z1, z2]), z3]
        left = [left0] + [shift_x(v, 1, nodes) for v in here[1:]]
        right = [right0] + [shift_x(v, -1, nodes) for v in here[1:]]
        across = [
            shift_x(right[0], -1, nodes),
            shift_x(left[1][0], 1, nodes),
            shift_x(right[1][1], -1, nodes),
            shift_x(left[2], 1, nodes),
        ]
    sources = here + right + across + left
    row, sources = lax.optimization_barrier((row, sources))


    with jax.named_scope("aggregate"):
        agg = pl.pallas_call(
            fwd_kernel,
            out_shape=jax.ShapeDtypeStruct((hid, width, span), BF16),
            in_specs=[spec(pltpu.SMEM)] * 2 + [spec(pl.ANY)] * (1 + len(sources)),
            out_specs=spec(VMEM),
            scratch_shapes=[
                VMEM((nodes + 1, width, rows), BF16),
                VMEM(blocks.shape, BF16),
                VMEM((row_blocks, width, block), F32),
                pltpu.SMEM((row_blocks * capacity // 2 + UNROLL,), jnp.int32),
                pltpu.SemaphoreType.DMA((len(sources),)),
                pltpu.SemaphoreType.DMA((row_blocks, capacity // QUARTER)),
            ],
            compiler_params=params(AGG),
            cost_estimate=cost(9),
        )(place, counts, blocks, *sources)
    agg = exchange(agg)

    with jax.named_scope("dense"):
        cross, kept = pl.pallas_call(
            mid_kernel,
            out_shape=[jax.ShapeDtypeStruct((hid, width, span), BF16), stay],
            in_specs=[spec(VMEM)] * 2,
            out_specs=[spec(VMEM)] * 2,
            compiler_params=params(16),
        )(agg, row)
    cross = exchange(cross)
    kept, cross = lax.optimization_barrier((kept, cross))
    kept = exchange_half(kept)

    one = jax.ShapeDtypeStruct((width, rows), BF16)
    two = jax.ShapeDtypeStruct((2, width, rows), BF16)
    with jax.named_scope("spread"):
        own, d2p, d2m, r1, l1, r2, l2 = pl.pallas_call(
            bwd_kernel,
            out_shape=[jax.ShapeDtypeStruct((ZN, width, rows), BF16)] + [two] * 6,
            in_specs=[spec(pltpu.SMEM)] * 2 + [spec(pl.ANY), spec(VMEM)],
            out_specs=[spec(VMEM)] * 7,
            scratch_shapes=[
                VMEM((nodes + 1, width, rows), F32),
                VMEM(blocks.shape, BF16),
                VMEM((row_blocks, width, block), BF16),
                pltpu.SMEM((row_blocks * capacity // 2 + UNROLL,), jnp.int32),
                pltpu.SemaphoreType.DMA((row_blocks, capacity // QUARTER)),
            ],
            compiler_params=params(SPR),
            cost_estimate=cost(9),
        )(place, counts, blocks, cross)

    def small(kernel, outs, *args):
        return pl.pallas_call(
            kernel,
            out_shape=outs,
            in_specs=[spec(VMEM)] * len(args),
            out_specs=[spec(VMEM)] * len(outs),
            compiler_params=params(8),
        )(*args)

    with jax.named_scope("node_sum"):
        from_left, from_right = shift_x(d2p, 1, nodes), shift_x(d2m, -1, nodes)
        r1, l1, r2, l2 = small(relay_kernel, [two] * 4, r1, l1, r2, l2, from_left, from_right)
        r1, l1 = shift_x(r1, 1, nodes), shift_x(l1, -1, nodes)
        r1, l1, r2, l2 = lax.optimization_barrier((r1, l1, r2, l2))
        r2, l2 = shift_x(r2, 1, nodes), shift_x(l2, -1, nodes)
        s2, s3 = small(join_far_kernel, [jax.ShapeDtypeStruct(one.shape, F32), one], own, r1, l1)
        s3 = flip_z(s3, 1, nodes)
        kept, _ = lax.optimization_barrier((kept, s3))
        hidden, parts = small(
            fold_kernel, [one, jax.ShapeDtypeStruct((nodes, width, 128), BF16)], kept
        )
        parts = lax.all_to_all(parts, "node", 0, 0, tiled=True)
        far = (s2 + s3.astype(F32)).astype(BF16)
        far = flip_z(far, 2, nodes)
        (s1,) = small(join_near_kernel, [one], own, r2, l2)
        near = flip_z(s1, 1, nodes)
        feat_grad, weight_grad, bias_grad = small(
            functools.partial(last_kernel, scale),
            [
                jax.ShapeDtypeStruct((width, rows), BF16),
                jax.ShapeDtypeStruct((width, width), F32),
                jax.ShapeDtypeStruct((1, width), F32),
            ],
            own, r2, l2, near, far, parts,
        )
    return hidden, feat_grad, weight_grad, bias_grad.reshape(width)


def solution(mesh):
    placed = (
        P("hid", "node"),
        P(None, "hid"),
        P("hid"),
        P("node", None, None, None),
        P("node", None),
        P("node"),
        P("hid", "node"),
    )
    return jax.shard_map(
        per_device,
        mesh=mesh,
        in_specs=placed,
        out_specs=(P("hid", "node"), P("hid", "node"), P("node", "hid"), P("hid")),
        check_vma=False,
    )
```

```python
import functools
import math

import jax
import jax.numpy as jnp
from jax import lax
from jax.experimental import pallas as pl
from jax.experimental.pallas import tpu as pltpu
from jax.sharding import PartitionSpec as P

F32 = jnp.float32
BF16 = jnp.bfloat16
ZN = 4
UNROLL = 8
QUARTER = 4
VMEM = pltpu.VMEM
MIB = 1024 * 1024
AGG, SPR = 56, 50


def shift_x(v, by, n):
    return lax.ppermute(v, "node", [(i, (i + ZN * by) % n) for i in range(n)])


def flip_z(v, by, n):
    return lax.ppermute(v, "node", [(i, i ^ by) for i in range(n)])


def split3(v):
    hi = v.astype(BF16).astype(F32)
    mid = (v - hi).astype(BF16).astype(F32)
    low = v - hi - mid
    lane = lax.broadcasted_iota(jnp.int32, (v.shape[0], 128), 1)
    return jnp.where(lane == 0, hi, jnp.where(lane == 1, mid, jnp.where(lane == 2, low, 0.0)))


def load_rows(counts_ref, adj_hbm, adj, sems, begin):
    row_blocks, pieces = sems.shape

    def one(r, q):
        at = pl.ds((r * pieces + q) * QUARTER, QUARTER)
        return pltpu.make_async_copy(adj_hbm.at[at], adj.at[at], sems.at[r, q])

    def row(r, carry):
        for q in range(pieces):

            @pl.when(counts_ref[r] > q * QUARTER)
            def _():
                one(r, q).start() if begin else one(r, q).wait()

        return carry

    return row


def list_pairs(counts_ref, pairs_ref, none):
    row_blocks = counts_ref.shape[0]
    capacity = none // row_blocks

    def row(r, n):
        def one(p, n):
            pairs_ref[n] = r * capacity + 2 * p
            return n + 1

        return lax.fori_loop(0, (counts_ref[r] + 1) >> 1, one, n)

    used = lax.fori_loop(0, row_blocks, row, 0)
    for i in range(UNROLL):
        pairs_ref[used + i] = none
    return (used + UNROLL - 1) // UNROLL


def over_pairs(place_ref, counts_ref, adj_hbm, adj, pairs, sems, steps, work, add):
    row_blocks = counts_ref.shape[0]
    none = adj.shape[0]
    shift = (none // row_blocks).bit_length() - 1

    def step(i, ready):
        slots = [pairs[i * UNROLL + u] for u in range(UNROLL)]
        inside = [slot & (none - 1) for slot in slots]
        rows = [at >> shift for at in inside]
        last = functools.reduce(jnp.maximum, rows)
        lax.fori_loop(ready, last + 1, load_rows(counts_ref, adj_hbm, adj, sems, False), 0)
        parts = []
        for slot, at, r in zip(slots, inside, rows):
            k = slot & (none // row_blocks - 1)
            both = jnp.concatenate([adj[at], adj[at + 1]], axis=1)
            parts.append((r, *work(r, both, (place_ref[slot >> shift, k], place_ref[slot >> shift, k + 1]))))
        for part in parts:
            add(*part)
        return jnp.maximum(ready, last + 1)

    lax.fori_loop(0, steps, step, 0)


def split_place(where, rows, block):
    return where >> (rows.bit_length() - 1), pl.ds(pl.multiple_of(where & (rows - 1), block), block)


def pack_kernel(me_ref, counts_ref, columns_ref, cot_ref, wt_ref, bias_ref, out_ref, place_ref):
    row_blocks, capacity = columns_ref.shape
    rows, block = cot_ref.shape[1], cot_ref.shape[1] // row_blocks
    x, z = me_ref[0] >> 2, me_ref[0] & (ZN - 1)
    column = columns_ref[...]
    index = lax.div(column, row_blocks)
    plane = (((index >> 2) - x) & (ZN - 1)) * ZN + ((index & (ZN - 1)) ^ z)
    place = plane * rows + lax.rem(column, row_blocks) * block
    slot = lax.broadcasted_iota(jnp.int32, (1, capacity), 1)
    place_ref[...] = jnp.full(place_ref.shape, me_ref[1] * rows, jnp.int32)
    for r in range(row_blocks):
        place_ref[r : r + 1, :capacity] = jnp.where(
            slot < counts_ref[r], place[r : r + 1], me_ref[1] * rows
        )
    parts = out_ref.shape[0]
    width, total = wt_ref.shape
    span = cot_ref.shape[1] // parts
    bias = jnp.broadcast_to(bias_ref[...], (width, width)).T[:, :1]
    tail = split3(bias).astype(BF16)
    for p in range(parts):
        out_ref[p, :, :span] = cot_ref[:, p * span : (p + 1) * span]
        out_ref[p, :, span : span + total] = wt_ref[...]
        out_ref[p, :, span + total :] = tail


def fwd_kernel(place_ref, counts_ref, adj_hbm, *refs):
    srcs, (out_ref, xs, adj, acc, pairs, sems, rsems) = refs[:-7], refs[-7:]
    row_blocks, _, block = acc.shape
    nodes, rows = xs.shape[0] - 1, xs.shape[2]
    copies, q = [], 0
    for n, ref in enumerate(srcs):
        blocks = ref.shape[0] if len(ref.shape) == 3 else 1
        to = xs.at[pl.ds(q, blocks)] if blocks > 1 else xs.at[q]
        copies.append(pltpu.make_async_copy(ref, to, sems.at[n]))
        q += blocks
    for c in copies:
        c.start()
    lax.fori_loop(0, row_blocks, load_rows(counts_ref, adj_hbm, adj, rsems, True), 0)
    steps = list_pairs(counts_ref, pairs, adj.shape[0])
    acc[...] = jnp.zeros_like(acc)
    xs[nodes] = jnp.zeros_like(xs[nodes])
    for c in copies:
        c.wait()

    def work(r, both, places):
        x = []
        for where in places:
            q, at = split_place(where, rows, block)
            x.append(xs[q, :, at])
        x = jnp.concatenate(x, axis=1)
        return (lax.dot_general(x, both, (((1,), (1,)), ((), ())), preferred_element_type=F32),)

    def add(r, got):
        acc[r] += got

    over_pairs(place_ref, counts_ref, adj_hbm, adj, pairs, rsems, steps, work, add)
    for r in range(row_blocks):
        done = acc[r].astype(BF16)
        for p in (r // 2, (row_blocks + r) // 2):
            out_ref[p, :, r % 2 * block : (r % 2 + 1) * block] = done


def mid_kernel(agg_ref, row_ref, cross_ref, stay_ref):
    hid, width, span = agg_ref.shape
    half = row_ref.shape[0]
    total = hid * width
    agg = agg_ref[...].reshape(total, span)
    row = row_ref[...].reshape(half * width, row_ref.shape[2])
    cot = row[:, :span].astype(F32)
    wt = row[:, span : span + total]
    bias = jnp.sum(row[:, span + total :].astype(F32), axis=1, keepdims=True)
    pre = jnp.dot(wt, agg, preferred_element_type=F32) + bias
    sig = jax.nn.sigmoid(pre)
    hidden = (pre * sig).astype(BF16)
    slope = (cot * sig * (1.0 + pre * (1.0 - sig))).astype(BF16)
    ws = lax.dot_general(wt, slope, (((0,), (0,)), ((), ())), preferred_element_type=F32)
    cross_ref[...] = ws.astype(BF16).reshape(hid, width, span)
    wg = lax.dot_general(slope, agg, (((1,), (1,)), ((), ())), preferred_element_type=F32)
    tail = split3(jnp.sum(slope.astype(F32), axis=1, keepdims=True))
    stay_ref[:, :, :span] = hidden.reshape(half, width, span)
    stay_ref[:, :, span : span + total] = wg.astype(BF16).reshape(half, width, total)
    stay_ref[:, :, span + total :] = tail.astype(BF16).reshape(half, width, 128)


def bwd_kernel(
    place_ref, counts_ref, adj_hbm, cross_ref,
    own_ref, d2p, d2m, r1, l1, r2, l2, acc, adj, ws, pairs, rsems,
):
    nodes, (width, rows) = acc.shape[0] - 1, acc.shape[1:]
    block = adj.shape[1]
    row_blocks = counts_ref.shape[0]
    lax.fori_loop(0, row_blocks, load_rows(counts_ref, adj_hbm, adj, rsems, True), 0)
    steps = list_pairs(counts_ref, pairs, adj.shape[0])
    acc[...] = jnp.zeros_like(acc)
    half = row_blocks // 2
    for p in range(half):
        both_halves = cross_ref[p].astype(F32) + cross_ref[half + p].astype(F32)
        ws[2 * p] = both_halves[:, :block].astype(BF16)
        ws[2 * p + 1] = both_halves[:, block:].astype(BF16)

    def work(r, both, places):
        made = jnp.dot(ws[r], both, preferred_element_type=F32)
        return made, places

    def add(r, made, places):
        for n, where in enumerate(places):
            q, at = split_place(where, rows, block)
            acc[q, :, at] += made[:, n * block : (n + 1) * block]

    over_pairs(place_ref, counts_ref, adj_hbm, adj, pairs, rsems, steps, work, add)

    def put(ref, n, q):
        ref[n] = acc[q].astype(BF16)

    for s in range(ZN):
        put(own_ref, s, s)
        right, left = (r2, l2) if s < 2 else (r1, l1)
        put(right, s % 2, ZN + s)
        put(left, s % 2, 3 * ZN + s)
    for n, s in enumerate((2, 0)):
        put(d2p, n, 2 * ZN + s)
        put(d2m, n, 2 * ZN + s + 1)


def fold_kernel(stay_ref, hidden_ref, out_ref):
    nodes, width, _ = out_ref.shape
    total = nodes * width
    half = stay_ref.shape[0]
    span = hidden_ref.shape[1] // half
    wg = jnp.zeros((width, total), F32)
    tail = jnp.zeros((width, 128), F32)
    for p in range(half):
        hidden_ref[:, p * span : (p + 1) * span] = stay_ref[p, :, :span]
        wg = wg + stay_ref[p, :, span : span + total].astype(F32)
        tail = tail + stay_ref[p, :, span + total :].astype(F32)
    tail = pltpu.roll(split3(jnp.sum(tail, axis=1, keepdims=True)), width, 1)
    lane = lax.broadcasted_iota(jnp.int32, (width, 128), 1)
    for a in range(nodes):
        tile = wg[:, (a * width) // 128 * 128 : (a * width) // 128 * 128 + 128]
        start = (a * width) % 128
        if start:
            tile = pltpu.roll(tile, 128 - start, 1)
        out_ref[a] = jnp.where(lane < width, tile, tail).astype(BF16)


def relay_kernel(r1, l1, r2, l2, from_left, from_right, r1_out, l1_out, r2_out, l2_out):
    for n, (right, left, right_out, left_out) in enumerate(
        ((r1, l1, r1_out, l1_out), (r2, l2, r2_out, l2_out))
    ):
        right_out[0] = (right[0].astype(F32) + from_left[n].astype(F32)).astype(BF16)
        right_out[1] = right[1]
        left_out[0] = left[0]
        left_out[1] = (left[1].astype(F32) + from_right[n].astype(F32)).astype(BF16)


def joined(own_ref, right, left, s):
    n = s % 2
    return own_ref[s].astype(F32) + right[n].astype(F32) + left[n].astype(F32)


def join_far_kernel(own_ref, right, left, s2, s3):
    s2[...] = joined(own_ref, right, left, 2)
    s3[...] = joined(own_ref, right, left, 3).astype(BF16)


def join_near_kernel(own_ref, right, left, s1):
    s1[...] = joined(own_ref, right, left, 1).astype(BF16)


def last_kernel(scale, own_ref, right, left, near, far, parts_ref, feat_ref, wg_ref, bias_ref):
    total = joined(own_ref, right, left, 0) + near[...].astype(F32) + far[...].astype(F32)
    feat_ref[...] = total.astype(BF16)
    width = feat_ref.shape[0]
    tail = parts_ref[0].astype(F32)
    for a in range(1, parts_ref.shape[0]):
        tail = tail + parts_ref[a].astype(F32)
    lane = lax.broadcasted_iota(jnp.int32, tail.shape, 1)
    bsum = jnp.sum(jnp.where(lane >= width, tail, 0.0), axis=1, keepdims=True)
    bias_ref[...] = jnp.broadcast_to(bsum * scale, (width, 128)).T[:1]
    wg_ref[...] = tail[:, :width].T * scale


def spec(space):
    return pl.BlockSpec(memory_space=space)


def cost(us):
    return pl.CostEstimate(flops=0, bytes_accessed=int(us * 3e6), transcendentals=0)


def params(mib):
    return pltpu.CompilerParams(vmem_limit_bytes=mib * MIB)


def per_device(feats, weight, bias, adjacency, columns, counts, cotangent):
    width, rows = feats.shape
    row_blocks, capacity, block, _ = adjacency.shape
    nodes, hid = lax.axis_size("node"), lax.axis_size("hid")
    total = weight.shape[0]
    scale = 1.0 / math.sqrt(nodes * rows)
    me = lax.axis_index("node")
    blocks = adjacency.reshape(row_blocks * capacity, block, block)

    half = hid // 2
    span = rows // half
    halves = [list(range(half)), list(range(half, hid))]

    def exchange_half(v):
        return lax.all_to_all(v, "hid", 0, 0, axis_index_groups=halves, tiled=True)

    def exchange(v):
        return lax.all_to_all(v, "hid", 0, 0, tiled=True)

    with jax.named_scope("pack"):
        stay = jax.ShapeDtypeStruct((half, width, span + total + 128), BF16)
        row, place = pl.pallas_call(
            pack_kernel,
            out_shape=[stay, jax.ShapeDtypeStruct((row_blocks + 8, 128), jnp.int32)],
            in_specs=[spec(pltpu.SMEM)] * 2 + [spec(VMEM)] * 4,
            out_specs=[spec(VMEM)] * 2,
            compiler_params=params(57),
        )(
            jnp.stack([me, nodes]).astype(jnp.int32),
            counts, columns, cotangent, weight.T, bias.reshape(1, width),
        )

    with jax.named_scope("node_gather"):
        z1, z2 = flip_z(feats, 1, nodes), flip_z(feats, 2, nodes)
        z3 = flip_z(z2, 1, nodes)
        later, place = lax.optimization_barrier((feats, place))
        left0, right0 = shift_x(later, 1, nodes), shift_x(later, -1, nodes)
        z1, place = lax.optimization_barrier((z1, place))
        row = exchange_half(row)
        here = [feats, jnp.stack([z1, z2]), z3]
        left = [left0] + [shift_x(v, 1, nodes) for v in here[1:]]
        right = [right0] + [shift_x(v, -1, nodes) for v in here[1:]]
        across = [
            shift_x(right[0], -1, nodes),
            shift_x(left[1][0], 1, nodes),
            shift_x(right[1][1], -1, nodes),
            shift_x(left[2], 1, nodes),
        ]
    sources = here + right + across + left
    row, sources = lax.optimization_barrier((row, sources))


    with jax.named_scope("aggregate"):
        agg = pl.pallas_call(
            fwd_kernel,
            out_shape=jax.ShapeDtypeStruct((hid, width, span), BF16),
            in_specs=[spec(pltpu.SMEM)] * 2 + [spec(pl.ANY)] * (1 + len(sources)),
            out_specs=spec(VMEM),
            scratch_shapes=[
                VMEM((nodes + 1, width, rows), BF16),
                VMEM(blocks.shape, BF16),
                VMEM((row_blocks, width, block), F32),
                pltpu.SMEM((row_blocks * capacity // 2 + UNROLL,), jnp.int32),
                pltpu.SemaphoreType.DMA((len(sources),)),
                pltpu.SemaphoreType.DMA((row_blocks, capacity // QUARTER)),
            ],
            compiler_params=params(AGG),
            cost_estimate=cost(9),
        )(place, counts, blocks, *sources)
    agg = exchange(agg)

    with jax.named_scope("dense"):
        cross, kept = pl.pallas_call(
            mid_kernel,
            out_shape=[jax.ShapeDtypeStruct((hid, width, span), BF16), stay],
            in_specs=[spec(VMEM)] * 2,
            out_specs=[spec(VMEM)] * 2,
            compiler_params=params(16),
        )(agg, row)
    cross = exchange(cross)
    kept, cross = lax.optimization_barrier((kept, cross))
    kept = exchange_half(kept)

    one = jax.ShapeDtypeStruct((width, rows), BF16)
    two = jax.ShapeDtypeStruct((2, width, rows), BF16)
    with jax.named_scope("spread"):
        own, d2p, d2m, r1, l1, r2, l2 = pl.pallas_call(
            bwd_kernel,
            out_shape=[jax.ShapeDtypeStruct((ZN, width, rows), BF16)] + [two] * 6,
            in_specs=[spec(pltpu.SMEM)] * 2 + [spec(pl.ANY), spec(VMEM)],
            out_specs=[spec(VMEM)] * 7,
            scratch_shapes=[
                VMEM((nodes + 1, width, rows), F32),
                VMEM(blocks.shape, BF16),
                VMEM((row_blocks, width, block), BF16),
                pltpu.SMEM((row_blocks * capacity // 2 + UNROLL,), jnp.int32),
                pltpu.SemaphoreType.DMA((row_blocks, capacity // QUARTER)),
            ],
            compiler_params=params(SPR),
            cost_estimate=cost(9),
        )(place, counts, blocks, cross)

    def small(kernel, outs, *args):
        return pl.pallas_call(
            kernel,
            out_shape=outs,
            in_specs=[spec(VMEM)] * len(args),
            out_specs=[spec(VMEM)] * len(outs),
            compiler_params=params(8),
        )(*args)

    with jax.named_scope("node_sum"):
        from_left, from_right = shift_x(d2p, 1, nodes), shift_x(d2m, -1, nodes)
        r1, l1, r2, l2 = small(relay_kernel, [two] * 4, r1, l1, r2, l2, from_left, from_right)
        r1, l1 = shift_x(r1, 1, nodes), shift_x(l1, -1, nodes)
        r1, l1, r2, l2 = lax.optimization_barrier((r1, l1, r2, l2))
        r2, l2 = shift_x(r2, 1, nodes), shift_x(l2, -1, nodes)
        s2, s3 = small(join_far_kernel, [jax.ShapeDtypeStruct(one.shape, F32), one], own, r1, l1)
        s3 = flip_z(s3, 1, nodes)
        kept, _ = lax.optimization_barrier((kept, s3))
        hidden, parts = small(
            fold_kernel, [one, jax.ShapeDtypeStruct((nodes, width, 128), BF16)], kept
        )
        parts = lax.all_to_all(parts, "node", 0, 0, tiled=True)
        far = (s2 + s3.astype(F32)).astype(BF16)
        far = flip_z(far, 2, nodes)
        (s1,) = small(join_near_kernel, [one], own, r2, l2)
        near = flip_z(s1, 1, nodes)
        feat_grad, weight_grad, bias_grad = small(
            functools.partial(last_kernel, scale),
            [
                jax.ShapeDtypeStruct((width, rows), BF16),
                jax.ShapeDtypeStruct((width, width), F32),
                jax.ShapeDtypeStruct((1, width), F32),
            ],
            own, r2, l2, near, far, parts,
        )
    return hidden, feat_grad, weight_grad, bias_grad.reshape(width)


def solution(mesh):
    placed = (
        P("hid", "node"),
        P(None, "hid"),
        P("hid"),
        P("node", None, None, None),
        P("node", None),
        P("node"),
        P("hid", "node"),
    )
    return jax.shard_map(
        per_device,
        mesh=mesh,
        in_specs=placed,
        out_specs=(P("hid", "node"), P("hid", "node"), P("node", "hid"), P("hid")),
        check_vma=False,
    )
```

```python
import functools
import math

import jax
import jax.numpy as jnp
from jax import lax
from jax.experimental import pallas as pl
from jax.experimental.pallas import tpu as pltpu
from jax.sharding import PartitionSpec as P

F32 = jnp.float32
BF16 = jnp.bfloat16
ZN = 4
UNROLL = 8
QUARTER = 4
VMEM = pltpu.VMEM
MIB = 1024 * 1024
AGG, SPR = 56, 50


def shift_x(v, by, n):
    return lax.ppermute(v, "node", [(i, (i + ZN * by) % n) for i in range(n)])


def flip_z(v, by, n):
    return lax.ppermute(v, "node", [(i, i ^ by) for i in range(n)])


def split3(v):
    hi = v.astype(BF16).astype(F32)
    mid = (v - hi).astype(BF16).astype(F32)
    low = v - hi - mid
    lane = lax.broadcasted_iota(jnp.int32, (v.shape[0], 128), 1)
    return jnp.where(lane == 0, hi, jnp.where(lane == 1, mid, jnp.where(lane == 2, low, 0.0)))


def load_rows(counts_ref, adj_hbm, adj, sems, begin):
    row_blocks, pieces = sems.shape

    def one(r, q):
        at = pl.ds((r * pieces + q) * QUARTER, QUARTER)
        return pltpu.make_async_copy(adj_hbm.at[at], adj.at[at], sems.at[r, q])

    def row(r, carry):
        for q in range(pieces):

            @pl.when(counts_ref[r] > q * QUARTER)
            def _():
                one(r, q).start() if begin else one(r, q).wait()

        return carry

    return row


def list_pairs(counts_ref, pairs_ref, none):
    row_blocks = counts_ref.shape[0]
    capacity = none // row_blocks

    def row(r, n):
        def one(p, n):
            pairs_ref[n] = r * capacity + 2 * p
            return n + 1

        return lax.fori_loop(0, (counts_ref[r] + 1) >> 1, one, n)

    used = lax.fori_loop(0, row_blocks, row, 0)
    for i in range(UNROLL):
        pairs_ref[used + i] = none
    return (used + UNROLL - 1) // UNROLL


def over_pairs(place_ref, counts_ref, adj_hbm, adj, pairs, sems, steps, work, add):
    row_blocks = counts_ref.shape[0]
    none = adj.shape[0]
    shift = (none // row_blocks).bit_length() - 1

    def step(i, ready):
        slots = [pairs[i * UNROLL + u] for u in range(UNROLL)]
        inside = [slot & (none - 1) for slot in slots]
        rows = [at >> shift for at in inside]
        last = functools.reduce(jnp.maximum, rows)
        lax.fori_loop(ready, last + 1, load_rows(counts_ref, adj_hbm, adj, sems, False), 0)
        parts = []
        for slot, at, r in zip(slots, inside, rows):
            k = slot & (none // row_blocks - 1)
            both = jnp.concatenate([adj[at], adj[at + 1]], axis=1)
            parts.append((r, *work(r, both, (place_ref[slot >> shift, k], place_ref[slot >> shift, k + 1]))))
        for part in parts:
            add(*part)
        return jnp.maximum(ready, last + 1)

    lax.fori_loop(0, steps, step, 0)


def split_place(where, rows, block):
    return where >> (rows.bit_length() - 1), pl.ds(pl.multiple_of(where & (rows - 1), block), block)


def pack_kernel(me_ref, counts_ref, columns_ref, cot_ref, wt_ref, bias_ref, out_ref, place_ref):
    row_blocks, capacity = columns_ref.shape
    rows, block = cot_ref.shape[1], cot_ref.shape[1] // row_blocks
    x, z = me_ref[0] >> 2, me_ref[0] & (ZN - 1)
    column = columns_ref[...]
    index = lax.div(column, row_blocks)
    plane = (((index >> 2) - x) & (ZN - 1)) * ZN + ((index & (ZN - 1)) ^ z)
    place = plane * rows + lax.rem(column, row_blocks) * block
    slot = lax.broadcasted_iota(jnp.int32, (1, capacity), 1)
    place_ref[...] = jnp.full(place_ref.shape, me_ref[1] * rows, jnp.int32)
    for r in range(row_blocks):
        place_ref[r : r + 1, :capacity] = jnp.where(
            slot < counts_ref[r], place[r : r + 1], me_ref[1] * rows
        )
    parts = out_ref.shape[0]
    width, total = wt_ref.shape
    span = cot_ref.shape[1] // parts
    bias = jnp.broadcast_to(bias_ref[...], (width, width)).T[:, :1]
    tail = split3(bias).astype(BF16)
    for p in range(parts):
        out_ref[p, :, :span] = cot_ref[:, p * span : (p + 1) * span]
        out_ref[p, :, span : span + total] = wt_ref[...]
        out_ref[p, :, span + total :] = tail


def fwd_kernel(place_ref, counts_ref, adj_hbm, *refs):
    srcs, (out_ref, xs, adj, acc, pairs, sems, rsems) = refs[:-7], refs[-7:]
    row_blocks, _, block = acc.shape
    nodes, rows = xs.shape[0] - 1, xs.shape[2]
    copies, q = [], 0
    for n, ref in enumerate(srcs):
        blocks = ref.shape[0] if len(ref.shape) == 3 else 1
        to = xs.at[pl.ds(q, blocks)] if blocks > 1 else xs.at[q]
        copies.append(pltpu.make_async_copy(ref, to, sems.at[n]))
        q += blocks
    for c in copies:
        c.start()
    lax.fori_loop(0, row_blocks, load_rows(counts_ref, adj_hbm, adj, rsems, True), 0)
    steps = list_pairs(counts_ref, pairs, adj.shape[0])
    acc[...] = jnp.zeros_like(acc)
    xs[nodes] = jnp.zeros_like(xs[nodes])
    for c in copies:
        c.wait()

    def work(r, both, places):
        x = []
        for where in places:
            q, at = split_place(where, rows, block)
            x.append(xs[q, :, at])
        x = jnp.concatenate(x, axis=1)
        return (lax.dot_general(x, both, (((1,), (1,)), ((), ())), preferred_element_type=F32),)

    def add(r, got):
        acc[r] += got

    over_pairs(place_ref, counts_ref, adj_hbm, adj, pairs, rsems, steps, work, add)
    for r in range(row_blocks):
        done = acc[r].astype(BF16)
        for p in (r // 2, (row_blocks + r) // 2):
            out_ref[p, :, r % 2 * block : (r % 2 + 1) * block] = done


def mid_kernel(agg_ref, row_ref, cross_ref, stay_ref):
    hid, width, span = agg_ref.shape
    half = row_ref.shape[0]
    total = hid * width
    agg = agg_ref[...].reshape(total, span)
    row = row_ref[...].reshape(half * width, row_ref.shape[2])
    cot = row[:, :span].astype(F32)
    wt = row[:, span : span + total]
    bias = jnp.sum(row[:, span + total :].astype(F32), axis=1, keepdims=True)
    pre = jnp.dot(wt, agg, preferred_element_type=F32) + bias
    sig = jax.nn.sigmoid(pre)
    hidden = (pre * sig).astype(BF16)
    slope = (cot * sig * (1.0 + pre * (1.0 - sig))).astype(BF16)
    ws = lax.dot_general(wt, slope, (((0,), (0,)), ((), ())), preferred_element_type=F32)
    cross_ref[...] = ws.astype(BF16).reshape(hid, width, span)
    wg = lax.dot_general(slope, agg, (((1,), (1,)), ((), ())), preferred_element_type=F32)
    tail = split3(jnp.sum(slope.astype(F32), axis=1, keepdims=True))
    stay_ref[:, :, :span] = hidden.reshape(half, width, span)
    stay_ref[:, :, span : span + total] = wg.astype(BF16).reshape(half, width, total)
    stay_ref[:, :, span + total :] = tail.astype(BF16).reshape(half, width, 128)


def bwd_kernel(
    place_ref, counts_ref, adj_hbm, cross_ref,
    own_ref, d2p, d2m, r1, l1, r2, l2, acc, adj, ws, pairs, rsems,
):
    nodes, (width, rows) = acc.shape[0] - 1, acc.shape[1:]
    block = adj.shape[1]
    row_blocks = counts_ref.shape[0]
    lax.fori_loop(0, row_blocks, load_rows(counts_ref, adj_hbm, adj, rsems, True), 0)
    steps = list_pairs(counts_ref, pairs, adj.shape[0])
    acc[...] = jnp.zeros_like(acc)
    half = row_blocks // 2
    for p in range(half):
        both_halves = cross_ref[p].astype(F32) + cross_ref[half + p].astype(F32)
        ws[2 * p] = both_halves[:, :block].astype(BF16)
        ws[2 * p + 1] = both_halves[:, block:].astype(BF16)

    def work(r, both, places):
        made = jnp.dot(ws[r], both, preferred_element_type=F32)
        return made, places

    def add(r, made, places):
        for n, where in enumerate(places):
            q, at = split_place(where, rows, block)
            acc[q, :, at] += made[:, n * block : (n + 1) * block]

    over_pairs(place_ref, counts_ref, adj_hbm, adj, pairs, rsems, steps, work, add)

    def put(ref, n, q):
        ref[n] = acc[q].astype(BF16)

    for s in range(ZN):
        put(own_ref, s, s)
        right, left = (r2, l2) if s < 2 else (r1, l1)
        put(right, s % 2, ZN + s)
        put(left, s % 2, 3 * ZN + s)
    for n, s in enumerate((2, 0)):
        put(d2p, n, 2 * ZN + s)
        put(d2m, n, 2 * ZN + s + 1)


def fold_kernel(stay_ref, hidden_ref, out_ref):
    nodes, width, _ = out_ref.shape
    total = nodes * width
    half = stay_ref.shape[0]
    span = hidden_ref.shape[1] // half
    wg = jnp.zeros((width, total), F32)
    tail = jnp.zeros((width, 128), F32)
    for p in range(half):
        hidden_ref[:, p * span : (p + 1) * span] = stay_ref[p, :, :span]
        wg = wg + stay_ref[p, :, span : span + total].astype(F32)
        tail = tail + stay_ref[p, :, span + total :].astype(F32)
    tail = pltpu.roll(split3(jnp.sum(tail, axis=1, keepdims=True)), width, 1)
    lane = lax.broadcasted_iota(jnp.int32, (width, 128), 1)
    for a in range(nodes):
        tile = wg[:, (a * width) // 128 * 128 : (a * width) // 128 * 128 + 128]
        start = (a * width) % 128
        if start:
            tile = pltpu.roll(tile, 128 - start, 1)
        out_ref[a] = jnp.where(lane < width, tile, tail).astype(BF16)


def relay_kernel(r1, l1, r2, l2, from_left, from_right, r1_out, l1_out, r2_out, l2_out):
    for n, (right, left, right_out, left_out) in enumerate(
        ((r1, l1, r1_out, l1_out), (r2, l2, r2_out, l2_out))
    ):
        right_out[0] = (right[0].astype(F32) + from_left[n].astype(F32)).astype(BF16)
        right_out[1] = right[1]
        left_out[0] = left[0]
        left_out[1] = (left[1].astype(F32) + from_right[n].astype(F32)).astype(BF16)


def joined(own_ref, right, left, s):
    n = s % 2
    return own_ref[s].astype(F32) + right[n].astype(F32) + left[n].astype(F32)


def join_far_kernel(own_ref, right, left, s2, s3):
    s2[...] = joined(own_ref, right, left, 2).astype(BF16)
    s3[...] = joined(own_ref, right, left, 3).astype(BF16)


def join_near_kernel(own_ref, right, left, s1):
    s1[...] = joined(own_ref, right, left, 1).astype(BF16)


def last_kernel(scale, own_ref, right, left, near, far2, far3, parts_ref, feat_ref, wg_ref, bias_ref):
    total = joined(own_ref, right, left, 0) + near[...].astype(F32)
    total = total + far2[...].astype(F32) + far3[...].astype(F32)
    feat_ref[...] = total.astype(BF16)
    width = feat_ref.shape[0]
    tail = parts_ref[0].astype(F32)
    for a in range(1, parts_ref.shape[0]):
        tail = tail + parts_ref[a].astype(F32)
    lane = lax.broadcasted_iota(jnp.int32, tail.shape, 1)
    bsum = jnp.sum(jnp.where(lane >= width, tail, 0.0), axis=1, keepdims=True)
    bias_ref[...] = jnp.broadcast_to(bsum * scale, (width, 128)).T[:1]
    wg_ref[...] = tail[:, :width].T * scale


def spec(space):
    return pl.BlockSpec(memory_space=space)


def cost(us):
    return pl.CostEstimate(flops=0, bytes_accessed=int(us * 3e6), transcendentals=0)


def params(mib):
    return pltpu.CompilerParams(vmem_limit_bytes=mib * MIB)


def per_device(feats, weight, bias, adjacency, columns, counts, cotangent):
    width, rows = feats.shape
    row_blocks, capacity, block, _ = adjacency.shape
    nodes, hid = lax.axis_size("node"), lax.axis_size("hid")
    total = weight.shape[0]
    scale = 1.0 / math.sqrt(nodes * rows)
    me = lax.axis_index("node")
    blocks = adjacency.reshape(row_blocks * capacity, block, block)

    half = hid // 2
    span = rows // half
    halves = [list(range(half)), list(range(half, hid))]

    def exchange_half(v):
        return lax.all_to_all(v, "hid", 0, 0, axis_index_groups=halves, tiled=True)

    def exchange(v):
        return lax.all_to_all(v, "hid", 0, 0, tiled=True)

    with jax.named_scope("pack"):
        stay = jax.ShapeDtypeStruct((half, width, span + total + 128), BF16)
        row, place = pl.pallas_call(
            pack_kernel,
            out_shape=[stay, jax.ShapeDtypeStruct((row_blocks + 8, 128), jnp.int32)],
            in_specs=[spec(pltpu.SMEM)] * 2 + [spec(VMEM)] * 4,
            out_specs=[spec(VMEM)] * 2,
            compiler_params=params(57),
        )(
            jnp.stack([me, nodes]).astype(jnp.int32),
            counts, columns, cotangent, weight.T, bias.reshape(1, width),
        )

    with jax.named_scope("node_gather"):
        z1, z2 = flip_z(feats, 1, nodes), flip_z(feats, 2, nodes)
        z3 = flip_z(z2, 1, nodes)
        left0, right0 = shift_x(feats, 1, nodes), shift_x(feats, -1, nodes)
        z1, left0, right0, place = lax.optimization_barrier((z1, left0, right0, place))
        row = exchange_half(row)
        here = [feats, jnp.stack([z1, z2]), z3]
        left = [left0] + [shift_x(v, 1, nodes) for v in here[1:]]
        right = [right0] + [shift_x(v, -1, nodes) for v in here[1:]]
        across = [
            shift_x(right[0], -1, nodes),
            shift_x(left[1][0], 1, nodes),
            shift_x(right[1][1], -1, nodes),
            shift_x(left[2], 1, nodes),
        ]
    sources = here + right + across + left
    row, sources = lax.optimization_barrier((row, sources))


    with jax.named_scope("aggregate"):
        agg = pl.pallas_call(
            fwd_kernel,
            out_shape=jax.ShapeDtypeStruct((hid, width, span), BF16),
            in_specs=[spec(pltpu.SMEM)] * 2 + [spec(pl.ANY)] * (1 + len(sources)),
            out_specs=spec(VMEM),
            scratch_shapes=[
                VMEM((nodes + 1, width, rows), BF16),
                VMEM(blocks.shape, BF16),
                VMEM((row_blocks, width, block), F32),
                pltpu.SMEM((row_blocks * capacity // 2 + UNROLL,), jnp.int32),
                pltpu.SemaphoreType.DMA((len(sources),)),
                pltpu.SemaphoreType.DMA((row_blocks, capacity // QUARTER)),
            ],
            compiler_params=params(AGG),
            cost_estimate=cost(9),
        )(place, counts, blocks, *sources)
    agg = exchange(agg)

    with jax.named_scope("dense"):
        cross, kept = pl.pallas_call(
            mid_kernel,
            out_shape=[jax.ShapeDtypeStruct((hid, width, span), BF16), stay],
            in_specs=[spec(VMEM)] * 2,
            out_specs=[spec(VMEM)] * 2,
            compiler_params=params(16),
        )(agg, row)
    cross = exchange(cross)
    kept, cross = lax.optimization_barrier((kept, cross))
    kept = exchange_half(kept)

    one = jax.ShapeDtypeStruct((width, rows), BF16)
    two = jax.ShapeDtypeStruct((2, width, rows), BF16)
    with jax.named_scope("spread"):
        own, d2p, d2m, r1, l1, r2, l2 = pl.pallas_call(
            bwd_kernel,
            out_shape=[jax.ShapeDtypeStruct((ZN, width, rows), BF16)] + [two] * 6,
            in_specs=[spec(pltpu.SMEM)] * 2 + [spec(pl.ANY), spec(VMEM)],
            out_specs=[spec(VMEM)] * 7,
            scratch_shapes=[
                VMEM((nodes + 1, width, rows), F32),
                VMEM(blocks.shape, BF16),
                VMEM((row_blocks, width, block), BF16),
                pltpu.SMEM((row_blocks * capacity // 2 + UNROLL,), jnp.int32),
                pltpu.SemaphoreType.DMA((row_blocks, capacity // QUARTER)),
            ],
            compiler_params=params(SPR),
            cost_estimate=cost(9),
        )(place, counts, blocks, cross)

    def small(kernel, outs, *args):
        return pl.pallas_call(
            kernel,
            out_shape=outs,
            in_specs=[spec(VMEM)] * len(args),
            out_specs=[spec(VMEM)] * len(outs),
            compiler_params=params(8),
        )(*args)

    with jax.named_scope("node_sum"):
        from_left, from_right = shift_x(d2p, 1, nodes), shift_x(d2m, -1, nodes)
        r1, l1, r2, l2 = small(relay_kernel, [two] * 4, r1, l1, r2, l2, from_left, from_right)
        r1, l1 = shift_x(r1, 1, nodes), shift_x(l1, -1, nodes)
        r1, l1, r2, l2 = lax.optimization_barrier((r1, l1, r2, l2))
        r2, l2 = shift_x(r2, 1, nodes), shift_x(l2, -1, nodes)
        s2, s3 = small(join_far_kernel, [one, one], own, r1, l1)
        kept, s2, s3 = lax.optimization_barrier((kept, s2, s3))
        far = [flip_z(s2, 2, nodes), flip_z(s3, 3, nodes)]
        hidden, parts = small(
            fold_kernel, [one, jax.ShapeDtypeStruct((nodes, width, 128), BF16)], kept
        )
        parts = lax.all_to_all(parts, "node", 0, 0, tiled=True)
        (s1,) = small(join_near_kernel, [one], own, r2, l2)
        near = flip_z(s1, 1, nodes)
        feat_grad, weight_grad, bias_grad = small(
            functools.partial(last_kernel, scale),
            [
                jax.ShapeDtypeStruct((width, rows), BF16),
                jax.ShapeDtypeStruct((width, width), F32),
                jax.ShapeDtypeStruct((1, width), F32),
            ],
            own, r2, l2, near, *far, parts,
        )
    return hidden, feat_grad, weight_grad, bias_grad.reshape(width)


def solution(mesh):
    placed = (
        P("hid", "node"),
        P(None, "hid"),
        P("hid"),
        P("node", None, None, None),
        P("node", None),
        P("node"),
        P("hid", "node"),
    )
    return jax.shard_map(
        per_device,
        mesh=mesh,
        in_specs=placed,
        out_specs=(P("hid", "node"), P("hid", "node"), P("node", "hid"), P("hid")),
        check_vma=False,
    )
```

```python
import functools
import math

import jax
import jax.numpy as jnp
from jax import lax
from jax.experimental import pallas as pl
from jax.experimental.pallas import tpu as pltpu
from jax.sharding import PartitionSpec as P

F32 = jnp.float32
BF16 = jnp.bfloat16
ZN = 4
UNROLL = 16
QUARTER = 4
VMEM = pltpu.VMEM
MIB = 1024 * 1024
AGG, SPR = 56, 50


def shift_x(v, by, n):
    return lax.ppermute(v, "node", [(i, (i + ZN * by) % n) for i in range(n)])


def flip_z(v, by, n):
    return lax.ppermute(v, "node", [(i, i ^ by) for i in range(n)])


def split3(v):
    hi = v.astype(BF16).astype(F32)
    mid = (v - hi).astype(BF16).astype(F32)
    low = v - hi - mid
    lane = lax.broadcasted_iota(jnp.int32, (v.shape[0], 128), 1)
    return jnp.where(lane == 0, hi, jnp.where(lane == 1, mid, jnp.where(lane == 2, low, 0.0)))


def load_rows(counts_ref, adj_hbm, adj, sems, begin):
    row_blocks, pieces = sems.shape

    def one(r, q):
        at = pl.ds((r * pieces + q) * QUARTER, QUARTER)
        return pltpu.make_async_copy(adj_hbm.at[at], adj.at[at], sems.at[r, q])

    def row(r, carry):
        for q in range(pieces):

            @pl.when(counts_ref[r] > q * QUARTER)
            def _():
                one(r, q).start() if begin else one(r, q).wait()

        return carry

    return row


def list_pairs(counts_ref, pairs_ref, none):
    row_blocks = counts_ref.shape[0]
    capacity = none // row_blocks

    def row(r, n):
        def one(p, n):
            pairs_ref[n] = r * capacity + 2 * p
            return n + 1

        return lax.fori_loop(0, (counts_ref[r] + 1) >> 1, one, n)

    used = lax.fori_loop(0, row_blocks, row, 0)
    for i in range(UNROLL):
        pairs_ref[used + i] = none
    return (used + UNROLL - 1) // UNROLL


def over_pairs(place_ref, counts_ref, adj_hbm, adj, pairs, sems, steps, work, add):
    row_blocks = counts_ref.shape[0]
    none = adj.shape[0]
    shift = (none // row_blocks).bit_length() - 1

    def step(i, ready):
        slots = [pairs[i * UNROLL + u] for u in range(UNROLL)]
        inside = [slot & (none - 1) for slot in slots]
        rows = [at >> shift for at in inside]
        last = functools.reduce(jnp.maximum, rows)
        lax.fori_loop(ready, last + 1, load_rows(counts_ref, adj_hbm, adj, sems, False), 0)
        for slot, at, r in zip(slots, inside, rows):
            k = slot & (none // row_blocks - 1)
            both = jnp.concatenate([adj[at], adj[at + 1]], axis=1)
            add(r, *work(r, both, (place_ref[slot >> shift, k], place_ref[slot >> shift, k + 1])))
        return jnp.maximum(ready, last + 1)

    lax.fori_loop(0, steps, step, 0)


def split_place(where, rows, block):
    return where >> (rows.bit_length() - 1), pl.ds(pl.multiple_of(where & (rows - 1), block), block)


def pack_kernel(me_ref, counts_ref, columns_ref, cot_ref, wt_ref, bias_ref, out_ref, place_ref):
    row_blocks, capacity = columns_ref.shape
    rows, block = cot_ref.shape[1], cot_ref.shape[1] // row_blocks
    x, z = me_ref[0] >> 2, me_ref[0] & (ZN - 1)
    column = columns_ref[...]
    index = lax.div(column, row_blocks)
    plane = (((index >> 2) - x) & (ZN - 1)) * ZN + ((index & (ZN - 1)) ^ z)
    place = plane * rows + lax.rem(column, row_blocks) * block
    slot = lax.broadcasted_iota(jnp.int32, (1, capacity), 1)
    place_ref[...] = jnp.full(place_ref.shape, me_ref[1] * rows, jnp.int32)
    for r in range(row_blocks):
        place_ref[r : r + 1, :capacity] = jnp.where(
            slot < counts_ref[r], place[r : r + 1], me_ref[1] * rows
        )
    parts = out_ref.shape[0]
    width, total = wt_ref.shape
    span = cot_ref.shape[1] // parts
    bias = jnp.broadcast_to(bias_ref[...], (width, width)).T[:, :1]
    tail = split3(bias).astype(BF16)
    for p in range(parts):
        out_ref[p, :, :span] = cot_ref[:, p * span : (p + 1) * span]
        out_ref[p, :, span : span + total] = wt_ref[...]
        out_ref[p, :, span + total :] = tail


def fwd_kernel(place_ref, counts_ref, adj_hbm, *refs):
    srcs, (out_ref, xs, adj, acc, pairs, sems, rsems) = refs[:-7], refs[-7:]
    row_blocks, _, block = acc.shape
    nodes, rows = xs.shape[0] - 1, xs.shape[2]
    copies, q = [], 0
    for n, ref in enumerate(srcs):
        blocks = ref.shape[0] if len(ref.shape) == 3 else 1
        to = xs.at[pl.ds(q, blocks)] if blocks > 1 else xs.at[q]
        copies.append(pltpu.make_async_copy(ref, to, sems.at[n]))
        q += blocks
    for c in copies:
        c.start()
    lax.fori_loop(0, row_blocks, load_rows(counts_ref, adj_hbm, adj, rsems, True), 0)
    steps = list_pairs(counts_ref, pairs, adj.shape[0])
    acc[...] = jnp.zeros_like(acc)
    xs[nodes] = jnp.zeros_like(xs[nodes])
    for c in copies:
        c.wait()

    def work(r, both, places):
        x = []
        for where in places:
            q, at = split_place(where, rows, block)
            x.append(xs[q, :, at])
        x = jnp.concatenate(x, axis=1)
        return (lax.dot_general(x, both, (((1,), (1,)), ((), ())), preferred_element_type=F32),)

    def add(r, got):
        acc[r] += got

    over_pairs(place_ref, counts_ref, adj_hbm, adj, pairs, rsems, steps, work, add)
    for r in range(row_blocks):
        done = acc[r].astype(BF16)
        for p in (r // 2, (row_blocks + r) // 2):
            out_ref[p, :, r % 2 * block : (r % 2 + 1) * block] = done


def mid_kernel(agg_ref, row_ref, cross_ref, stay_ref):
    hid, width, span = agg_ref.shape
    half = row_ref.shape[0]
    total = hid * width
    agg = agg_ref[...].reshape(total, span)
    row = row_ref[...].reshape(half * width, row_ref.shape[2])
    cot = row[:, :span].astype(F32)
    wt = row[:, span : span + total]
    bias = jnp.sum(row[:, span + total :].astype(F32), axis=1, keepdims=True)
    pre = jnp.dot(wt, agg, preferred_element_type=F32) + bias
    sig = jax.nn.sigmoid(pre)
    hidden = (pre * sig).astype(BF16)
    slope = (cot * sig * (1.0 + pre * (1.0 - sig))).astype(BF16)
    ws = lax.dot_general(wt, slope, (((0,), (0,)), ((), ())), preferred_element_type=F32)
    cross_ref[...] = ws.astype(BF16).reshape(hid, width, span)
    wg = lax.dot_general(slope, agg, (((1,), (1,)), ((), ())), preferred_element_type=F32)
    tail = split3(jnp.sum(slope.astype(F32), axis=1, keepdims=True))
    stay_ref[:, :, :span] = hidden.reshape(half, width, span)
    stay_ref[:, :, span : span + total] = wg.astype(BF16).reshape(half, width, total)
    stay_ref[:, :, span + total :] = tail.astype(BF16).reshape(half, width, 128)


def bwd_kernel(
    place_ref, counts_ref, adj_hbm, cross_ref,
    own_ref, d2p, d2m, r1, l1, r2, l2, acc, adj, ws, pairs, rsems,
):
    nodes, (width, rows) = acc.shape[0] - 1, acc.shape[1:]
    block = adj.shape[1]
    row_blocks = counts_ref.shape[0]
    lax.fori_loop(0, row_blocks, load_rows(counts_ref, adj_hbm, adj, rsems, True), 0)
    steps = list_pairs(counts_ref, pairs, adj.shape[0])
    acc[...] = jnp.zeros_like(acc)
    half = row_blocks // 2
    for p in range(half):
        both_halves = cross_ref[p].astype(F32) + cross_ref[half + p].astype(F32)
        ws[2 * p] = both_halves[:, :block].astype(BF16)
        ws[2 * p + 1] = both_halves[:, block:].astype(BF16)

    def work(r, both, places):
        made = jnp.dot(ws[r], both, preferred_element_type=F32)
        return made, places

    def add(r, made, places):
        for n, where in enumerate(places):
            q, at = split_place(where, rows, block)
            acc[q, :, at] += made[:, n * block : (n + 1) * block]

    over_pairs(place_ref, counts_ref, adj_hbm, adj, pairs, rsems, steps, work, add)

    def put(ref, n, q):
        ref[n] = acc[q].astype(BF16)

    for s in range(ZN):
        put(own_ref, s, s)
        right, left = (r2, l2) if s < 2 else (r1, l1)
        put(right, s % 2, ZN + s)
        put(left, s % 2, 3 * ZN + s)
    for n, s in enumerate((2, 0)):
        put(d2p, n, 2 * ZN + s)
        put(d2m, n, 2 * ZN + s + 1)


def fold_kernel(stay_ref, hidden_ref, out_ref):
    nodes, width, _ = out_ref.shape
    total = nodes * width
    half = stay_ref.shape[0]
    span = hidden_ref.shape[1] // half
    wg = jnp.zeros((width, total), F32)
    tail = jnp.zeros((width, 128), F32)
    for p in range(half):
        hidden_ref[:, p * span : (p + 1) * span] = stay_ref[p, :, :span]
        wg = wg + stay_ref[p, :, span : span + total].astype(F32)
        tail = tail + stay_ref[p, :, span + total :].astype(F32)
    tail = pltpu.roll(split3(jnp.sum(tail, axis=1, keepdims=True)), width, 1)
    lane = lax.broadcasted_iota(jnp.int32, (width, 128), 1)
    for a in range(nodes):
        tile = wg[:, (a * width) // 128 * 128 : (a * width) // 128 * 128 + 128]
        start = (a * width) % 128
        if start:
            tile = pltpu.roll(tile, 128 - start, 1)
        out_ref[a] = jnp.where(lane < width, tile, tail).astype(BF16)


def relay_kernel(r1, l1, r2, l2, from_left, from_right, r1_out, l1_out, r2_out, l2_out):
    for n, (right, left, right_out, left_out) in enumerate(
        ((r1, l1, r1_out, l1_out), (r2, l2, r2_out, l2_out))
    ):
        right_out[0] = (right[0].astype(F32) + from_left[n].astype(F32)).astype(BF16)
        right_out[1] = right[1]
        left_out[0] = left[0]
        left_out[1] = (left[1].astype(F32) + from_right[n].astype(F32)).astype(BF16)


def joined(own_ref, right, left, s):
    n = s % 2
    return own_ref[s].astype(F32) + right[n].astype(F32) + left[n].astype(F32)


def join_far_kernel(own_ref, right, left, s2, s3):
    s2[...] = joined(own_ref, right, left, 2)
    s3[...] = joined(own_ref, right, left, 3).astype(BF16)


def join_near_kernel(own_ref, right, left, s1):
    s1[...] = joined(own_ref, right, left, 1).astype(BF16)


def last_kernel(scale, own_ref, right, left, near, far, parts_ref, feat_ref, wg_ref, bias_ref):
    total = joined(own_ref, right, left, 0) + near[...].astype(F32) + far[...].astype(F32)
    feat_ref[...] = total.astype(BF16)
    width = feat_ref.shape[0]
    tail = parts_ref[0].astype(F32)
    for a in range(1, parts_ref.shape[0]):
        tail = tail + parts_ref[a].astype(F32)
    lane = lax.broadcasted_iota(jnp.int32, tail.shape, 1)
    bsum = jnp.sum(jnp.where(lane >= width, tail, 0.0), axis=1, keepdims=True)
    bias_ref[...] = jnp.broadcast_to(bsum * scale, (width, 128)).T[:1]
    wg_ref[...] = tail[:, :width].T * scale


def spec(space):
    return pl.BlockSpec(memory_space=space)


def cost(us):
    return pl.CostEstimate(flops=0, bytes_accessed=int(us * 3e6), transcendentals=0)


def params(mib):
    return pltpu.CompilerParams(vmem_limit_bytes=mib * MIB)


def per_device(feats, weight, bias, adjacency, columns, counts, cotangent):
    width, rows = feats.shape
    row_blocks, capacity, block, _ = adjacency.shape
    nodes, hid = lax.axis_size("node"), lax.axis_size("hid")
    total = weight.shape[0]
    scale = 1.0 / math.sqrt(nodes * rows)
    me = lax.axis_index("node")
    blocks = adjacency.reshape(row_blocks * capacity, block, block)

    half = hid // 2
    span = rows // half
    halves = [list(range(half)), list(range(half, hid))]

    def exchange_half(v):
        return lax.all_to_all(v, "hid", 0, 0, axis_index_groups=halves, tiled=True)

    def exchange(v):
        return lax.all_to_all(v, "hid", 0, 0, tiled=True)

    with jax.named_scope("pack"):
        stay = jax.ShapeDtypeStruct((half, width, span + total + 128), BF16)
        row, place = pl.pallas_call(
            pack_kernel,
            out_shape=[stay, jax.ShapeDtypeStruct((row_blocks + 8, 128), jnp.int32)],
            in_specs=[spec(pltpu.SMEM)] * 2 + [spec(VMEM)] * 4,
            out_specs=[spec(VMEM)] * 2,
            compiler_params=params(57),
        )(
            jnp.stack([me, nodes]).astype(jnp.int32),
            counts, columns, cotangent, weight.T, bias.reshape(1, width),
        )

    with jax.named_scope("node_gather"):
        z1, z2 = flip_z(feats, 1, nodes), flip_z(feats, 2, nodes)
        z3 = flip_z(z2, 1, nodes)
        left0, right0 = shift_x(feats, 1, nodes), shift_x(feats, -1, nodes)
        z1, left0, right0, place = lax.optimization_barrier((z1, left0, right0, place))
        row = exchange_half(row)
        here = [feats, jnp.stack([z1, z2]), z3]
        left = [left0] + [shift_x(v, 1, nodes) for v in here[1:]]
        right = [right0] + [shift_x(v, -1, nodes) for v in here[1:]]
        row, left[1], right[1] = lax.optimization_barrier((row, left[1], right[1]))
        across = [
            shift_x(right[0], -1, nodes),
            shift_x(left[1][0], 1, nodes),
            shift_x(right[1][1], -1, nodes),
            shift_x(left[2], 1, nodes),
        ]
    sources = here + right + across + left


    with jax.named_scope("aggregate"):
        agg = pl.pallas_call(
            fwd_kernel,
            out_shape=jax.ShapeDtypeStruct((hid, width, span), BF16),
            in_specs=[spec(pltpu.SMEM)] * 2 + [spec(pl.ANY)] * (1 + len(sources)),
            out_specs=spec(VMEM),
            scratch_shapes=[
                VMEM((nodes + 1, width, rows), BF16),
                VMEM(blocks.shape, BF16),
                VMEM((row_blocks, width, block), F32),
                pltpu.SMEM((row_blocks * capacity // 2 + UNROLL,), jnp.int32),
                pltpu.SemaphoreType.DMA((len(sources),)),
                pltpu.SemaphoreType.DMA((row_blocks, capacity // QUARTER)),
            ],
            compiler_params=params(AGG),
            cost_estimate=cost(9),
        )(place, counts, blocks, *sources)
    agg = exchange(agg)

    with jax.named_scope("dense"):
        cross, kept = pl.pallas_call(
            mid_kernel,
            out_shape=[jax.ShapeDtypeStruct((hid, width, span), BF16), stay],
            in_specs=[spec(VMEM)] * 2,
            out_specs=[spec(VMEM)] * 2,
            compiler_params=params(16),
        )(agg, row)
    cross = exchange(cross)
    kept, cross = lax.optimization_barrier((kept, cross))
    kept = exchange_half(kept)

    one = jax.ShapeDtypeStruct((width, rows), BF16)
    two = jax.ShapeDtypeStruct((2, width, rows), BF16)
    with jax.named_scope("spread"):
        own, d2p, d2m, r1, l1, r2, l2 = pl.pallas_call(
            bwd_kernel,
            out_shape=[jax.ShapeDtypeStruct((ZN, width, rows), BF16)] + [two] * 6,
            in_specs=[spec(pltpu.SMEM)] * 2 + [spec(pl.ANY), spec(VMEM)],
            out_specs=[spec(VMEM)] * 7,
            scratch_shapes=[
                VMEM((nodes + 1, width, rows), F32),
                VMEM(blocks.shape, BF16),
                VMEM((row_blocks, width, block), BF16),
                pltpu.SMEM((row_blocks * capacity // 2 + UNROLL,), jnp.int32),
                pltpu.SemaphoreType.DMA((row_blocks, capacity // QUARTER)),
            ],
            compiler_params=params(SPR),
            cost_estimate=cost(9),
        )(place, counts, blocks, cross)

    def small(kernel, outs, *args):
        return pl.pallas_call(
            kernel,
            out_shape=outs,
            in_specs=[spec(VMEM)] * len(args),
            out_specs=[spec(VMEM)] * len(outs),
            compiler_params=params(8),
        )(*args)

    with jax.named_scope("node_sum"):
        from_left, from_right = shift_x(d2p, 1, nodes), shift_x(d2m, -1, nodes)
        r1, l1, r2, l2 = small(relay_kernel, [two] * 4, r1, l1, r2, l2, from_left, from_right)
        r1, l1 = shift_x(r1, 1, nodes), shift_x(l1, -1, nodes)
        r1, l1, r2, l2 = lax.optimization_barrier((r1, l1, r2, l2))
        r2, l2 = shift_x(r2, 1, nodes), shift_x(l2, -1, nodes)
        s2, s3 = small(join_far_kernel, [jax.ShapeDtypeStruct(one.shape, F32), one], own, r1, l1)
        s3 = flip_z(s3, 1, nodes)
        kept, _ = lax.optimization_barrier((kept, s3))
        hidden, parts = small(
            fold_kernel, [one, jax.ShapeDtypeStruct((nodes, width, 128), BF16)], kept
        )
        parts = lax.all_to_all(parts, "node", 0, 0, tiled=True)
        far = (s2 + s3.astype(F32)).astype(BF16)
        far = flip_z(far, 2, nodes)
        (s1,) = small(join_near_kernel, [one], own, r2, l2)
        near = flip_z(s1, 1, nodes)
        feat_grad, weight_grad, bias_grad = small(
            functools.partial(last_kernel, scale),
            [
                jax.ShapeDtypeStruct((width, rows), BF16),
                jax.ShapeDtypeStruct((width, width), F32),
                jax.ShapeDtypeStruct((1, width), F32),
            ],
            own, r2, l2, near, far, parts,
        )
    return hidden, feat_grad, weight_grad, bias_grad.reshape(width)


def solution(mesh):
    placed = (
        P("hid", "node"),
        P(None, "hid"),
        P("hid"),
        P("node", None, None, None),
        P("node", None),
        P("node"),
        P("hid", "node"),
    )
    return jax.shard_map(
        per_device,
        mesh=mesh,
        in_specs=placed,
        out_specs=(P("hid", "node"), P("hid", "node"), P("node", "hid"), P("hid")),
        check_vma=False,
    )
```
